32 devices in a mesh: dp: 16 (over z, y, core), tensor: 2 (over x).
Axes of the slice: x: 2, y: 2, z: 4, core: 2. Of those that a mesh axis runs over, the one named last changes fastest.
Arguments:
- visual: bfloat16 [6912, 768], P(('dp', 'tensor')), may hold values from -6 to 6
- query: bfloat16 [8192, 768], P(('dp', 'tensor')), may hold values from -6 to 6
- seg_ids: int32 [16, 512], P('dp'), may hold values from 0 to 31, as said below
- shifts: int32 [16, 2], P('dp'), may hold values from 0 to 11
- valid_rows: int32 [16], P('dp'), may hold values from 19 to 36
- attn_in: float32 [4, 768, 3, 768], P(None, 'dp', None, 'tensor'), may hold values from -0.21875 to 0.21875
- attn_out: float32 [4, 768, 768], P(None, 'tensor', 'dp'), may hold values from -1.25 to 1.25
- mlp_in: float32 [2, 768, 3072], P(None, 'dp', 'tensor'), may hold values from -0.21875 to 0.21875
- mlp_out: float32 [2, 3072, 768], P(None, 'tensor', 'dp'), may hold values from -0.109375 to 0.109375
- gains: float32 [6, 768], P(None, 'dp'), may hold values from 0.5 to 1.5
- cot_visual: bfloat16 [6912, 768], P(('dp', 'tensor')), may hold values from -6 to 6
- cot_query: bfloat16 [8192, 768], P(('dp', 'tensor')), may hold values from -6 to 6
Outputs:
- out_visual: bfloat16 [6912, 768], P(('dp', 'tensor'))
- out_query: bfloat16 [8192, 768], P(('dp', 'tensor'))
- grad_visual: bfloat16 [6912, 768], P(('dp', 'tensor'))
- grad_query: bfloat16 [8192, 768], P(('dp', 'tensor'))
- grad_attn_in: float32 [4, 768, 3, 768], P(None, 'dp', None, 'tensor')
- grad_attn_out: float32 [4, 768, 768], P(None, 'tensor', 'dp')
- grad_mlp_in: float32 [2, 768, 3072], P(None, 'dp', 'tensor')
- grad_mlp_out: float32 [2, 3072, 768], P(None, 'tensor', 'dp')
- grad_gains: float32 [6, 768], P(None, 'dp')
The draws below stay inside these ranges and needn't reach their ends.
Inputs may be any that keep to these rules, and one draw needn't show every extreme that they name: `seg_ids`: in each page the ids start at 0, rise by at most one from a slot to the next and never fall, and the last slot holds id 512 // 16 - 1; slots 512 // 2 - 512 // 8 to 320 share one id.
All inputs are finite; a program needn't handle non-finite values.
Results may differ from the reference program's by a relative error of at most 0.025.
Values may be sent and summed in bfloat16 or wider, within the bound.
No kernel may reach another device: no remote copies, remote signals or barrier semaphores. Data moves between devices by JAX's collectives and lax.ppermute only.
A program may use at most 192 MiB of HBM per device.

```python
import jax
import jax.numpy as jnp
from jax import lax

D = 768
HEADS = 12
HD = 64
FF = 3072
WIN = 12
PH = 36
PW = 12
Q = 512
PAGES = 16
VIS = 6912
QUERIES = 8192


def draw_seg_ids(key, part):
    key = jax.random.fold_in(key, 7)
    place = jnp.arange(Q, dtype=jnp.int32)[None, :]
    middle = (place >= Q // 2 - Q // 8) & (place <= Q // 2 + Q // 8)
    usable = (place > 0) & jnp.logical_not(middle)
    picks = jax.random.randint(key, (PAGES, Q), 0, 1048576)
    attention_logits = jnp.where(usable, picks, 1048576) * Q + place
    order = jnp.argsort(attention_logits, axis=1, stable=True)
    ranks = jnp.argsort(order, axis=1, stable=True).astype(jnp.int32)
    starts = usable & (ranks < Q // 16 - 1)
    return jnp.cumsum(starts.astype(jnp.int32), axis=1).astype(jnp.int32)


def plant(values, key, least, top_value):
    dims = values.shape
    spot = [jax.random.randint(jax.random.fold_in(key, axis), (), 0, dims[axis]) for axis in range(len(dims))]
    values = values.at[tuple(spot)].set(least)
    longest = dims.index(max(dims))
    spot[longest] = (spot[longest] + 1) % dims[longest]
    return values.at[tuple(spot)].set(top_value)


def spiked(drawn, own_key, source, target, parts, factor):
    owner, partner = [(jnp.arange(drawn.shape[position]) // (drawn.shape[position] // parts)).reshape([-1 if axis == position else 1 for axis in range(drawn.ndim)]) for position in (source, target)]
    chosen = jax.random.permutation(own_key, parts)[partner]
    strong = (owner == chosen) | (owner == (partner + parts // 2) % parts)
    return jnp.where(strong, factor * drawn, drawn)


def steps_of(rng, dims, pieces, least, high):
    def one(position, parts):
        draws = jax.random.uniform(jax.random.fold_in(jax.random.fold_in(rng, 6), position), (parts,), jnp.float32, least / len(pieces), high / len(pieces))
        return jnp.repeat(jnp.exp(draws), dims[position] // parts).reshape((-1,) + (1,) * (len(dims) - position - 1))

    factor_of = one(*pieces[0])
    for cut in pieces[1:]:
        factor_of = factor_of * one(*cut)
    return factor_of


def scatter_about(own_key, extent, scale, reach, cuts=(), kind=jnp.bfloat16):
    entries = scale * jax.random.normal(own_key, extent, jnp.float32)
    if cuts:
        entries = entries * steps_of(own_key, extent, cuts, -0.22, 0.18)
    return jnp.clip(entries, -reach, reach).astype(kind)


def noise_with(own_key, dims, deviation, most, cuts, heavy, held_as=jnp.bfloat16):
    values = deviation * jax.random.normal(own_key, dims, jnp.float32)
    if cuts:
        values = values * steps_of(own_key, dims, cuts, -0.22, 0.18)
    return jnp.clip(spiked(values, jax.random.fold_in(own_key, 3), *heavy), -most, most).astype(held_as)


def setup_inputs(seed: int = 0) -> dict:
    key_list = jax.random.split(jax.random.key(seed), 13)
    visual = scatter_about(key_list[0], (VIS, D), 1.0, 6.0, ((0, 32),))
    query = scatter_about(key_list[1], (QUERIES, D), 1.0, 6.0, ((0, 32),))
    seg_ids = draw_seg_ids(jax.random.fold_in(key_list[12], 71), 0)
    shifts = plant(jax.random.randint(key_list[3], (PAGES, 2), 0, WIN), jax.random.fold_in(key_list[3], 1), 0, WIN - 1).astype(jnp.int32)
    valid_rows = plant(jax.random.randint(key_list[4], (PAGES,), PH // 2 + 1, PH + 1), jax.random.fold_in(key_list[4], 1), PH // 2 + 1, PH).astype(jnp.int32)
    attn_in = scatter_about(key_list[5], (4, D, 3, D), D ** -0.5, 0.21875, ((1, 16), (3, 2)), jnp.float32)
    attn_out = scatter_about(key_list[6], (4, D, D), (D // 32) ** -0.5, 1.25, ((1, 2), (2, 16)), jnp.float32)
    mlp_in = scatter_about(key_list[7], (2, D, FF), D ** -0.5, 0.21875, ((1, 16), (2, 2)), jnp.float32)
    mlp_out = scatter_about(key_list[8], (2, FF, D), FF ** -0.5, 0.109375, ((1, 2), (2, 16)), jnp.float32)
    gains = jnp.clip(1.0 + 0.1 * jax.random.normal(key_list[9], (6, D), jnp.float32), 0.5, 1.5)
    cot_visual = noise_with(key_list[10], (VIS, D), 1.0, 6.0, ((0, 32),), (0, 1, 32, 2.75))
    cot_query = noise_with(key_list[11], (QUERIES, D), 1.0, 6.0, ((0, 32),), (0, 1, 32, 2.75))
    return {"visual": visual, "query": query, "seg_ids": seg_ids, "shifts": shifts, "valid_rows": valid_rows, "attn_in": attn_in, "attn_out": attn_out, "mlp_in": mlp_in, "mlp_out": mlp_out, "gains": gains, "cot_visual": cot_visual, "cot_query": cot_query}


@jax.custom_vjp
def low(v):
    return lax.optimization_barrier(v.astype(jnp.bfloat16)).astype(jnp.float32)

@jax.custom_vjp
def low_back(v):
    return v

def low_keep(v):
    return (low(v), None)

def low_pass(kept, grad):
    return (grad,)

def back_keep(v):
    return (v, None)

def back_low(kept, grad):
    return (low(grad),)
low.defvjp(low_keep, low_pass)
low_back.defvjp(back_keep, back_low)
EPSILON = 1e-05
MASKED = -1e+30

def matmul(left_side, right_side):
    return jnp.dot(left_side, right_side, precision=lax.Precision.HIGHEST, preferred_element_type=jnp.float32)

def layer_norm(row_block, gain_row):
    average = lax.optimization_barrier(jnp.mean(row_block, axis=-1, keepdims=True))
    centred = row_block - average
    return centred * lax.rsqrt(lax.optimization_barrier(jnp.mean(centred * centred, axis=-1, keepdims=True)) + EPSILON) * gain_row

def tile_grid(page_grid):
    tiled = page_grid.reshape(PH // WIN, WIN, PW // WIN, WIN, -1).transpose(0, 2, 1, 3, 4)
    return tiled.reshape(PH // WIN * (PW // WIN), WIN * WIN, -1)

def untile_grid(blocks):
    page_grid = blocks.reshape(PH // WIN, PW // WIN, WIN, WIN, -1).transpose(0, 2, 1, 3, 4)
    return page_grid.reshape(PH, PW, -1)

def to_windows(row_block, offset):
    page_grid = jnp.roll(row_block.reshape(PH, PW, -1), (-offset[0], -offset[1]), axis=(0, 1))
    return tile_grid(page_grid)

def from_windows(blocks, offset):
    page_grid = jnp.roll(untile_grid(blocks), (offset[0], offset[1]), axis=(0, 1))
    return page_grid.reshape(PH * PW, -1)

def window_mask(offset, rows_valid):
    row_place = jnp.arange(PH, dtype=jnp.int32) + offset[0]
    col_place = jnp.arange(PW, dtype=jnp.int32) + offset[1]
    region = (row_place >= PH).astype(jnp.int32)[:, None] * 2 + (col_place >= PW).astype(jnp.int32)[None, :]
    usable_rows = jnp.broadcast_to((row_place % PH < rows_valid)[:, None], (PH, PW)).astype(jnp.int32)
    regions = tile_grid(region[:, :, None])[:, :, 0]
    usable = tile_grid(usable_rows[:, :, None])[:, :, 0] > 0
    same_region = regions[:, :, None] == regions[:, None, :]
    itself = jnp.eye(WIN * WIN, dtype=bool)[None]
    return same_region & (usable[:, None, :] | itself)

def attend(queries, keys, values, allowed):
    logit_scale = HD ** (-0.5)

    def heads_first(block):
        return block.reshape(block.shape[0], block.shape[1], HEADS, HD).transpose(2, 0, 1, 3)

    def one_head(head_parts):
        per_head_queries, per_head_keys, per_head_values = head_parts
        attention_logits = jnp.einsum('jty,joy->jto', per_head_queries, per_head_keys, precision=lax.Precision.HIGHEST) * logit_scale
        attention_logits = low_back(jnp.where(allowed, attention_logits, MASKED))
        highest = lax.optimization_barrier(jnp.max(attention_logits, axis=-1, keepdims=True))
        weights = jnp.exp(attention_logits - highest)
        attention_probs = low(weights / lax.optimization_barrier(jnp.sum(weights, axis=-1, keepdims=True)))
        blended_rows = jnp.einsum('osy,oya->osa', attention_probs, per_head_values, precision=lax.Precision.HIGHEST)
        return low_back(low(blended_rows))
    outputs = lax.map(jax.checkpoint(one_head), (heads_first(queries), heads_first(keys), heads_first(values)))
    return outputs.transpose(1, 2, 0, 3).reshape(queries.shape)

def attention_branch(query_rows, source_rows, weight_in, weight_out, allowed, arrange, restore):
    queries = low_back(low(matmul(query_rows, weight_in[:, 0])))
    keys = low_back(low(matmul(source_rows, weight_in[:, 1])))
    values = low_back(low(matmul(source_rows, weight_in[:, 2])))
    blended_rows = restore(attend(arrange(queries), arrange(keys), arrange(values), allowed))
    return low_back(matmul(blended_rows, weight_out))

def mlp_branch(row_block, weight_up, weight_down):
    hidden = low_back(matmul(row_block, weight_up))
    active = low(jax.nn.gelu(hidden, approximate=False))
    return low_back(matmul(active, weight_down))

def add_batch(row_block):
    return row_block[None]

def drop_batch(blocks):
    return blocks[0]

def page_layer(visual_in, query_in, params, segment, offset, rows_valid):
    master_in, master_out, master_up, master_down, master_gain = params
    weight_in = low(master_in)
    weight_out = low(master_out)
    mlp_up = low(master_up)
    mlp_down = low(master_down)
    gain_rows = low(master_gain)
    win_allowed = window_mask(offset, rows_valid)
    self_allowed = (segment[:, None] == segment[None, :])[None]
    patch_rows = jnp.arange(PH * PW, dtype=jnp.int32) // PW
    read_allowed = (patch_rows < rows_valid)[None, None, :]
    open_allowed = jnp.ones((1, 1, 1), dtype=bool)

    def windows_in(row_block):
        return to_windows(row_block, offset)

    def windows_out(blocks):
        return from_windows(blocks, offset)
    norm_win = low(layer_norm(visual_in, gain_rows[0]))
    norm_self = low(layer_norm(query_in, gain_rows[1]))
    visual_one = visual_in + attention_branch(norm_win, norm_win, weight_in[0], weight_out[0], win_allowed, windows_in, windows_out)
    query_one = query_in + attention_branch(norm_self, norm_self, weight_in[1], weight_out[1], self_allowed, add_batch, drop_batch)
    norm_vis = low(layer_norm(visual_one, gain_rows[2]))
    norm_qry = low(layer_norm(query_one, gain_rows[3]))
    query_two = query_one + attention_branch(norm_qry, norm_vis, weight_in[2], weight_out[2], read_allowed, add_batch, drop_batch)
    visual_two = visual_one + attention_branch(norm_vis, norm_qry, weight_in[3], weight_out[3], open_allowed, add_batch, drop_batch)
    visual_three = visual_two + mlp_branch(low(layer_norm(visual_two, gain_rows[4])), mlp_up[0], mlp_down[0])
    query_three = query_two + mlp_branch(low(layer_norm(query_two, gain_rows[5])), mlp_up[1], mlp_down[1])
    return (visual_three, query_three)

def reference(visual, query, seg_ids, shifts, valid_rows, attn_in, attn_out, mlp_in, mlp_out, gains, cot_visual, cot_query):
    params = (attn_in, attn_out, mlp_in, mlp_out, gains)
    visual_pages = visual.astype(jnp.float32).reshape(PAGES, PH * PW, D)
    query_pages = query.astype(jnp.float32).reshape(PAGES, Q, D)
    cot_vis_pages = cot_visual.astype(jnp.float32).reshape(PAGES, PH * PW, D)
    cot_qry_pages = cot_query.astype(jnp.float32).reshape(PAGES, Q, D)

    def one_page(totals, page_data):
        visual_in, query_in, segment, offset, rows_valid, cot_vis, cot_qry = page_data

        def forward(visual_rows, query_rows, weights):
            return page_layer(visual_rows, query_rows, weights, segment, offset, rows_valid)
        outputs, pullback = jax.vjp(forward, visual_in, query_in, params)
        grad_vis, grad_qry, grad_params = pullback((cot_vis, cot_qry))
        totals = jax.tree.map(jnp.add, totals, grad_params)
        return (totals, (outputs[0].astype(jnp.bfloat16), outputs[1].astype(jnp.bfloat16), grad_vis.astype(jnp.bfloat16), grad_qry.astype(jnp.bfloat16)))
    zeros = jax.tree.map(jnp.zeros_like, params)
    totals, results = lax.scan(one_page, zeros, (visual_pages, query_pages, seg_ids, shifts, valid_rows, cot_vis_pages, cot_qry_pages))
    out_visual, out_query, grad_visual, grad_query = results
    return (out_visual.reshape(PAGES * PH * PW, D), out_query.reshape(PAGES * Q, D), grad_visual.reshape(PAGES * PH * PW, D), grad_query.reshape(PAGES * Q, D), totals[0], totals[1], totals[2], totals[3], totals[4])
```

```python
import jax
import jax.numpy as jnp
from jax import lax
from jax.experimental import pallas as pl
from jax.experimental.pallas import tpu as pltpu
from jax.sharding import PartitionSpec as P

PH = 36
PW = 12
SCALE = 0.125
EPSILON = 1e-05
MASKED = -1e30
ROOT_HALF = 0.7071067811865476
INV_ROOT_TAU = 0.3989422804014327
F32 = jnp.float32
BF16 = jnp.bfloat16
WIDE = 1152
HALF = 384


def nn(a, b):
    return lax.dot_general(a, b, (((1,), (0,)), ((), ())), preferred_element_type=F32)


def nt(a, b):
    return lax.dot_general(a, b, (((1,), (1,)), ((), ())), preferred_element_type=F32)


def tn(a, b):
    return lax.dot_general(a, b, (((0,), (0,)), ((), ())), preferred_element_type=F32)


def unit_of(s):
    centred = s - jnp.mean(s, axis=-1, keepdims=True)
    inverse = lax.rsqrt(jnp.mean(centred * centred, axis=-1, keepdims=True) + EPSILON)
    return centred * inverse, inverse


def norm_back(dn, u, inverse, gain):
    scaled = dn * gain
    centre = jnp.mean(scaled, axis=-1, keepdims=True)
    slope = jnp.mean(scaled * u, axis=-1, keepdims=True)
    return inverse * (scaled - centre - u * slope)


def assemble(dst, own, other, t):
    half = own.shape[0]
    dst[pl.ds(pl.multiple_of(t * half, 8), half), :] = own[...].astype(F32)
    dst[pl.ds(pl.multiple_of((1 - t) * half, 8), half), :] = other[...].astype(F32)


def own_rows(ref, which, half):
    return ref[pl.ds(pl.multiple_of(which * half, 8), half), :]


def head_mask(h, value):
    lane = lax.broadcasted_iota(jnp.int32, (1, 128), 1)
    return jnp.where((lane >= 64) == (h == 1), value, 0.0).astype(BF16)


def twelfth(v):
    return lax.shift_right_logical(v * 43691, 19)


def places(shape, axis, scal):
    a, b = scal[1], scal[2]
    i = lax.broadcasted_iota(jnp.int32, shape, axis)
    r = twelfth(i)
    c = i - 12 * r
    rolled = jnp.where(r < a, r - a + PH, r - a)
    region = jnp.where(r < a, 2, 0) + jnp.where(c < b, 1, 0)
    return i, r, twelfth(rolled) * 4 + region


def window_bias(n, scal, key_axis):
    shape_k = (1, n) if key_axis == 1 else (n, 1)
    shape_q = (n, 1) if key_axis == 1 else (1, n)
    ik, rk, pk = places(shape_k, key_axis, scal)
    iq, _, pq = places(shape_q, 1 - key_axis, scal)
    usable = jnp.where(rk < scal[3], pk, -1)
    allowed = (usable == pq) | (ik == iq)
    return jnp.where(allowed, 0.0, MASKED).astype(F32)


def read_bias(n, scal, key_axis):
    shape = (1, n) if key_axis == 1 else (n, 1)
    i = lax.broadcasted_iota(jnp.int32, shape, key_axis)
    return jnp.where(twelfth(i) < scal[3], 0.0, MASKED).astype(F32)


def attend(q_ref, q_at, kv_ref, k_at, v_at, bias, o_ref):
    lane = lax.broadcasted_iota(jnp.int32, (1, 128), 1)
    for pair in range(3):
        at = pair * 128
        q = q_ref[:, q_at + at : q_at + at + 128]
        k = kv_ref[:, k_at + at : k_at + at + 128]
        v = kv_ref[:, v_at + at : v_at + at + 128]
        outs = []
        for h in range(2):
            s = nt(q * head_mask(h, SCALE), k)
            if bias is not None:
                s = s + bias
            e = jnp.exp(s - jnp.max(s, axis=1, keepdims=True))
            total = jnp.sum(e, axis=1, keepdims=True)
            outs.append(nn(e.astype(BF16), v) * (1.0 / total))
        o_ref[:, at : at + 128] = jnp.where(lane < 64, outs[0], outs[1]).astype(BF16)


def attend_back(q_ref, q_at, kv_ref, k_at, v_at, bias, do, dq_ref, dq_at, dk_ref, dk_at, dv_at):
    for pair in range(3):
        at = pair * 128
        q = q_ref[:, q_at + at : q_at + at + 128]
        k = kv_ref[:, k_at + at : k_at + at + 128]
        v = kv_ref[:, v_at + at : v_at + at + 128]
        dop = do[:, at : at + 128]
        dq, dk, dv = 0.0, 0.0, 0.0
        for h in range(2):
            keep = head_mask(h, 1.0)
            qm = q * head_mask(h, SCALE)
            dom = dop * keep
            s = nt(k, qm)
            if bias is not None:
                s = s + bias
            e = jnp.exp(s - jnp.max(s, axis=0, keepdims=True))
            p = e * (1.0 / jnp.sum(e, axis=0, keepdims=True))
            dp = nt(v, dom)
            delta = jnp.sum(p * dp, axis=0, keepdims=True)
            ds = (p * (dp - delta)).astype(BF16)
            dv = dv + nn(p.astype(BF16), dom)
            dk = dk + nn(ds, qm)
            dq = dq + tn(ds, k * keep)
        dq_ref[:, dq_at + at : dq_at + at + 128] = (dq * SCALE).astype(BF16)
        dk_ref[:, dk_at + at : dk_at + at + 128] = dk.astype(BF16)
        dk_ref[:, dv_at + at : dv_at + at + 128] = dv.astype(BF16)


def first_kernel(windowed, index, *refs):
    if windowed:
        scal, own, other, gains, w, s_ref, n_ref, qkv, o_ref, gr_ref = refs
    else:
        scal, own, other, gains, w, seg_c, seg_r, s_ref, n_ref, qkv, o_ref = refs
    assemble(s_ref, own, other, scal[0])
    gr = gains[...].astype(F32).T[0:8, :]
    if windowed:
        gr_ref[...] = gr
    u, _ = unit_of(s_ref[...])
    n = (u * gr[index : index + 1, :]).astype(BF16)
    n_ref[...] = n
    qkv[...] = nn(n, w[...]).astype(BF16)
    if windowed:
        bias = window_bias(qkv.shape[0], scal, 1)
    else:
        bias = jnp.where(seg_c[...] == seg_r[...], 0.0, MASKED).astype(F32)
    attend(qkv, 0, qkv, HALF, 2 * HALF, bias, o_ref)


def middle_kernel(index, s, o_own, o_oth, ao_own, ao_oth, gr, w, s1, n_ref, proj):
    branch = nt(o_own[...], ao_own[...]) + nt(o_oth[...], ao_oth[...])
    stream = s[...] + branch
    s1[...] = stream
    u, _ = unit_of(stream)
    n = (u * gr[index : index + 1, :]).astype(BF16)
    n_ref[...] = n
    proj[...] = nn(n, w[...]).astype(BF16)


def cross_kernel(masked, scal, q_ref, kv_ref, o_ref):
    bias = read_bias(kv_ref.shape[0], scal, 1) if masked else None
    attend(q_ref, 0, kv_ref, HALF, 2 * HALF, bias, o_ref)


def mlp_kernel(index, steps, scal, s1, o_own, o_oth, ao_own, ao_oth, gr, cot_own, cot_oth, w_in, w_out,
               s2, send, keep, dn_ref, dg_ref, dm_ref, n_s, dy_s, nt_s, dyt_s, part_s, dn_s, cot_s):
    step = pl.program_id(0)
    half = cot_own.shape[0]
    t = scal[0]

    @pl.when(step == 0)
    def _():
        branch = nt(o_own[...], ao_own[...]) + nt(o_oth[...], ao_oth[...])
        stream = s1[...] + branch
        s2[...] = stream
        u, _ = unit_of(stream)
        n = (u * gr[index : index + 1, :]).astype(BF16)
        n_s[...] = n
        nt_s[...] = n.T
        assemble(cot_s, cot_own, cot_oth, t)
        dy = cot_s[...].astype(BF16)
        dy_s[...] = dy
        dyt_s[...] = dy.T

    hidden = nn(n_s[...], w_in[...])
    phi = 0.5 * (1.0 + lax.erf(hidden * ROOT_HALF))
    act = (hidden * phi).astype(BF16)
    slope = phi + hidden * jnp.exp(-0.5 * hidden * hidden) * INV_ROOT_TAU
    dh = (nn(dy_s[...], w_out[...]) * slope).astype(BF16)
    part = nt(act, w_out[...])
    dn = nt(dh, w_in[...])

    @pl.when(step == 0)
    def _():
        part_s[...] = part
        dn_s[...] = dn

    @pl.when(step > 0)
    def _():
        part_s[...] += part
        dn_s[...] += dn

    fb = w_in.shape[1]
    dm_ref[:, 0:fb] = nn(nt_s[...], dh).astype(BF16)
    dm_ref[:, fb : 2 * fb] = nn(dyt_s[...], act).astype(BF16)

    @pl.when(step == steps - 1)
    def _():
        send[...] = own_rows(part_s, 1 - t, half).astype(BF16)
        keep[...] = own_rows(part_s, t, half) + own_rows(s2, t, half)
        dn_all = dn_s[...]
        dn_ref[...] = dn_all.astype(BF16)
        u, _ = unit_of(s2[...])
        dg_ref[...] = jnp.sum(dn_all * u, axis=0, keepdims=True)


def cross_back_kernel(masked, index, scal, cot_own, cot_oth, dn_own, dn_oth, s2, gr, ao_own, q_ref, kv_ref,
                      g_ref, dy_ref, dq_ref, dkv_ref):
    assemble(g_ref, cot_own, cot_oth, scal[0])
    u, inverse = unit_of(s2[...])
    dn = dn_own[...].astype(F32) + dn_oth[...].astype(F32)
    grad = g_ref[...] + norm_back(dn, u, inverse, gr[index : index + 1, :])
    g_ref[...] = grad
    dy = grad.astype(BF16)
    dy_ref[...] = dy
    do = nn(dy, ao_own[...]).astype(BF16)
    bias = read_bias(kv_ref.shape[0], scal, 0) if masked else None
    attend_back(q_ref, 0, kv_ref, HALF, 2 * HALF, bias, do, dq_ref, 0, dkv_ref, 0, HALF)


def dn_kernel(dq, dkv, w, s1, dn_ref, dg_ref):
    dn = nt(dq[...], w[:, 0:HALF]) + nt(dkv[...], w[:, HALF:WIDE])
    dn_ref[...] = dn.astype(BF16)
    u, _ = unit_of(s1[...])
    dg_ref[...] = jnp.sum(dn * u, axis=0, keepdims=True)


def middle_weights_kernel(nv, nq, dq3, dkv2, dq2, dkv3, dyv, o_look, dyq, o_read, out):
    out[:, 0:HALF] = tn(nv[...], dq3[...]).astype(BF16)
    out[:, HALF:WIDE] = tn(nv[...], dkv2[...]).astype(BF16)
    out[:, WIDE : WIDE + HALF] = tn(nq[...], dq2[...]).astype(BF16)
    out[:, WIDE + HALF : 2 * WIDE] = tn(nq[...], dkv3[...]).astype(BF16)
    out[:, 2 * WIDE : 2 * WIDE + HALF] = tn(dyq[...], o_read[...]).astype(BF16)
    out[:, 2 * WIDE + HALF : 2 * WIDE + 2 * HALF] = tn(dyv[...], o_look[...]).astype(BF16)


def first_back_kernel(windowed, index, later, scal, *refs):
    if windowed:
        grad, dn_own, dn_oth, s1, s0, gr, ao_own, w, qkv, g_ref, dy_ref, dqkv, send, keep, dg_ref, g_s = refs
    else:
        (grad, dn_own, dn_oth, s1, s0, gr, ao_own, w, qkv, seg_c, seg_r,
         g_ref, dy_ref, dqkv, send, keep, dg_ref, g_s) = refs
    t = scal[0]
    half = g_ref.shape[0]
    u, inverse = unit_of(s1[...])
    dn = dn_own[...].astype(F32) + dn_oth[...].astype(F32)
    g = grad[...] + norm_back(dn, u, inverse, gr[later : later + 1, :])
    g_s[...] = g
    g_ref[...] = own_rows(g_s, t, half)
    dy = g.astype(BF16)
    dy_ref[...] = dy
    do = nn(dy, ao_own[...]).astype(BF16)
    if windowed:
        bias = window_bias(qkv.shape[0], scal, 0)
    else:
        bias = jnp.where(seg_c[...] == seg_r[...], 0.0, MASKED).astype(F32)
    attend_back(qkv, 0, qkv, HALF, 2 * HALF, bias, do, dqkv, 0, dqkv, HALF, 2 * HALF)
    dn0 = nt(dqkv[...], w[...])
    g_s[...] = dn0
    send[...] = own_rows(g_s, 1 - t, half).astype(BF16)
    keep[...] = own_rows(g_s, t, half)
    u, _ = unit_of(s0[...])
    dg_ref[...] = jnp.sum(dn0 * u, axis=0, keepdims=True)


def first_weights_kernel(n0, n1, d0, d1, dy0, o0, dy1, o1, g0, g1, g2, g3, g4, g5, out, rows):
    out[:, 0:WIDE] = tn(n0[...], d0[...]).astype(BF16)
    out[:, WIDE : 2 * WIDE] = tn(n1[...], d1[...]).astype(BF16)
    out[:, 2 * WIDE : 2 * WIDE + HALF] = tn(dy0[...], o0[...]).astype(BF16)
    out[:, 2 * WIDE + HALF : 2 * WIDE + 2 * HALF] = tn(dy1[...], o1[...]).astype(BF16)
    rows[...] = jnp.zeros_like(rows)
    for i, g in enumerate((g0, g1, g2, g3, g4, g5)):
        rows[i : i + 1, :] = g[...]
    out[:, 2 * WIDE + 2 * HALF :] = rows[...].T.astype(BF16)


def last_kernel(index, grad, keep, got, own, gr, out):
    u, inverse = unit_of(own[...].astype(F32))
    dn = keep[...] + got[...].astype(F32)
    out[...] = (grad[...] + norm_back(dn, u, inverse, gr[index : index + 1, :])).astype(BF16)


SMEM = pl.BlockSpec(memory_space=pltpu.SMEM)
FULL = None


def call(body, args, specs, outs, name, flops, scratch=(), grid=(1,), out_specs=None):
    def whole(shape):
        return pl.BlockSpec(shape, lambda *_: (0,) * len(shape))

    in_specs = [whole(a.shape) if s is FULL else s for a, s in zip(args, specs)]
    out_specs = [whole(o.shape) if s is FULL else s for o, s in zip(outs, out_specs or [FULL] * len(outs))]
    moved = sum(a.size * a.dtype.itemsize for a in outs)
    for a, s in zip(args, in_specs):
        size = a.size if s.block_shape is None else min(a.size, s.block_shape[0] * s.block_shape[1] * grid[0])
        moved += size * a.dtype.itemsize
    return pl.pallas_call(
        body,
        out_shape=outs,
        grid=grid,
        in_specs=in_specs,
        out_specs=out_specs,
        scratch_shapes=list(scratch),
        name=name,
        compiler_params=pltpu.CompilerParams(vmem_limit_bytes=56 * 2**20),
        cost_estimate=pl.CostEstimate(flops=int(flops), bytes_accessed=int(moved), transcendentals=0),
    )(*args)


def cols(width, at):
    return pl.BlockSpec((768, width), lambda *_: (0, at))


def part(body, *fixed):
    return lambda *refs: body(*fixed, *refs)


def sds(shape, dtype):
    return jax.ShapeDtypeStruct(shape, dtype)


def on_device(visual, query, seg_ids, shifts, valid_rows, attn_in, attn_out, mlp_in, mlp_out, gains, cot_visual, cot_query):
    def swap(a):
        return lax.ppermute(a, "tensor", [(0, 1), (1, 0)])

    def gather(a):
        return lax.all_gather(a, "dp", axis=0, tiled=True)

    def scatter(a):
        return lax.psum_scatter(a, "dp", scatter_dimension=0, tiled=True)

    depth = gains.shape[1]
    rv, rq = 2 * visual.shape[0], 2 * query.shape[0]
    t = lax.axis_index("tensor").astype(jnp.int32)
    scal = jnp.concatenate([t[None], shifts[0], valid_rows])
    seg_r = seg_ids
    seg_c = seg_ids.reshape(-1, 1)

    x_oth, q_oth = swap(visual), swap(query)
    a_in = attn_in.astype(BF16)
    gain_cols = jnp.pad(gains.T.astype(BF16), ((0, 0), (0, 122)))
    g1 = gather(jnp.concatenate([a_in[0].reshape(depth, WIDE), a_in[1].reshape(depth, WIDE), gain_cols], axis=1))
    aot = attn_out.astype(BF16).transpose(2, 0, 1).reshape(depth, 4 * HALF)
    aot = gather(jnp.concatenate([aot, swap(aot)], axis=1))
    g2 = gather(jnp.concatenate([a_in[3][:, 0], a_in[2][:, 1], a_in[2][:, 2], a_in[2][:, 0], a_in[3][:, 1], a_in[3][:, 2]], axis=1))
    m_in = mlp_in.astype(BF16)
    m_out = mlp_out.astype(BF16).transpose(0, 2, 1)
    g3 = gather(jnp.concatenate([m_in[0], m_out[0], m_in[1], m_out[1]], axis=1))
    cv_oth, cq_oth = swap(cot_visual), swap(cot_query)

    def first(windowed, own, other, at, rows):
        args = [scal, own, other, g1, g1]
        specs = [SMEM, FULL, FULL, cols(128, 18), cols(WIDE, at)]
        outs = [sds((rows, 768), F32), sds((rows, 768), BF16), sds((rows, WIDE), BF16), sds((rows, HALF), BF16)]
        if windowed:
            outs.append(sds((8, 768), F32))
        else:
            args += [seg_c, seg_r]
            specs += [FULL, FULL]
        return call(part(first_kernel, windowed, at), args, specs, outs, "first_%d" % at, 4e9)

    sv0, nv0, qkv0, o0, gr = first(True, visual, x_oth, 0, rv)
    o0_oth = swap(o0)
    sq0, nq0, qkv1, o1 = first(False, query, q_oth, 1, rq)
    o1_oth = swap(o1)

    def middle(index, s, o, o_oth, a, at, rows):
        return call(
            part(middle_kernel, index), [s, o, o_oth, aot, aot, gr, g2],
            [FULL, FULL, FULL, cols(HALF, a), cols(HALF, 4 + a), FULL, cols(WIDE, at)],
            [sds((rows, 768), F32), sds((rows, 768), BF16), sds((rows, WIDE), BF16)], "middle_%d" % at, 2e9)

    sv1, nv, pv = middle(2, sv0, o0, o0_oth, 0, 0, rv)
    sq1, nq, pq = middle(3, sq0, o1, o1_oth, 1, 1, rq)

    def cross(masked, q, kv, name):
        return call(part(cross_kernel, masked), [scal, q, kv], [SMEM, FULL, FULL], [sds((q.shape[0], HALF), BF16)], name, 2e9)[0]

    o3 = cross(False, pv, pq, "look")
    o3_oth = swap(o3)
    o2 = cross(True, pq, pv, "read")
    o2_oth = swap(o2)

    fb = 512
    steps = 1536 // fb

    def mlp(index, s1, o, o_oth, a, cot, cot_oth, m, rows):
        half = rows // 2

        def block(at):
            return pl.BlockSpec((768, fb), lambda i: (0, at * steps + i))

        return call(
            part(mlp_kernel, index, steps), [scal, s1, o, o_oth, aot, aot, gr, cot, cot_oth, g3, g3],
            [SMEM, FULL, FULL, FULL, cols(HALF, a), cols(HALF, 4 + a), FULL, FULL, FULL, block(2 * m), block(2 * m + 1)],
            [sds((rows, 768), F32), sds((half, 768), BF16), sds((half, 768), F32), sds((rows, 768), BF16),
             sds((1, 768), F32), sds((768, 3072), BF16)], "mlp_%d" % m, 10 * rows * 768 * 1536,
            scratch=[pltpu.VMEM((rows, 768), BF16), pltpu.VMEM((rows, 768), BF16), pltpu.VMEM((768, rows), BF16),
                     pltpu.VMEM((768, rows), BF16), pltpu.VMEM((rows, 768), F32), pltpu.VMEM((rows, 768), F32),
                     pltpu.VMEM((rows, 768), F32)],
            grid=(steps,), out_specs=[FULL] * 5 + [pl.BlockSpec((768, 2 * fb), lambda i: (0, i))])

    sv2, part_v, keep_v, dnv4, dg4, dm0 = mlp(4, sv1, o3, o3_oth, 3, cot_visual, cv_oth, 0, rv)
    dnv4_oth = swap(dnv4)
    sq2, part_q, keep_q, dnq5, dg5, dm1 = mlp(5, sq1, o2, o2_oth, 2, cot_query, cq_oth, 1, rq)
    dnq5_oth = swap(dnq5)
    s3v, s3q = scatter(dm0), scatter(dm1)
    out_visual = (keep_v + swap(part_v).astype(F32)).astype(BF16)
    out_query = (keep_q + swap(part_q).astype(F32)).astype(BF16)

    def cross_back(masked, index, cot, cot_oth, dn, dn_oth, s2, a, q, kv, name):
        return call(
            part(cross_back_kernel, masked, index), [scal, cot, cot_oth, dn, dn_oth, s2, gr, aot, q, kv],
            [SMEM, FULL, FULL, FULL, FULL, FULL, FULL, cols(HALF, a), FULL, FULL],
            [sds((q.shape[0], 768), F32), sds((q.shape[0], 768), BF16), sds((q.shape[0], HALF), BF16), sds((kv.shape[0], 768), BF16)],
            name, 6e9)

    gv2, dyv, dq3, dkv3 = cross_back(False, 4, cot_visual, cv_oth, dnv4, dnv4_oth, sv2, 3, pv, pq, "look_back")
    gq2, dyq, dq2, dkv2 = cross_back(True, 5, cot_query, cq_oth, dnq5, dnq5_oth, sq2, 2, pq, pv, "read_back")

    def dn_of(dq, dkv, at, s1, rows):
        return call(dn_kernel, [dq, dkv, g2, s1], [FULL, FULL, cols(WIDE, at), FULL],
                    [sds((rows, 768), BF16), sds((1, 768), F32)], "dn_%d" % at, 1e9)

    dnv2, dg2 = dn_of(dq3, dkv2, 0, sv1, rv)
    dnv2_oth = swap(dnv2)
    dnq3, dg3 = dn_of(dq2, dkv3, 1, sq1, rq)
    dnq3_oth = swap(dnq3)
    args = [nv, nq, dq3, dkv2, dq2, dkv3, dyv, o3, dyq, o2]
    (dw2,) = call(middle_weights_kernel, args, [FULL] * len(args), [sds((768, 2 * WIDE + 2 * HALF), BF16)], "middle_weights", 2.5e9)
    s2 = scatter(dw2)

    def first_back(windowed, index, later, grad, dn, dn_oth, s1, s0, a, qkv, rows):
        half = rows // 2
        args = [scal, grad, dn, dn_oth, s1, s0, gr, aot, g1, qkv]
        specs = [SMEM, FULL, FULL, FULL, FULL, FULL, FULL, cols(HALF, a), cols(WIDE, a), FULL]
        if not windowed:
            args += [seg_c, seg_r]
            specs += [FULL, FULL]
        outs = [sds((half, 768), F32), sds((rows, 768), BF16), sds((rows, WIDE), BF16), sds((half, 768), BF16),
                sds((half, 768), F32), sds((1, 768), F32)]
        return call(part(first_back_kernel, windowed, index, later), args, specs, outs, "first_back_%d" % a, 7e9,
                    scratch=[pltpu.VMEM((rows, 768), F32)])

    gv1, dy0, d0, send_v, hold_v, dg0 = first_back(True, 0, 2, gv2, dnv2, dnv2_oth, sv1, sv0, 0, qkv0, rv)
    got_v = swap(send_v)
    gq1, dy1, d1, send_q, hold_q, dg1 = first_back(False, 1, 3, gq2, dnq3, dnq3_oth, sq1, sq0, 1, qkv1, rq)
    got_q = swap(send_q)
    args = [nv0, nq0, d0, d1, dy0, o0, dy1, o1, dg0, dg1, dg2, dg3, dg4, dg5]
    (dw1,) = call(first_weights_kernel, args, [FULL] * len(args), [sds((768, 2 * WIDE + 2 * HALF + 128), BF16)],
                  "first_weights", 3e9, scratch=[pltpu.VMEM((128, 768), F32)])
    s1 = scatter(dw1)

    def last(index, grad, keep, got, own):
        return call(part(last_kernel, index), [grad, keep, got, own, gr], [FULL] * 5, [sds(own.shape, BF16)], "last_%d" % index, 1e7)[0]

    grad_visual = last(0, gv1, hold_v, got_v, visual)
    grad_query = last(1, gq1, hold_q, got_q, query)

    def slots(a):
        return a.reshape(depth, 3, HALF)

    v2, q2 = slots(s2[:, 0:WIDE]), slots(s2[:, WIDE : 2 * WIDE])
    in2 = jnp.stack([q2[:, 0], v2[:, 1], v2[:, 2]], axis=1)
    in3 = jnp.stack([v2[:, 0], q2[:, 1], q2[:, 2]], axis=1)
    grad_in = jnp.stack([slots(s1[:, 0:WIDE]), slots(s1[:, WIDE : 2 * WIDE]), in2, in3]).astype(F32)
    base = 2 * WIDE
    grad_out = jnp.stack([s1[:, base : base + HALF].T, s1[:, base + HALF : base + 2 * HALF].T,
                          s2[:, base : base + HALF].T, s2[:, base + HALF : base + 2 * HALF].T]).astype(F32)
    m3 = jnp.stack([s3v, s3q]).reshape(2, depth, steps, 2, fb)
    grad_up = m3[:, :, :, 0].reshape(2, depth, 1536).astype(F32)
    grad_down = m3[:, :, :, 1].reshape(2, depth, 1536).transpose(0, 2, 1).astype(F32)
    gsum = s1[:, base + 2 * HALF :].astype(F32)
    gsum = gsum + swap(gsum)
    grad_gain = gsum[:, 0:6].T
    return out_visual, out_query, grad_visual, grad_query, grad_in, grad_out, grad_up, grad_down, grad_gain


def solution(mesh):
    rows = P(("dp", "tensor"), None)
    weights = (P(None, "dp", None, "tensor"), P(None, "tensor", "dp"), P(None, "dp", "tensor"), P(None, "tensor", "dp"), P(None, "dp"))
    in_specs = (rows, rows, P("dp", None), P("dp", None), P("dp")) + weights + (rows, rows)
    out_specs = (rows, rows, rows, rows) + weights
    return jax.shard_map(on_device, mesh=mesh, in_specs=in_specs, out_specs=out_specs, check_vma=False)
```

```python
import jax
import jax.numpy as jnp
from jax import lax
from jax.experimental import pallas as pl
from jax.experimental.pallas import tpu as pltpu
from jax.sharding import PartitionSpec as P

PH = 36
PW = 12
SCALE = 0.125
EPSILON = 1e-05
MASKED = -1e30
ROOT_HALF = 0.7071067811865476
INV_ROOT_TAU = 0.3989422804014327
F32 = jnp.float32
BF16 = jnp.bfloat16
WIDE = 1152
HALF = 384


def nn(a, b):
    return lax.dot_general(a, b, (((1,), (0,)), ((), ())), preferred_element_type=F32)


def nt(a, b):
    return lax.dot_general(a, b, (((1,), (1,)), ((), ())), preferred_element_type=F32)


def tn(a, b):
    return lax.dot_general(a, b, (((0,), (0,)), ((), ())), preferred_element_type=F32)


def unit_of(s):
    centred = s - jnp.mean(s, axis=-1, keepdims=True)
    inverse = lax.rsqrt(jnp.mean(centred * centred, axis=-1, keepdims=True) + EPSILON)
    return centred * inverse, inverse


def norm_back(dn, u, inverse, gain):
    scaled = dn * gain
    centre = jnp.mean(scaled, axis=-1, keepdims=True)
    slope = jnp.mean(scaled * u, axis=-1, keepdims=True)
    return inverse * (scaled - centre - u * slope)


def assemble(dst, own, other, t):
    half = own.shape[0]
    dst[pl.ds(pl.multiple_of(t * half, 8), half), :] = own[...].astype(F32)
    dst[pl.ds(pl.multiple_of((1 - t) * half, 8), half), :] = other[...].astype(F32)


def own_rows(ref, which, half):
    return ref[pl.ds(pl.multiple_of(which * half, 8), half), :]


def head_mask(h, value):
    lane = lax.broadcasted_iota(jnp.int32, (1, 128), 1)
    return jnp.where((lane >= 64) == (h == 1), value, 0.0).astype(BF16)


def twelfth(v):
    return lax.shift_right_logical(v * 43691, 19)


def places(shape, axis, scal):
    a, b = scal[1], scal[2]
    i = lax.broadcasted_iota(jnp.int32, shape, axis)
    r = twelfth(i)
    c = i - 12 * r
    rolled = jnp.where(r < a, r - a + PH, r - a)
    region = jnp.where(r < a, 2, 0) + jnp.where(c < b, 1, 0)
    return i, r, twelfth(rolled) * 4 + region


def window_bias(n, scal, key_axis):
    shape_k = (1, n) if key_axis == 1 else (n, 1)
    shape_q = (n, 1) if key_axis == 1 else (1, n)
    ik, rk, pk = places(shape_k, key_axis, scal)
    iq, _, pq = places(shape_q, 1 - key_axis, scal)
    usable = jnp.where(rk < scal[3], pk, -1)
    allowed = (usable == pq) | (ik == iq)
    return jnp.where(allowed, 0.0, MASKED).astype(F32)


def read_bias(n, scal, key_axis):
    shape = (1, n) if key_axis == 1 else (n, 1)
    i = lax.broadcasted_iota(jnp.int32, shape, key_axis)
    return jnp.where(twelfth(i) < scal[3], 0.0, MASKED).astype(F32)


def attend(q_ref, q_at, kv_ref, k_at, v_at, bias, o_ref):
    lane = lax.broadcasted_iota(jnp.int32, (1, 128), 1)
    for pair in range(3):
        at = pair * 128
        q = q_ref[:, q_at + at : q_at + at + 128]
        k = kv_ref[:, k_at + at : k_at + at + 128]
        v = kv_ref[:, v_at + at : v_at + at + 128]
        outs = []
        for h in range(2):
            s = nt(q * head_mask(h, SCALE), k)
            if bias is not None:
                s = s + bias
            e = jnp.exp(s - jnp.max(s, axis=1, keepdims=True))
            total = jnp.sum(e, axis=1, keepdims=True)
            outs.append(nn(e.astype(BF16), v) * (1.0 / total))
        o_ref[:, at : at + 128] = jnp.where(lane < 64, outs[0], outs[1]).astype(BF16)


def attend_back(q_ref, q_at, kv_ref, k_at, v_at, bias, do, dq_ref, dq_at, dk_ref, dk_at, dv_at):
    for pair in range(3):
        at = pair * 128
        q = q_ref[:, q_at + at : q_at + at + 128]
        k = kv_ref[:, k_at + at : k_at + at + 128]
        v = kv_ref[:, v_at + at : v_at + at + 128]
        dop = do[:, at : at + 128]
        dq, dk, dv = 0.0, 0.0, 0.0
        for h in range(2):
            keep = head_mask(h, 1.0)
            qm = q * head_mask(h, SCALE)
            dom = dop * keep
            s = nt(k, qm)
            if bias is not None:
                s = s + bias
            e = jnp.exp(s - jnp.max(s, axis=0, keepdims=True))
            p = e * (1.0 / jnp.sum(e, axis=0, keepdims=True))
            dp = nt(v, dom)
            delta = jnp.sum(p * dp, axis=0, keepdims=True)
            ds = (p * (dp - delta)).astype(BF16)
            dv = dv + nn(p.astype(BF16), dom)
            dk = dk + nn(ds, qm)
            dq = dq + tn(ds, k * keep)
        dq_ref[:, dq_at + at : dq_at + at + 128] = (dq * SCALE).astype(BF16)
        dk_ref[:, dk_at + at : dk_at + at + 128] = dk.astype(BF16)
        dk_ref[:, dv_at + at : dv_at + at + 128] = dv.astype(BF16)


def first_kernel(windowed, index, ws, *refs):
    if windowed:
        scal, own, other, s_ref, n_ref, qkv, o_ref, gr_ref = refs
    else:
        scal, own, other, gr, seg_c, seg_r, s_ref, n_ref, qkv, o_ref = refs
    assemble(s_ref, own, other, scal[0])
    u, _ = unit_of(s_ref[...])
    w = ws[0]()
    if windowed:
        gr = w[:, WIDE:].astype(F32).T[0:8, :]
        gr_ref[...] = gr
    n = (u * gr[index : index + 1, :]).astype(BF16)
    n_ref[...] = n
    qkv[...] = nn(n, w[:, 0:WIDE]).astype(BF16)
    if windowed:
        bias = window_bias(qkv.shape[0], scal, 1)
    else:
        bias = jnp.where(seg_c[...] == seg_r[...], 0.0, MASKED).astype(F32)
    attend(qkv, 0, qkv, HALF, 2 * HALF, bias, o_ref)


def middle_kernel(index, ws, scal, s, o_own, o_oth, gr, s1, n_ref, proj):
    branch = nt(o_own[...], ws[0]()[...]) + nt(o_oth[...], ws[1]()[...])
    stream = s[...] + branch
    s1[...] = stream
    u, _ = unit_of(stream)
    n = (u * gr[index : index + 1, :]).astype(BF16)
    n_ref[...] = n
    proj[...] = nn(n, ws[2]()[...]).astype(BF16)


def cross_kernel(masked, ws, scal, q_ref, kv_ref, o_ref):
    bias = read_bias(kv_ref.shape[0], scal, 1) if masked else None
    attend(q_ref, 0, kv_ref, HALF, 2 * HALF, bias, o_ref)


def mlp_kernel(index, steps, ws, scal, s1, o_own, o_oth, gr, cot_own, cot_oth,
               s2, send, keep, dn_ref, dg_ref, dm_ref, n_s, dy_s, nt_s, dyt_s, part_s, dn_s, cot_s):
    step = pl.program_id(0)
    half = cot_own.shape[0]
    t = scal[0]

    @pl.when(step == 0)
    def _():
        for w in ws:
            w.start()
        branch = nt(o_own[...], ws[0]()[...]) + nt(o_oth[...], ws[1]()[...])
        stream = s1[...] + branch
        s2[...] = stream
        u, _ = unit_of(stream)
        n = (u * gr[index : index + 1, :]).astype(BF16)
        n_s[...] = n
        nt_s[...] = n.T
        assemble(cot_s, cot_own, cot_oth, t)
        dy = cot_s[...].astype(BF16)
        dy_s[...] = dy
        dyt_s[...] = dy.T

    for i in range(steps):

        @pl.when(step == i)
        def _(i=i):
            ws[2](i)
            ws[3](i)

    fb = ws[2].width
    w_in = ws[2].stack[step]
    w_out = ws[3].stack[step]
    hidden = nn(n_s[...], w_in)
    phi = 0.5 * (1.0 + lax.erf(hidden * ROOT_HALF))
    act = (hidden * phi).astype(BF16)
    slope = phi + hidden * jnp.exp(-0.5 * hidden * hidden) * INV_ROOT_TAU
    dh = (nn(dy_s[...], w_out) * slope).astype(BF16)
    part = nt(act, w_out)
    dn = nt(dh, w_in)

    @pl.when(step == 0)
    def _():
        part_s[...] = part
        dn_s[...] = dn

    @pl.when(step > 0)
    def _():
        part_s[...] += part
        dn_s[...] += dn

    dm_ref[:, 0:fb] = nn(nt_s[...], dh).astype(BF16)
    dm_ref[:, fb : 2 * fb] = nn(dyt_s[...], act).astype(BF16)

    @pl.when(step == steps - 1)
    def _():
        send[...] = own_rows(part_s, 1 - t, half).astype(BF16)
        keep[...] = own_rows(part_s, t, half) + own_rows(s2, t, half)
        dn_all = dn_s[...]
        dn_ref[...] = dn_all.astype(BF16)
        u, _ = unit_of(s2[...])
        dg_ref[...] = jnp.sum(dn_all * u, axis=0, keepdims=True)


def cross_back_kernel(masked, index, ws, scal, cot_own, cot_oth, dn_own, dn_oth, s2, gr, q_ref, kv_ref,
                      g_ref, dy_ref, dq_ref, dkv_ref):
    assemble(g_ref, cot_own, cot_oth, scal[0])
    u, inverse = unit_of(s2[...])
    dn = dn_own[...].astype(F32) + dn_oth[...].astype(F32)
    grad = g_ref[...] + norm_back(dn, u, inverse, gr[index : index + 1, :])
    g_ref[...] = grad
    dy = grad.astype(BF16)
    dy_ref[...] = dy
    do = nn(dy, ws[0]()[...]).astype(BF16)
    bias = read_bias(kv_ref.shape[0], scal, 0) if masked else None
    attend_back(q_ref, 0, kv_ref, HALF, 2 * HALF, bias, do, dq_ref, 0, dkv_ref, 0, HALF)


def dn_kernel(ws, scal, dq, dkv, s1, dn_ref, dg_ref):
    w = ws[0]()
    dn = nt(dq[...], w[:, 0:HALF]) + nt(dkv[...], w[:, HALF:WIDE])
    dn_ref[...] = dn.astype(BF16)
    u, _ = unit_of(s1[...])
    dg_ref[...] = jnp.sum(dn * u, axis=0, keepdims=True)


def fill_weights(out, n, grads, dy, o):
    at = 0
    for grad in grads:
        width = grad.shape[1]
        out[:, at : at + width] = tn(n[...], grad[...]).astype(BF16)
        at += width
    out[:, at : at + HALF] = tn(dy[...], o[...]).astype(BF16)


def middle_weights_kernel(ws, scal, n, dq, dkv, dy, o, into, out):
    fill_weights(out, n, [dq, dkv], dy, o)


def first_weights_kernel(table, gains, ws, scal, n, d, dy, o, *refs):
    rows, refs = refs[:gains], refs[gains:]
    if table is None:
        out = refs[0]
    else:
        *dealt, out = refs[:3]
    fill_weights(out, n, [d], dy, o)
    if gains:
        stack = refs[-1]
        stack[...] = jnp.zeros_like(stack)
        for i, row in enumerate(rows):
            stack[i : i + 1, :] = row[...]
        out[:, WIDE + HALF :] = stack[...].T.astype(BF16)
    if table is not None:
        deal(out, dealt, scal, table)


def first_back_kernel(windowed, index, later, ws, scal, *refs):
    if windowed:
        grad, dn_own, dn_oth, s1, s0, gr, qkv, g_ref, dy_ref, dqkv, send, keep, dg_ref, g_s = refs
    else:
        (grad, dn_own, dn_oth, s1, s0, gr, qkv, seg_c, seg_r,
         g_ref, dy_ref, dqkv, send, keep, dg_ref, g_s) = refs
    t = scal[0]
    half = g_ref.shape[0]
    u, inverse = unit_of(s1[...])
    dn = dn_own[...].astype(F32) + dn_oth[...].astype(F32)
    g = grad[...] + norm_back(dn, u, inverse, gr[later : later + 1, :])
    g_s[...] = g
    g_ref[...] = own_rows(g_s, t, half)
    dy = g.astype(BF16)
    dy_ref[...] = dy
    do = nn(dy, ws[0]()[...]).astype(BF16)
    if windowed:
        bias = window_bias(qkv.shape[0], scal, 0)
    else:
        bias = jnp.where(seg_c[...] == seg_r[...], 0.0, MASKED).astype(F32)
    attend_back(qkv, 0, qkv, HALF, 2 * HALF, bias, do, dqkv, 0, dqkv, HALF, 2 * HALF)
    dn0 = nt(dqkv[...], ws[1]()[...])
    g_s[...] = dn0
    send[...] = own_rows(g_s, 1 - t, half).astype(BF16)
    keep[...] = own_rows(g_s, t, half)
    u, _ = unit_of(s0[...])
    dg_ref[...] = jnp.sum(dn0 * u, axis=0, keepdims=True)


def last_kernel(index, ws, scal, grad, keep, got, own, gr, out):
    u, inverse = unit_of(own[...].astype(F32))
    dn = keep[...] + got[...].astype(F32)
    out[...] = (grad[...] + norm_back(dn, u, inverse, gr[index : index + 1, :])).astype(BF16)


class Weight:
    def __init__(self, scal, pieces, rooms, sems, at, width, table):
        self.scal, self.pieces, self.rooms, self.sems = scal, pieces, rooms, sems
        self.at, self.width, self.table, self.waited = at, width, table, set()

    def start(self):
        for i, room in enumerate(self.rooms):
            if self.table is None:
                source = self.pieces[0].at[:, pl.ds(self.at + i * self.width, self.width)]
                pltpu.make_async_copy(source, room, self.sems[i]).start()
                continue
            for p in range(16):
                to = pl.multiple_of(self.scal[self.table + p] * 48, 16)
                pltpu.make_async_copy(
                    self.pieces[p // 8].at[pl.ds(p % 8 * 48, 48), pl.ds(self.at + i * self.width, self.width)],
                    room.at[pl.ds(to, 48), :],
                    self.sems[i],
                ).start()

    def __call__(self, i=0):
        if i not in self.waited:
            pltpu.make_async_copy(self.rooms[i], self.rooms[i], self.sems[i]).wait()
            self.waited.add(i)
        return self.rooms[i]


def deal(whole, outs, scal, table):
    for p in range(16):
        block = whole[pl.ds(pl.multiple_of(scal[table + p] * 48, 16), 48), :]
        outs[p // 8][p % 8 * 48 : p % 8 * 48 + 48, :] = block


TABLE_A = 4
TABLE_B = 20


def call(body, args, weights, outs, name, flops, scratch=(), grid=(1,), out_specs=None, into=None):
    def whole(shape):
        return pl.BlockSpec(shape, lambda *_: (0,) * len(shape))

    in_specs = [pl.BlockSpec(memory_space=pltpu.SMEM)] + [whole(a.shape) for a in args[1:]]
    if into is not None:
        in_specs[into] = pl.BlockSpec(memory_space=pl.ANY)
    out_specs = out_specs or [whole(o.shape) for o in outs]
    pieces = [piece for unit, _, _, _ in weights for piece in unit[0]]
    moved = sum(a.size * a.dtype.itemsize for a in list(outs) + list(args)) + sum(1536 * w * n for _, _, w, n in weights)
    n_in, n_w, n_out = len(args), len(weights), len(outs)

    def run(*refs):
        ins, refs = refs[:n_in], refs[n_in:]
        held, refs = refs[: len(pieces)], refs[len(pieces) :]
        out, refs = refs[:n_out], refs[n_out:]
        own, refs = refs[: len(scratch)], refs[len(scratch) :]
        ws = []
        for i, (unit, at, width, n) in enumerate(weights):
            rooms, sems = refs[2 * i], refs[2 * i + 1]
            mine, held = held[: len(unit[0])], held[len(unit[0]) :]
            ws.append(Weight(ins[0], mine, [rooms.at[j] for j in range(n)],
                             [sems.at[j] for j in range(n)], at, width, unit[1]))
            ws[-1].stack = rooms
        if grid == (1,):
            for w in ws:
                w.start()
        body(ws, *ins, *out, *own)

    rooms = []
    for _, _, width, n in weights:
        rooms += [pltpu.VMEM((n, 768, width), BF16), pltpu.SemaphoreType.DMA((n,))]
    return pl.pallas_call(
        run,
        out_shape=outs,
        grid=grid,
        in_specs=in_specs + [pl.BlockSpec(memory_space=pl.ANY)] * len(pieces),
        out_specs=out_specs,
        scratch_shapes=list(scratch) + rooms,
        input_output_aliases={} if into is None else {into: 0},
        name=name,
        compiler_params=pltpu.CompilerParams(vmem_limit_bytes=56 * 2**20),
        cost_estimate=pl.CostEstimate(flops=int(flops), bytes_accessed=int(moved), transcendentals=0),
    )(*args, *pieces)


def part(body, *fixed):
    return lambda *refs: body(*fixed, *refs)


def sds(shape, dtype):
    return jax.ShapeDtypeStruct(shape, dtype)


def sds(shape, dtype):
    return jax.ShapeDtypeStruct(shape, dtype)


ORDER_A = (8, 4, 2)
ORDER_B = (8, 2, 4)


def table_of(order):
    bits = (1, *order[::-1])
    return [sum(bit for i, bit in enumerate(bits) if p >> (3 - i) & 1) for p in range(16)]


def on_device(size, visual, query, seg_ids, shifts, valid_rows, attn_in, attn_out, mlp_in, mlp_out, gains, cot_visual, cot_query):
    by_steps = size == 16
    depth = gains.shape[1]
    rv, rq = 2 * visual.shape[0], 2 * query.shape[0]

    def swap(a):
        return lax.ppermute(a, "tensor", [(0, 1), (1, 0)])

    def across(a, bit):
        return lax.ppermute(a, "dp", [(i, i ^ bit) for i in range(size)])

    def gather(a, order=None):
        if not by_steps or order is None:
            return [lax.all_gather(a, "dp", axis=0, tiled=True)], None
        for bit in order:
            a = jnp.concatenate([a, across(a, bit)], axis=0)
        return [a, across(a, 1)], TABLE_A if order == ORDER_A else TABLE_B

    def after(a, *others):
        return lax.optimization_barrier((a, *others))[0]

    def scatter(dealt, order=None):
        if not by_steps or order is None:
            return lax.psum_scatter(dealt[0], "dp", scatter_dimension=0, tiled=True)
        kept, sent = dealt
        for bit in (1, *order[::-1]):
            got = across(sent, bit)
            total = kept.astype(F32) + got.astype(F32)
            half = total.shape[0] // 2
            kept, sent = total[:half].astype(BF16), total[half:].astype(BF16)
        return total

    def table_for(order):
        return None if order is None or not by_steps else TABLE_A if order == ORDER_A else TABLE_B

    def dealt_shapes(width, table):
        return [sds((768, width), BF16)] if table is None else [sds((HALF, width), BF16)] * 2

    t = lax.axis_index("tensor").astype(jnp.int32)
    me = lax.axis_index("dp").astype(jnp.int32)
    tables = jnp.array(table_of(ORDER_A) + table_of(ORDER_B), jnp.int32) ^ me
    scal = jnp.concatenate([t[None], shifts[0], valid_rows, tables])
    seg_r = seg_ids
    seg_c = seg_ids.reshape(-1, 1)

    a_in = attn_in.astype(BF16)
    gain_cols = jnp.pad(gains.T.astype(BF16), ((0, 0), (0, 122)))
    in0 = gather(jnp.concatenate([a_in[0].reshape(depth, WIDE), gain_cols], axis=1), ORDER_A)
    in1 = gather(a_in[1].reshape(depth, WIDE), ORDER_B)
    x_oth, q_oth = swap(visual), swap(query)
    aot = attn_out.astype(BF16).transpose(2, 0, 1).reshape(depth, 4 * HALF)
    bulk = [a_in[3][:, 0], a_in[2][:, 1], a_in[2][:, 2], a_in[2][:, 0], a_in[3][:, 1], a_in[3][:, 2], aot, swap(aot)]
    bulk_own = jnp.concatenate(bulk, axis=1)
    bulk = gather(bulk_own)
    m_in = mlp_in.astype(BF16)
    m_out = mlp_out.astype(BF16).transpose(0, 2, 1)
    mlps = gather(after(jnp.concatenate([m_in[0], m_out[0], m_in[1], m_out[1]], axis=1), bulk_own))
    cv_oth, cq_oth = swap(cot_visual), swap(cot_query)

    def outputs(a):
        return [(bulk, 2 * WIDE + a * HALF, HALF, 1), (bulk, 2 * WIDE + (4 + a) * HALF, HALF, 1)]

    def first(windowed, own, other, at, rows, unit, more):
        outs = [sds((rows, 768), F32), sds((rows, 768), BF16), sds((rows, WIDE), BF16), sds((rows, HALF), BF16)]
        if windowed:
            outs.append(sds((8, 768), F32))
        width = WIDE + 128 if windowed else WIDE
        return call(part(first_kernel, windowed, at), [scal, own, other, *more], [(unit, 0, width, 1)], outs, "first_%d" % at, 4e9)

    sv0, nv0, qkv0, o0, gr = first(True, visual, x_oth, 0, rv, in0, [])
    o0_oth = swap(o0)
    sq0, nq0, qkv1, o1 = first(False, query, q_oth, 1, rq, in1, [gr, seg_c, seg_r])
    o1_oth = swap(o1)

    def middle(index, s, o, o_oth, a, at, rows):
        return call(
            part(middle_kernel, index), [scal, s, o, o_oth, gr], [*outputs(a), (bulk, at, WIDE, 1)],
            [sds((rows, 768), F32), sds((rows, 768), BF16), sds((rows, WIDE), BF16)], "middle_%d" % a, 2e9)

    sv1, nv, pv = middle(2, sv0, o0, o0_oth, 0, 0, rv)
    sq1, nq, pq = middle(3, sq0, o1, o1_oth, 1, WIDE, rq)

    def cross(masked, q, kv, name):
        return call(part(cross_kernel, masked), [scal, q, kv], [], [sds((q.shape[0], HALF), BF16)], name, 2e9)[0]

    o3 = cross(False, pv, pq, "look")
    o3_oth = swap(o3)
    o2 = cross(True, pq, pv, "read")
    o2_oth = swap(o2)

    fb = 512
    steps = 1536 // fb

    def mlp(index, s1, o, o_oth, a, cot, cot_oth, at, rows, total):
        half = rows // 2
        dealt = pl.BlockSpec((768, 2 * fb), lambda i: (0, i))
        outs = [sds((rows, 768), F32), sds((half, 768), BF16), sds((half, 768), F32), sds((rows, 768), BF16), sds((1, 768), F32)]
        return call(
            part(mlp_kernel, index, steps), [scal, s1, o, o_oth, gr, cot, cot_oth],
            [*outputs(a), (mlps, at, fb, steps), (mlps, at + 1536, fb, steps)], outs + [sds((768, total), BF16)],
            "mlp_%d" % index, 10 * rows * 768 * 1536,
            scratch=[pltpu.VMEM((rows, 768), BF16), pltpu.VMEM((rows, 768), BF16), pltpu.VMEM((768, rows), BF16),
                     pltpu.VMEM((768, rows), BF16), pltpu.VMEM((rows, 768), F32), pltpu.VMEM((rows, 768), F32),
                     pltpu.VMEM((rows, 768), F32)],
            grid=(steps,), out_specs=[pl.BlockSpec(o.shape, lambda i: (0, 0)) for o in outs] + [dealt])

    sv2, part_v, keep_v, dnv4, dg4, dm0 = mlp(4, sv1, o3, o3_oth, 3, cot_visual, cv_oth, 0, rv, 3072)
    dnv4_oth = swap(dnv4)
    sq2, part_q, keep_q, dnq5, dg5, dm1 = mlp(5, sq1, o2, o2_oth, 2, cot_query, cq_oth, 3072, rq, 6144)
    dnq5_oth = swap(dnq5)
    s3v = scatter([dm0])
    out_visual = (keep_v + swap(part_v).astype(F32)).astype(BF16)
    out_query = (keep_q + swap(part_q).astype(F32)).astype(BF16)

    def cross_back(masked, index, cot, cot_oth, dn, dn_oth, s2, a, q, kv, name):
        return call(
            part(cross_back_kernel, masked, index), [scal, cot, cot_oth, dn, dn_oth, s2, gr, q, kv], outputs(a)[:1],
            [sds((q.shape[0], 768), F32), sds((q.shape[0], 768), BF16), sds((q.shape[0], HALF), BF16), sds((kv.shape[0], 768), BF16)],
            name, 6e9)

    gv2, dyv, dq3, dkv3 = cross_back(False, 4, cot_visual, cv_oth, dnv4, dnv4_oth, sv2, 3, pv, pq, "look_back")
    gq2, dyq, dq2, dkv2 = cross_back(True, 5, cot_query, cq_oth, dnq5, dnq5_oth, sq2, 2, pq, pv, "read_back")

    def dn_of(dq, dkv, at, s1, rows, name):
        return call(dn_kernel, [scal, dq, dkv, s1], [(bulk, at, WIDE, 1)], [sds((rows, 768), BF16), sds((1, 768), F32)], name, 1e9)

    dnv2, dg2 = dn_of(dq3, dkv2, 0, sv1, rv, "dn_2")
    dnv2_oth = swap(dnv2)
    dnq3, dg3 = dn_of(dq2, dkv3, WIDE, sq1, rq, "dn_3")
    dnq3_oth = swap(dnq3)

    def middle_weights(n, dq, dkv, dy, o, into, at, name):
        block = pl.BlockSpec((768, WIDE + HALF), lambda i: (0, at))
        return call(middle_weights_kernel, [scal, n, dq, dkv, dy, o, into], [], [sds(into.shape, BF16)],
                    name, 1.5e9, out_specs=[block], into=6)[0]

    dm1 = middle_weights(nv, dq3, dkv2, dyv, o3, dm1, 2, "weights_v")
    dm1 = middle_weights(nq, dq2, dkv3, dyq, o2, dm1, 3, "weights_q")
    rest = scatter([dm1])
    s3q, s2v, s2q = rest[:, 0:3072], rest[:, 3072:4608], rest[:, 4608:6144]

    def first_weights(n, d, dy, o, order, name, gains):
        table = table_for(order)
        width = WIDE + HALF + (128 if gains else 0)
        scratch = [] if table is None else [pltpu.VMEM((768, width), BF16)]
        if gains:
            scratch.append(pltpu.VMEM((128, 768), F32))
        return call(part(first_weights_kernel, table, len(gains)), [scal, n, d, dy, o, *gains], [], dealt_shapes(width, table),
                    name, 1.5e9, scratch=scratch)

    def first_back(windowed, index, later, grad, dn, dn_oth, s1, s0, unit, qkv, rows, more):
        half = rows // 2
        outs = [sds((half, 768), F32), sds((rows, 768), BF16), sds((rows, WIDE), BF16), sds((half, 768), BF16),
                sds((half, 768), F32), sds((1, 768), F32)]
        return call(part(first_back_kernel, windowed, index, later), [scal, grad, dn, dn_oth, s1, s0, gr, qkv, *more],
                    [outputs(index)[0], (unit, 0, WIDE, 1)], outs, "first_back_%d" % index, 7e9,
                    scratch=[pltpu.VMEM((rows, 768), F32)])

    gv1, dy0, d0, send_v, hold_v, dg0 = first_back(True, 0, 2, gv2, dnv2, dnv2_oth, sv1, sv0, in0, qkv0, rv, [])
    got_v = swap(send_v)
    s0 = scatter(first_weights(nv0, d0, dy0, o0, ORDER_A, "weights_0", []), ORDER_A)
    gq1, dy1, d1, send_q, hold_q, dg1 = first_back(False, 1, 3, gq2, dnq3, dnq3_oth, sq1, sq0, in1, qkv1, rq, [seg_c, seg_r])
    got_q = swap(send_q)
    s1 = scatter(first_weights(nq0, d1, dy1, o1, ORDER_B, "weights_1", [dg0, dg1, dg2, dg3, dg4, dg5]), ORDER_B)

    def last(index, grad, keep, got, own):
        return call(part(last_kernel, index), [scal, grad, keep, got, own, gr], [], [sds(own.shape, BF16)], "last_%d" % index, 1e7)[0]

    grad_visual = last(0, gv1, hold_v, got_v, visual)
    grad_query = last(1, gq1, hold_q, got_q, query)

    def slots(a):
        return a[:, 0:WIDE].reshape(depth, 3, HALF)

    v2, q2 = slots(s2v), slots(s2q)
    in2 = jnp.stack([q2[:, 0], v2[:, 1], v2[:, 2]], axis=1)
    in3 = jnp.stack([v2[:, 0], q2[:, 1], q2[:, 2]], axis=1)
    grad_in = jnp.stack([slots(s0), slots(s1), in2, in3]).astype(F32)
    grad_out = jnp.stack([a[:, WIDE : WIDE + HALF].T for a in (s0, s1, s2q, s2v)]).astype(F32)
    m3 = jnp.stack([s3v, s3q]).reshape(2, depth, steps, 2, fb)
    grad_up = m3[:, :, :, 0].reshape(2, depth, 1536).astype(F32)
    grad_down = m3[:, :, :, 1].reshape(2, depth, 1536).transpose(0, 2, 1).astype(F32)
    gsum = s1[:, WIDE + HALF :].astype(F32)
    gsum = gsum + swap(gsum)
    grad_gain = gsum[:, 0:6].T
    return out_visual, out_query, grad_visual, grad_query, grad_in, grad_out, grad_up, grad_down, grad_gain


def solution(mesh):
    rows = P(("dp", "tensor"), None)
    weights = (P(None, "dp", None, "tensor"), P(None, "tensor", "dp"), P(None, "dp", "tensor"), P(None, "tensor", "dp"), P(None, "dp"))
    in_specs = (rows, rows, P("dp", None), P("dp", None), P("dp")) + weights + (rows, rows)
    out_specs = (rows, rows, rows, rows) + weights
    body = part(on_device, mesh.shape["dp"])
    return jax.shard_map(body, mesh=mesh, in_specs=in_specs, out_specs=out_specs, check_vma=False)
```

```python
import jax
import jax.numpy as jnp
from jax import lax
from jax.experimental import pallas as pl
from jax.experimental.pallas import tpu as pltpu
from jax.sharding import PartitionSpec as P

PH = 36
PW = 12
SCALE = 0.125
EPSILON = 1e-05
MASKED = -1e30
ROOT_HALF = 0.7071067811865476
INV_ROOT_TAU = 0.3989422804014327
F32 = jnp.float32
BF16 = jnp.bfloat16
WIDE = 1152
HALF = 384


def nn(a, b):
    return lax.dot_general(a, b, (((1,), (0,)), ((), ())), preferred_element_type=F32)


def nt(a, b):
    return lax.dot_general(a, b, (((1,), (1,)), ((), ())), preferred_element_type=F32)


def tn(a, b):
    return lax.dot_general(a, b, (((0,), (0,)), ((), ())), preferred_element_type=F32)


def unit_of(s):
    centred = s - jnp.mean(s, axis=-1, keepdims=True)
    inverse = lax.rsqrt(jnp.mean(centred * centred, axis=-1, keepdims=True) + EPSILON)
    return centred * inverse, inverse


def norm_back(dn, u, inverse, gain):
    scaled = dn * gain
    centre = jnp.mean(scaled, axis=-1, keepdims=True)
    slope = jnp.mean(scaled * u, axis=-1, keepdims=True)
    return inverse * (scaled - centre - u * slope)


def assemble(dst, own, other, t):
    half = own.shape[0]
    dst[pl.ds(pl.multiple_of(t * half, 8), half), :] = own[...].astype(F32)
    dst[pl.ds(pl.multiple_of((1 - t) * half, 8), half), :] = other[...].astype(F32)


def own_rows(ref, which, half):
    return ref[pl.ds(pl.multiple_of(which * half, 8), half), :]


def head_mask(h, value):
    lane = lax.broadcasted_iota(jnp.int32, (1, 128), 1)
    return jnp.where((lane >= 64) == (h == 1), value, 0.0).astype(BF16)


def twelfth(v):
    return lax.shift_right_logical(v * 43691, 19)


def places(shape, axis, scal):
    a, b = scal[1], scal[2]
    i = lax.broadcasted_iota(jnp.int32, shape, axis)
    r = twelfth(i)
    c = i - 12 * r
    rolled = jnp.where(r < a, r - a + PH, r - a)
    region = jnp.where(r < a, 2, 0) + jnp.where(c < b, 1, 0)
    return i, r, twelfth(rolled) * 4 + region


def window_bias(n, scal, key_axis):
    shape_k = (1, n) if key_axis == 1 else (n, 1)
    shape_q = (n, 1) if key_axis == 1 else (1, n)
    ik, rk, pk = places(shape_k, key_axis, scal)
    iq, _, pq = places(shape_q, 1 - key_axis, scal)
    usable = jnp.where(rk < scal[3], pk, -1)
    allowed = (usable == pq) | (ik == iq)
    return jnp.where(allowed, 0.0, MASKED).astype(F32)


def read_bias(n, scal, key_axis):
    shape = (1, n) if key_axis == 1 else (n, 1)
    i = lax.broadcasted_iota(jnp.int32, shape, key_axis)
    return jnp.where(twelfth(i) < scal[3], 0.0, MASKED).astype(F32)


def attend(q_ref, q_at, kv_ref, k_at, v_at, bias, o_ref):
    lane = lax.broadcasted_iota(jnp.int32, (1, 128), 1)
    for pair in range(3):
        at = pair * 128
        q = q_ref[:, q_at + at : q_at + at + 128]
        k = kv_ref[:, k_at + at : k_at + at + 128]
        v = kv_ref[:, v_at + at : v_at + at + 128]
        outs = []
        for h in range(2):
            s = nt(q * head_mask(h, SCALE), k)
            if bias is not None:
                s = s + bias
            e = jnp.exp(s - jnp.max(s, axis=1, keepdims=True))
            total = jnp.sum(e, axis=1, keepdims=True)
            outs.append(nn(e.astype(BF16), v) * (1.0 / total))
        o_ref[:, at : at + 128] = jnp.where(lane < 64, outs[0], outs[1]).astype(BF16)


def attend_back(q_ref, q_at, kv_ref, k_at, v_at, bias, do, dq_ref, dq_at, dk_ref, dk_at, dv_at):
    for pair in range(3):
        at = pair * 128
        q = q_ref[:, q_at + at : q_at + at + 128]
        k = kv_ref[:, k_at + at : k_at + at + 128]
        v = kv_ref[:, v_at + at : v_at + at + 128]
        dop = do[:, at : at + 128]
        dq, dk, dv = 0.0, 0.0, 0.0
        for h in range(2):
            keep = head_mask(h, 1.0)
            qm = q * head_mask(h, SCALE)
            dom = dop * keep
            s = nt(k, qm)
            if bias is not None:
                s = s + bias
            e = jnp.exp(s - jnp.max(s, axis=0, keepdims=True))
            p = e * (1.0 / jnp.sum(e, axis=0, keepdims=True))
            dp = nt(v, dom)
            delta = jnp.sum(p * dp, axis=0, keepdims=True)
            ds = (p * (dp - delta)).astype(BF16)
            dv = dv + nn(p.astype(BF16), dom)
            dk = dk + nn(ds, qm)
            dq = dq + tn(ds, k * keep)
        dq_ref[:, dq_at + at : dq_at + at + 128] = (dq * SCALE).astype(BF16)
        dk_ref[:, dk_at + at : dk_at + at + 128] = dk.astype(BF16)
        dk_ref[:, dv_at + at : dv_at + at + 128] = dv.astype(BF16)


def first_kernel(windowed, index, ws, *refs):
    if windowed:
        scal, own, other, s_ref, n_ref, qkv, o_ref, p_ref, gr_ref = refs
    else:
        scal, own, other, gr, seg_c, seg_r, s_ref, n_ref, qkv, o_ref, p_ref = refs
    assemble(s_ref, own, other, scal[0])
    u, _ = unit_of(s_ref[...])
    w = ws[0]()
    if windowed:
        gr = w[:, WIDE:].astype(F32).T[0:8, :]
        gr_ref[...] = gr
    n = (u * gr[index : index + 1, :]).astype(BF16)
    n_ref[...] = n
    qkv[...] = nn(n, w[:, 0:WIDE]).astype(BF16)
    if windowed:
        bias = window_bias(qkv.shape[0], scal, 1)
    else:
        bias = jnp.where(seg_c[...] == seg_r[...], 0.0, MASKED).astype(F32)
    attend(qkv, 0, qkv, HALF, 2 * HALF, bias, o_ref)
    p_ref[...] = nt(o_ref[...], ws[1]()[...]).astype(BF16)


def middle_kernel(index, ws, scal, s, p_own, p_oth, gr, s1, n_ref, proj):
    stream = s[...] + (p_own[...].astype(F32) + p_oth[...].astype(F32))
    s1[...] = stream
    u, _ = unit_of(stream)
    n = (u * gr[index : index + 1, :]).astype(BF16)
    n_ref[...] = n
    proj[...] = nn(n, ws[0]()[...]).astype(BF16)


def cross_kernel(masked, ws, scal, q_ref, kv_ref, o_ref, p_ref):
    bias = read_bias(kv_ref.shape[0], scal, 1) if masked else None
    attend(q_ref, 0, kv_ref, HALF, 2 * HALF, bias, o_ref)
    p_ref[...] = nt(o_ref[...], ws[0]()[...]).astype(BF16)


def mlp_kernel(index, steps, ws, scal, s1, p_own, p_oth, gr, cot_own, cot_oth,
               *refs):
    s2, send, keep, dn_ref, dg_ref, dm_ref, n_s, dy_s, nt_s, dyt_s, part_s, dn_s, cot_s = refs[-13:]
    step = pl.program_id(0)
    half = cot_own.shape[0]
    t = scal[0]

    @pl.when(step == 0)
    def _():
        for w in ws:
            w.start()
        stream = s1[...] + (p_own[...].astype(F32) + p_oth[...].astype(F32))
        s2[...] = stream
        u, _ = unit_of(stream)
        n = (u * gr[index : index + 1, :]).astype(BF16)
        n_s[...] = n
        nt_s[...] = n.T
        assemble(cot_s, cot_own, cot_oth, t)
        dy = cot_s[...].astype(BF16)
        dy_s[...] = dy
        dyt_s[...] = dy.T

    for i in range(steps):

        @pl.when(step == i)
        def _(i=i):
            ws[0](i)
            ws[1](i)

    fb = ws[0].width
    w_in = ws[0].stack[step]
    w_out = ws[1].stack[step]
    hidden = nn(n_s[...], w_in)
    phi = 0.5 * (1.0 + lax.erf(hidden * ROOT_HALF))
    act = (hidden * phi).astype(BF16)
    slope = phi + hidden * jnp.exp(-0.5 * hidden * hidden) * INV_ROOT_TAU
    dh = (nn(dy_s[...], w_out) * slope).astype(BF16)
    part = nt(act, w_out)
    dn = nt(dh, w_in)

    @pl.when(step == 0)
    def _():
        part_s[...] = part
        dn_s[...] = dn

    @pl.when(step > 0)
    def _():
        part_s[...] += part
        dn_s[...] += dn

    dm_ref[:, 0:fb] = nn(nt_s[...], dh).astype(BF16)
    dm_ref[:, fb : 2 * fb] = nn(dyt_s[...], act).astype(BF16)

    @pl.when(step == steps - 1)
    def _():
        send[...] = own_rows(part_s, 1 - t, half).astype(BF16)
        keep[...] = own_rows(part_s, t, half) + own_rows(s2, t, half)
        dn_all = dn_s[...]
        dn_ref[...] = dn_all.astype(BF16)
        u, _ = unit_of(s2[...])
        dg_ref[...] = jnp.sum(dn_all * u, axis=0, keepdims=True)


def cross_back_kernel(masked, index, ws, scal, cot_own, cot_oth, dn_own, dn_oth, s2, gr, q_ref, kv_ref,
                      g_ref, dy_ref, dq_ref, dkv_ref):
    assemble(g_ref, cot_own, cot_oth, scal[0])
    u, inverse = unit_of(s2[...])
    dn = dn_own[...].astype(F32) + dn_oth[...].astype(F32)
    grad = g_ref[...] + norm_back(dn, u, inverse, gr[index : index + 1, :])
    g_ref[...] = grad
    dy = grad.astype(BF16)
    dy_ref[...] = dy
    do = nn(dy, ws[0]()[...]).astype(BF16)
    bias = read_bias(kv_ref.shape[0], scal, 0) if masked else None
    attend_back(q_ref, 0, kv_ref, HALF, 2 * HALF, bias, do, dq_ref, 0, dkv_ref, 0, HALF)


def dn_kernel(ws, scal, dq, dkv, s1, dn_ref, dg_ref):
    w = ws[0]()
    dn = nt(dq[...], w[:, 0:HALF]) + nt(dkv[...], w[:, HALF:WIDE])
    dn_ref[...] = dn.astype(BF16)
    u, _ = unit_of(s1[...])
    dg_ref[...] = jnp.sum(dn * u, axis=0, keepdims=True)


def fill_weights(out, grads, dy, o):
    at = 0
    for n, grad in zip(grads[0::2], grads[1::2]):
        width = grad.shape[1]
        out[:, at : at + width] = tn(n[...], grad[...]).astype(BF16)
        at += width
    out[:, at : at + HALF] = tn(dy[...], o[...]).astype(BF16)


def weights_kernel(table, gains, parts, held, ws, scal, dy, o, *refs):
    grads, rows = refs[:parts], refs[parts : parts + gains]
    refs = refs[parts + gains + held :]
    if table is None:
        out = refs[0]
    else:
        *dealt, out = refs[:3]
    fill_weights(out, grads, dy, o)
    if gains:
        stack = refs[-1]
        stack[...] = jnp.zeros_like(stack)
        for i, row in enumerate(rows):
            stack[i : i + 1, :] = row[...]
        out[:, WIDE + HALF :] = stack[...].T.astype(BF16)
    if table is not None:
        deal(out, dealt, scal, table)


def first_back_kernel(windowed, index, later, ws, scal, *refs):
    if windowed:
        grad, dn_own, dn_oth, s1, s0, gr, qkv, g_ref, dy_ref, dqkv, send, keep, dg_ref, g_s = refs
    else:
        (grad, dn_own, dn_oth, s1, s0, gr, qkv, seg_c, seg_r,
         g_ref, dy_ref, dqkv, send, keep, dg_ref, g_s) = refs
    t = scal[0]
    half = g_ref.shape[0]
    u, inverse = unit_of(s1[...])
    dn = dn_own[...].astype(F32) + dn_oth[...].astype(F32)
    g = grad[...] + norm_back(dn, u, inverse, gr[later : later + 1, :])
    g_s[...] = g
    g_ref[...] = own_rows(g_s, t, half)
    dy = g.astype(BF16)
    dy_ref[...] = dy
    do = nn(dy, ws[0]()[...]).astype(BF16)
    if windowed:
        bias = window_bias(qkv.shape[0], scal, 0)
    else:
        bias = jnp.where(seg_c[...] == seg_r[...], 0.0, MASKED).astype(F32)
    attend_back(qkv, 0, qkv, HALF, 2 * HALF, bias, do, dqkv, 0, dqkv, HALF, 2 * HALF)
    dn0 = nt(dqkv[...], ws[1]()[...])
    g_s[...] = dn0
    send[...] = own_rows(g_s, 1 - t, half).astype(BF16)
    keep[...] = own_rows(g_s, t, half)
    u, _ = unit_of(s0[...])
    dg_ref[...] = jnp.sum(dn0 * u, axis=0, keepdims=True)


def last_kernel(index, ws, scal, grad, keep, got, own, gr, out):
    u, inverse = unit_of(own[...].astype(F32))
    dn = keep[...] + got[...].astype(F32)
    out[...] = (grad[...] + norm_back(dn, u, inverse, gr[index : index + 1, :])).astype(BF16)


class Weight:
    def __init__(self, scal, pieces, rooms, sems, at, width, table):
        self.scal, self.pieces, self.rooms, self.sems = scal, pieces, rooms, sems
        self.at, self.width, self.table, self.waited = at, width, table, set()

    def start(self):
        for i, room in enumerate(self.rooms):
            if self.table is None:
                source = self.pieces[0].at[:, pl.ds(self.at + i * self.width, self.width)]
                pltpu.make_async_copy(source, room, self.sems[i]).start()
                continue
            for p in range(16):
                to = pl.multiple_of(self.scal[self.table + p] * 48, 16)
                pltpu.make_async_copy(
                    self.pieces[p // 8].at[pl.ds(p % 8 * 48, 48), pl.ds(self.at + i * self.width, self.width)],
                    room.at[pl.ds(to, 48), :],
                    self.sems[i],
                ).start()

    def __call__(self, i=0):
        if i not in self.waited:
            pltpu.make_async_copy(self.rooms[i], self.rooms[i], self.sems[i]).wait()
            self.waited.add(i)
        return self.rooms[i]


def deal(whole, outs, scal, table):
    for p in range(16):
        block = whole[pl.ds(pl.multiple_of(scal[table + p] * 48, 16), 48), :]
        outs[p // 8][p % 8 * 48 : p % 8 * 48 + 48, :] = block


TABLE = 4


def call(body, args, weights, outs, name, flops, scratch=(), grid=(1,), out_specs=None, into=None, gates=()):
    def whole(shape):
        return pl.BlockSpec(shape, lambda *_: (0,) * len(shape))

    in_specs = [pl.BlockSpec(memory_space=pltpu.SMEM)] + [whole(a.shape) for a in args[1:]]
    for i in into or {}:
        in_specs[i] = pl.BlockSpec(memory_space=pl.ANY)
    out_specs = out_specs or [whole(o.shape) for o in outs]
    pieces = [piece for unit, _, _, _ in weights for piece in unit[0]]
    moved = sum(a.size * a.dtype.itemsize for a in list(outs) + list(args)) + sum(1536 * w * n for _, _, w, n in weights)
    n_in, n_w, n_out = len(args), len(weights), len(outs)

    def run(*refs):
        ins, refs = refs[:n_in], refs[n_in:]
        held, refs = refs[: len(pieces)], refs[len(pieces) + len(gates) :]
        out, refs = refs[:n_out], refs[n_out:]
        own, refs = refs[: len(scratch)], refs[len(scratch) :]
        ws = []
        for i, (unit, at, width, n) in enumerate(weights):
            rooms, sems = refs[2 * i], refs[2 * i + 1]
            mine, held = held[: len(unit[0])], held[len(unit[0]) :]
            ws.append(Weight(ins[0], mine, [rooms.at[j] for j in range(n)],
                             [sems.at[j] for j in range(n)], at, width, unit[1]))
            ws[-1].stack = rooms
        if grid == (1,):
            for w in ws:
                w.start()
        body(ws, *ins, *out, *own)

    rooms = []
    for _, _, width, n in weights:
        rooms += [pltpu.VMEM((n, 768, width), BF16), pltpu.SemaphoreType.DMA((n,))]
    return pl.pallas_call(
        run,
        out_shape=outs,
        grid=grid,
        in_specs=in_specs + [pl.BlockSpec(memory_space=pl.ANY)] * (len(pieces) + len(gates)),
        out_specs=out_specs,
        scratch_shapes=list(scratch) + rooms,
        input_output_aliases=into or {},
        name=name,
        compiler_params=pltpu.CompilerParams(vmem_limit_bytes=56 * 2**20),
        cost_estimate=pl.CostEstimate(flops=int(10 * flops), bytes_accessed=int(10 * moved), transcendentals=0),
    )(*args, *pieces, *gates)


def part(body, *fixed):
    return lambda *refs: body(*fixed, *refs)


def sds(shape, dtype):
    return jax.ShapeDtypeStruct(shape, dtype)


def sds(shape, dtype):
    return jax.ShapeDtypeStruct(shape, dtype)


PLACES = [(p >> 3) | (p >> 2 & 1) << 1 | (p & 3) << 2 for p in range(16)]


def on_device(size, visual, query, seg_ids, shifts, valid_rows, attn_in, attn_out, mlp_in, mlp_out, gains, cot_visual, cot_query):
    by_steps = size == 16
    depth = gains.shape[1]
    rv, rq = 2 * visual.shape[0], 2 * query.shape[0]

    def swap(a):
        return lax.ppermute(a, "tensor", [(0, 1), (1, 0)])

    def across(a, bit):
        return lax.ppermute(a, "dp", [(i, i ^ bit) for i in range(size)])

    def gather(a):
        return [lax.all_gather(a, "dp", axis=0, tiled=True)], None

    def after(a, *others):
        return lax.optimization_barrier((a, *others))[0]

    def scatter(a):
        return lax.psum_scatter(a, "dp", scatter_dimension=0, tiled=True)

    table = TABLE if by_steps else None

    class Gather:
        def __init__(self, a, *others):
            self.cur = after(a, *others) if others else a
            if by_steps:
                self.cur = jnp.concatenate([self.cur] + [across(self.cur, 4 * k) for k in (1, 2, 3)], axis=0)

        def along_y(self, *others):
            if by_steps:
                cur = after(self.cur, *others) if others else self.cur
                self.cur = jnp.concatenate([cur, across(cur, 2)], axis=0)

        def finish(self, *others):
            if not by_steps:
                return gather(self.cur)
            cur = after(self.cur, *others) if others else self.cur
            return [cur, across(cur, 1)], table

    class Scatter:
        def __init__(self, dealt):
            self.kept, self.sent, self.step = dealt[0], [dealt[-1]], 0
            self.got = None
            if not by_steps:
                self.kept = self.total = scatter(dealt[0])

        def send(self, *others):
            if not by_steps:
                return
            sent = [after(a, *others) if others else a for a in self.sent]
            bits = ((1,), (2,), (4, 8, 12))[self.step]
            self.got = [across(a, bit) for a, bit in zip(sent, bits)]
            self.step += 1

        def add(self):
            if not by_steps:
                return self.total
            total = sum([a.astype(F32) for a in self.got], self.kept.astype(F32))
            self.total, low = total, total.astype(BF16)
            if self.step == 1:
                self.kept, self.sent = low[:192], [low[192:]]
            else:
                self.kept, self.sent = low[:48], [low[48:96], low[96:144], low[144:]]
            return self.kept

    def dealt_shapes(width, table):
        return [sds((768, width), BF16)] if table is None else [sds((HALF, width), BF16)] * 2

    t = lax.axis_index("tensor").astype(jnp.int32)
    me = lax.axis_index("dp").astype(jnp.int32)
    scal = jnp.concatenate([t[None], shifts[0], valid_rows, jnp.array(PLACES, jnp.int32) ^ me])
    seg_r = seg_ids
    seg_c = seg_ids.reshape(-1, 1)

    a_in = attn_in.astype(BF16)
    gain_cols = jnp.pad(gains.T.astype(BF16), ((0, 0), (0, 122)))
    m_in = mlp_in.astype(BF16)
    m_out = mlp_out.astype(BF16).transpose(0, 2, 1)
    aot = attn_out.astype(BF16).transpose(0, 2, 1)
    g0 = Gather(jnp.concatenate([a_in[0].reshape(depth, WIDE), gain_cols, aot[0]], axis=1))
    g1 = Gather(jnp.concatenate([a_in[1].reshape(depth, WIDE), aot[1]], axis=1))
    bulk = [a_in[3][:, 0], a_in[2][:, 1], a_in[2][:, 2], a_in[2][:, 0], a_in[3][:, 1], a_in[3][:, 2], aot[2], aot[3]]
    bulk_own = jnp.concatenate(bulk, axis=1)
    bulk = gather(bulk_own)
    mlps = gather(after(jnp.concatenate([m_in[0], m_out[0], m_in[1], m_out[1]], axis=1), bulk_own))
    x_oth, q_oth = swap(visual), swap(query)
    cv_oth, cq_oth = swap(after(cot_visual, x_oth, q_oth)), swap(after(cot_query, x_oth, q_oth))
    g0.along_y()
    in0 = g0.finish()
    g1.along_y()
    in1 = g1.finish()

    def output(a):
        return ((in0, WIDE + 128), (in1, WIDE), (bulk, 2 * WIDE), (bulk, 2 * WIDE + HALF))[a] + (HALF, 1)

    def first(windowed, own, other, at, rows, unit, more, gates):
        outs = [sds((rows, 768), F32), sds((rows, 768), BF16), sds((rows, WIDE), BF16), sds((rows, HALF), BF16), sds((rows, 768), BF16)]
        if windowed:
            outs.append(sds((8, 768), F32))
        width = WIDE + 128 if windowed else WIDE
        return call(part(first_kernel, windowed, at), [scal, own, other, *more], [(unit, 0, width, 1), output(at)], outs, "first_%d" % at, 4e9, gates=gates)

    sv0, nv0, qkv0, o0, p0, gr = first(True, visual, x_oth, 0, rv, in0, [], [cv_oth])
    p0_oth = swap(p0)
    sq0, nq0, qkv1, o1, p1 = first(False, query, q_oth, 1, rq, in1, [gr, seg_c, seg_r], [cq_oth])
    p1_oth = swap(p1)

    def middle(index, s, p, p_oth, at, rows):
        return call(
            part(middle_kernel, index), [scal, s, p, p_oth, gr], [(bulk, at, WIDE, 1)],
            [sds((rows, 768), F32), sds((rows, 768), BF16), sds((rows, WIDE), BF16)], "middle_%d" % index, 2e9)

    sv1, nv, pv = middle(2, sv0, p0, p0_oth, 0, rv)
    sq1, nq, pq = middle(3, sq0, p1, p1_oth, WIDE, rq)

    def cross(masked, q, kv, a, name, gates):
        outs = [sds((q.shape[0], HALF), BF16), sds((q.shape[0], 768), BF16)]
        return call(part(cross_kernel, masked), [scal, q, kv], [output(a)], outs, name, 2e9, gates=gates)

    o3, p3 = cross(False, pv, pq, 3, "look", [])
    p3_oth = swap(p3)
    o2, p2 = cross(True, pq, pv, 2, "read", [o3])
    p2_oth = swap(p2)

    fb = 512
    steps = 1536 // fb

    def mlp(index, s1, p, p_oth, cot, cot_oth, at, rows, into, gates=()):
        half = rows // 2
        first = 0 if into is None else steps
        dealt = pl.BlockSpec((768, 2 * fb), lambda i: (0, first + i))
        args = [scal, s1, p, p_oth, gr, cot, cot_oth] + ([] if into is None else [into])
        outs = [sds((rows, 768), F32), sds((half, 768), BF16), sds((half, 768), F32), sds((rows, 768), BF16), sds((1, 768), F32)]
        return call(
            part(mlp_kernel, index, steps), args,
            [(mlps, at, fb, steps), (mlps, at + 1536, fb, steps)], outs + [sds((768, 6144), BF16)],
            "mlp_%d" % index, 10 * rows * 768 * 1536,
            scratch=[pltpu.VMEM((rows, 768), BF16), pltpu.VMEM((rows, 768), BF16), pltpu.VMEM((768, rows), BF16),
                     pltpu.VMEM((768, rows), BF16), pltpu.VMEM((rows, 768), F32), pltpu.VMEM((rows, 768), F32),
                     pltpu.VMEM((rows, 768), F32)],
            grid=(steps,), out_specs=[pl.BlockSpec(o.shape, lambda i: (0, 0)) for o in outs] + [dealt], gates=gates, into={} if into is None else {7: 5})

    sv2, part_v, keep_v, dnv4, dg4, dm = mlp(4, sv1, p3, p3_oth, cot_visual, cv_oth, 0, rv, None, [p2_oth])
    dnv4_oth = swap(dnv4)
    sq2, part_q, keep_q, dnq5, dg5, dm = mlp(5, sq1, p2, p2_oth, cot_query, cq_oth, 3072, rq, dm, [dnv4])
    dnq5_oth = swap(dnq5)
    s3 = scatter(dm)

    def cross_back(masked, index, cot, cot_oth, dn, dn_oth, s2, a, q, kv, name, gates=()):
        return call(
            part(cross_back_kernel, masked, index), [scal, cot, cot_oth, dn, dn_oth, s2, gr, q, kv], [output(a)],
            [sds((q.shape[0], 768), F32), sds((q.shape[0], 768), BF16), sds((q.shape[0], HALF), BF16), sds((kv.shape[0], 768), BF16)],
            name, 6e9, gates=gates)

    gv2, dyv, dq3, dkv3 = cross_back(False, 4, cot_visual, cv_oth, dnv4, dnv4_oth, sv2, 3, pv, pq, "look_back", [sq2])
    def dn_of(dq, dkv, at, s1, rows, name, gates):
        return call(dn_kernel, [scal, dq, dkv, s1], [(bulk, at, WIDE, 1)], [sds((rows, 768), BF16), sds((1, 768), F32)], name, 1e9, gates=gates)

    def weights(grads, dy, o, name, gains=(), gates=(), at=0, blocks=1, into=()):
        width = WIDE + HALF + (128 if gains else 0)
        scratch = [] if table is None else [pltpu.VMEM((768, width), BF16)]
        if gains:
            scratch.append(pltpu.VMEM((128, 768), F32))
        args = [scal, dy, o, *grads, *gains, *into]
        shapes = dealt_shapes(width * blocks, table)
        return call(part(weights_kernel, table, len(gains), len(grads), len(into)), args, [], shapes, name, 1.5e9,
                    scratch=scratch, gates=gates, out_specs=[pl.BlockSpec((a.shape[0], width), lambda i: (0, at)) for a in shapes],
                    into={len(args) - len(into) + i: i for i in range(len(into))})

    hl = Scatter(weights([nv, dq3, nq, dkv3], dyv, o3, "weights_look"))
    gates = [hl.kept]
    hl.send()
    gq2, dyq, dq2, dkv2 = cross_back(True, 5, cot_query, cq_oth, dnq5, dnq5_oth, sq2, 2, pq, pv, "read_back", gates)

    dnv2, dg2 = dn_of(dq3, dkv2, 0, sv1, rv, "dn_2", [hl.add()])
    dnv2_oth = swap(dnv2)
    dnq3, dg3 = dn_of(dq2, dkv3, WIDE, sq1, rq, "dn_3", [dnv2])
    dnq3_oth = swap(dnq3)

    hl.send()
    hr = Scatter(weights([nq, dq2, nv, dkv2], dyq, o2, "weights_read", gates=[dnv2, dnq3]))
    gates = [hr.kept]
    hr.send()

    def first_back(windowed, index, later, grad, dn, dn_oth, s1, s0, unit, qkv, rows, more, gates):
        half = rows // 2
        outs = [sds((half, 768), F32), sds((rows, 768), BF16), sds((rows, WIDE), BF16), sds((half, 768), BF16),
                sds((half, 768), F32), sds((1, 768), F32)]
        return call(part(first_back_kernel, windowed, index, later), [scal, grad, dn, dn_oth, s1, s0, gr, qkv, *more],
                    [output(index), (unit, 0, WIDE, 1)], outs, "first_back_%d" % index, 7e9,
                    scratch=[pltpu.VMEM((rows, 768), F32)], gates=gates)

    gv1, dy0, d0, send_v, hold_v, dg0 = first_back(True, 0, 2, gv2, dnv2, dnv2_oth, sv1, sv0, in0, qkv0, rv, [], gates)
    got_v = swap(send_v)
    h0 = Scatter(weights([nv0, d0], dy0, o0, "weights_0", gates=[hl.add(), hr.add()]))
    hl.send()
    hr.send()
    h0.send()
    gates = [h0.kept]
    gq1, dy1, d1, send_q, hold_q, dg1 = first_back(False, 1, 3, gq2, dnq3, dnq3_oth, sq1, sq0, in1, qkv1, rq, [seg_c, seg_r], gates)
    h1 = Scatter(weights([nq0, d1], dy1, o1, "weights_1", [dg0, dg1, dg2, dg3, dg4, dg5], [hl.add(), h0.add()]))
    h0.send()
    ready = h1.kept
    h1.send()
    hr.add()
    hr.send(ready)
    got_q = swap(after(send_q, ready))
    gates = [h1.add()]
    h1.send()
    h0.add()
    h0.send(*gates)
    hr.add()
    h1.add()
    h0.add()
    m3 = s3.reshape(depth, 2, steps, 2, fb)
    grad_up = m3[:, :, :, 0].transpose(1, 0, 2, 3).reshape(2, depth, 1536).astype(F32)
    grad_down = m3[:, :, :, 1].reshape(depth, 2, 1536).transpose(1, 2, 0).astype(F32)
    h1.send()
    h1.add()
    look, read, s0, s1 = hl.total, hr.total, h0.total, h1.total
    out_visual = (keep_v + swap(after(part_v, *gates)).astype(F32)).astype(BF16)
    out_query = (keep_q + swap(after(part_q, *gates)).astype(F32)).astype(BF16)

    def last(index, grad, keep, got, own, gates):
        return call(part(last_kernel, index), [scal, grad, keep, got, own, gr], [], [sds(own.shape, BF16)], "last_%d" % index, 1e7, gates=gates)[0]

    grad_visual = last(0, gv1, hold_v, got_v, visual, gates)
    grad_query = last(1, gq1, hold_q, got_q, query, gates)

    def slots(a):
        return a[:, 0:WIDE].reshape(depth, 3, HALF)

    grad_in = jnp.stack([slots(s0), slots(s1), slots(read), slots(look)]).astype(F32)
    grad_out = jnp.stack([a[:, WIDE : WIDE + HALF].T for a in (s0, s1, read, look)]).astype(F32)
    gsum = s1[:, WIDE + HALF :].astype(F32)
    gsum = gsum + swap(gsum)
    grad_gain = gsum[:, 0:6].T
    return out_visual, out_query, grad_visual, grad_query, grad_in, grad_out, grad_up, grad_down, grad_gain


def solution(mesh):
    rows = P(("dp", "tensor"), None)
    weights = (P(None, "dp", None, "tensor"), P(None, "tensor", "dp"), P(None, "dp", "tensor"), P(None, "tensor", "dp"), P(None, "dp"))
    in_specs = (rows, rows, P("dp", None), P("dp", None), P("dp")) + weights + (rows, rows)
    out_specs = (rows, rows, rows, rows) + weights
    body = part(on_device, mesh.shape["dp"])
    return jax.shard_map(body, mesh=mesh, in_specs=in_specs, out_specs=out_specs, check_vma=False)
```

```python
import jax
import jax.numpy as jnp
from jax import lax
from jax.experimental import pallas as pl
from jax.experimental.pallas import tpu as pltpu
from jax.sharding import PartitionSpec as P

PH = 36
PW = 12
SCALE = 0.125
EPSILON = 1e-05
MASKED = -1e30
ROOT_HALF = 0.7071067811865476
INV_ROOT_TAU = 0.3989422804014327
F32 = jnp.float32
BF16 = jnp.bfloat16
WIDE = 1152
HALF = 384


def nn(a, b):
    return lax.dot_general(a, b, (((1,), (0,)), ((), ())), preferred_element_type=F32)


def nt(a, b):
    return lax.dot_general(a, b, (((1,), (1,)), ((), ())), preferred_element_type=F32)


def tn(a, b):
    return lax.dot_general(a, b, (((0,), (0,)), ((), ())), preferred_element_type=F32)


def unit_of(s):
    centred = s - jnp.mean(s, axis=-1, keepdims=True)
    inverse = lax.rsqrt(jnp.mean(centred * centred, axis=-1, keepdims=True) + EPSILON)
    return centred * inverse, inverse


def norm_back(dn, u, inverse, gain):
    scaled = dn * gain
    centre = jnp.mean(scaled, axis=-1, keepdims=True)
    slope = jnp.mean(scaled * u, axis=-1, keepdims=True)
    return inverse * (scaled - centre - u * slope)


def assemble(dst, own, other, t):
    half = own.shape[0]
    dst[pl.ds(pl.multiple_of(t * half, 8), half), :] = own[...].astype(F32)
    dst[pl.ds(pl.multiple_of((1 - t) * half, 8), half), :] = other[...].astype(F32)


def own_rows(ref, which, half):
    return ref[pl.ds(pl.multiple_of(which * half, 8), half), :]


def head_mask(h, value):
    lane = lax.broadcasted_iota(jnp.int32, (1, 128), 1)
    return jnp.where((lane >= 64) == (h == 1), value, 0.0).astype(BF16)


def twelfth(v):
    return lax.shift_right_logical(v * 43691, 19)


def places(shape, axis, scal):
    a, b = scal[1], scal[2]
    i = lax.broadcasted_iota(jnp.int32, shape, axis)
    r = twelfth(i)
    c = i - 12 * r
    rolled = jnp.where(r < a, r - a + PH, r - a)
    region = jnp.where(r < a, 2, 0) + jnp.where(c < b, 1, 0)
    return i, r, twelfth(rolled) * 4 + region


def window_bias(n, scal, key_axis):
    shape_k = (1, n) if key_axis == 1 else (n, 1)
    shape_q = (n, 1) if key_axis == 1 else (1, n)
    ik, rk, pk = places(shape_k, key_axis, scal)
    iq, _, pq = places(shape_q, 1 - key_axis, scal)
    usable = jnp.where(rk < scal[3], pk, -1)
    allowed = (usable == pq) | (ik == iq)
    return jnp.where(allowed, 0.0, MASKED).astype(F32)


def read_bias(n, scal, key_axis):
    shape = (1, n) if key_axis == 1 else (n, 1)
    i = lax.broadcasted_iota(jnp.int32, shape, key_axis)
    return jnp.where(twelfth(i) < scal[3], 0.0, MASKED).astype(F32)


def attend(q_ref, q_at, kv_ref, k_at, v_at, bias, o_ref, lse_ref):
    lane = lax.broadcasted_iota(jnp.int32, (1, 128), 1)
    logs = jnp.zeros((q_ref.shape[0], 128), F32)
    for pair in range(3):
        at = pair * 128
        q = q_ref[:, q_at + at : q_at + at + 128]
        k = kv_ref[:, k_at + at : k_at + at + 128]
        v = kv_ref[:, v_at + at : v_at + at + 128]
        outs = []
        for h in range(2):
            s = nt(q * head_mask(h, SCALE), k)
            if bias is not None:
                s = s + bias
            top = jnp.max(s, axis=1, keepdims=True)
            e = jnp.exp(s - top)
            total = jnp.sum(e, axis=1, keepdims=True)
            outs.append(nn(e.astype(BF16), v) * (1.0 / total))
            logs = jnp.where(lane == 2 * pair + h, top + jnp.log(total), logs)
        o_ref[:, at : at + 128] = jnp.where(lane < 64, outs[0], outs[1]).astype(BF16)
    lse_ref[...] = logs.T[0:8, :]


def attend_back(q_ref, q_at, kv_ref, k_at, v_at, bias, do, o_ref, lse_ref, dq_ref, dq_at, dk_ref, dk_at, dv_at):
    product = do.astype(F32) * o_ref[...].astype(F32)
    high = product.astype(BF16)
    low = (product - high.astype(F32)).astype(BF16)
    head = lax.broadcasted_iota(jnp.int32, (8, HALF), 0)
    column = lax.broadcasted_iota(jnp.int32, (8, HALF), 1)
    pick = jnp.where((column >= 64 * head) & (column < 64 * head + 64), 1.0, 0.0).astype(BF16)
    deltas = nt(pick, high) + nt(pick, low)
    for pair in range(3):
        at = pair * 128
        q = q_ref[:, q_at + at : q_at + at + 128]
        k = kv_ref[:, k_at + at : k_at + at + 128]
        v = kv_ref[:, v_at + at : v_at + at + 128]
        dop = do[:, at : at + 128]
        dq, dk, dv = 0.0, 0.0, 0.0
        for h in range(2):
            row = 2 * pair + h
            keep = head_mask(h, 1.0)
            qm = q * head_mask(h, SCALE)
            dom = dop * keep
            s = nt(k, qm)
            if bias is not None:
                s = s + bias
            p = jnp.exp(s - lse_ref[row : row + 1, :])
            ds = (p * (nt(v, dom) - deltas[row : row + 1, :])).astype(BF16)
            dv = dv + nn(p.astype(BF16), dom)
            dk = dk + nn(ds, qm)
            dq = dq + tn(ds, k * keep)
        dq_ref[:, dq_at + at : dq_at + at + 128] = (dq * SCALE).astype(BF16)
        dk_ref[:, dk_at + at : dk_at + at + 128] = dk.astype(BF16)
        dk_ref[:, dv_at + at : dv_at + at + 128] = dv.astype(BF16)


def first_kernel(windowed, index, ws, *refs):
    if windowed:
        scal, own, other, s_ref, n_ref, qkv, o_ref, p_ref, lse_ref, gr_ref = refs
    else:
        scal, own, other, gr, seg_c, seg_r, s_ref, n_ref, qkv, o_ref, p_ref, lse_ref = refs
    assemble(s_ref, own, other, scal[0])
    u, _ = unit_of(s_ref[...])
    w = ws[0]()
    if windowed:
        gr = w[:, WIDE:].astype(F32).T[0:8, :]
        gr_ref[...] = gr
    n = (u * gr[index : index + 1, :]).astype(BF16)
    n_ref[...] = n
    qkv[...] = nn(n, w[:, 0:WIDE]).astype(BF16)
    if windowed:
        bias = window_bias(qkv.shape[0], scal, 1)
    else:
        bias = jnp.where(seg_c[...] == seg_r[...], 0.0, MASKED).astype(F32)
    attend(qkv, 0, qkv, HALF, 2 * HALF, bias, o_ref, lse_ref)
    p_ref[...] = nt(o_ref[...], ws[1]()[...]).astype(BF16)


def middle_kernel(index, ws, scal, s, p_own, p_oth, gr, s1, n_ref, proj):
    stream = s[...] + (p_own[...].astype(F32) + p_oth[...].astype(F32))
    s1[...] = stream
    u, _ = unit_of(stream)
    n = (u * gr[index : index + 1, :]).astype(BF16)
    n_ref[...] = n
    proj[...] = nn(n, ws[0]()[...]).astype(BF16)


def cross_kernel(masked, ws, scal, q_ref, kv_ref, o_ref, p_ref, lse_ref):
    bias = read_bias(kv_ref.shape[0], scal, 1) if masked else None
    attend(q_ref, 0, kv_ref, HALF, 2 * HALF, bias, o_ref, lse_ref)
    p_ref[...] = nt(o_ref[...], ws[0]()[...]).astype(BF16)


def mlp_kernel(index, steps, ws, scal, s1, p_own, p_oth, gr, cot_own, cot_oth,
               *refs):
    s2, send, keep, dn_ref, dg_ref, dm_ref, n_s, dy_s, nt_s, dyt_s, part_s, dn_s, cot_s = refs[-13:]
    step = pl.program_id(0)
    half = cot_own.shape[0]
    t = scal[0]

    @pl.when(step == 0)
    def _():
        for w in ws:
            w.start()
        stream = s1[...] + (p_own[...].astype(F32) + p_oth[...].astype(F32))
        s2[...] = stream
        u, _ = unit_of(stream)
        n = (u * gr[index : index + 1, :]).astype(BF16)
        n_s[...] = n
        nt_s[...] = n.T
        assemble(cot_s, cot_own, cot_oth, t)
        dy = cot_s[...].astype(BF16)
        dy_s[...] = dy
        dyt_s[...] = dy.T

    for i in range(steps):

        @pl.when(step == i)
        def _(i=i):
            ws[0](i)
            ws[1](i)

    fb = ws[0].width
    w_in = ws[0].stack[step]
    w_out = ws[1].stack[step]
    hidden = nn(n_s[...], w_in)
    phi = 0.5 * (1.0 + lax.erf(hidden * ROOT_HALF))
    act = (hidden * phi).astype(BF16)
    slope = phi + hidden * jnp.exp(-0.5 * hidden * hidden) * INV_ROOT_TAU
    dh = (nn(dy_s[...], w_out) * slope).astype(BF16)
    part = nt(act, w_out)
    dn = nt(dh, w_in)

    @pl.when(step == 0)
    def _():
        part_s[...] = part
        dn_s[...] = dn

    @pl.when(step > 0)
    def _():
        part_s[...] += part
        dn_s[...] += dn

    dm_ref[:, 0:fb] = nn(nt_s[...], dh).astype(BF16)
    dm_ref[:, fb : 2 * fb] = nn(dyt_s[...], act).astype(BF16)

    @pl.when(step == steps - 1)
    def _():
        send[...] = own_rows(part_s, 1 - t, half).astype(BF16)
        keep[...] = own_rows(part_s, t, half) + own_rows(s2, t, half)
        dn_all = dn_s[...]
        dn_ref[...] = dn_all.astype(BF16)
        u, _ = unit_of(s2[...])
        dg_ref[...] = jnp.sum(dn_all * u, axis=0, keepdims=True)


def cross_back_kernel(masked, index, ws, scal, cot_own, cot_oth, dn_own, dn_oth, s2, gr, q_ref, kv_ref, o_ref, lse_ref,
                      g_ref, dy_ref, dq_ref, dkv_ref):
    assemble(g_ref, cot_own, cot_oth, scal[0])
    u, inverse = unit_of(s2[...])
    dn = dn_own[...].astype(F32) + dn_oth[...].astype(F32)
    grad = g_ref[...] + norm_back(dn, u, inverse, gr[index : index + 1, :])
    g_ref[...] = grad
    dy = grad.astype(BF16)
    dy_ref[...] = dy
    do = nn(dy, ws[0]()[...]).astype(BF16)
    bias = read_bias(kv_ref.shape[0], scal, 0) if masked else None
    attend_back(q_ref, 0, kv_ref, HALF, 2 * HALF, bias, do, o_ref, lse_ref, dq_ref, 0, dkv_ref, 0, HALF)


def dn_kernel(ws, scal, dq, dkv, dn_ref):
    w = ws[0]()
    dn_ref[...] = (nt(dq[...], w[:, 0:HALF]) + nt(dkv[...], w[:, HALF:WIDE])).astype(BF16)


def gain_kernel(ws, scal, sv, dnv, sq, dnq, dgv, dgq):
    for s, dn, dg in ((sv, dnv, dgv), (sq, dnq, dgq)):
        u, _ = unit_of(s[...])
        dg[...] = jnp.sum(dn[...].astype(F32) * u, axis=0, keepdims=True)


def fill_weights(out, grads, dy, o):
    at = 0
    for n, grad in zip(grads[0::2], grads[1::2]):
        width = grad.shape[1]
        out[:, at : at + width] = tn(n[...], grad[...]).astype(BF16)
        at += width
    out[:, at : at + HALF] = tn(dy[...], o[...]).astype(BF16)


def weights_kernel(table, gains, parts, held, ws, scal, dy, o, *refs):
    grads, rows = refs[:parts], refs[parts : parts + gains]
    refs = refs[parts + gains + held :]
    if table is None:
        out = refs[0]
    else:
        *dealt, out = refs[:3]
    fill_weights(out, grads, dy, o)
    if gains:
        stack = refs[-1]
        stack[...] = jnp.zeros_like(stack)
        for i, row in enumerate(rows):
            stack[i : i + 1, :] = row[...]
        out[:, WIDE + HALF :] = stack[...].T.astype(BF16)
    if table is not None:
        deal(out, dealt, scal, table)


def first_back_kernel(windowed, index, later, ws, scal, *refs):
    if windowed:
        grad, dn_own, dn_oth, s1, s0, gr, qkv, o_ref, lse_ref, g_ref, dy_ref, dqkv, send, keep, dg_ref, g_s = refs
    else:
        (grad, dn_own, dn_oth, s1, s0, gr, qkv, o_ref, lse_ref, seg_c, seg_r,
         g_ref, dy_ref, dqkv, send, keep, dg_ref, g_s) = refs
    t = scal[0]
    half = g_ref.shape[0]
    u, inverse = unit_of(s1[...])
    dn = dn_own[...].astype(F32) + dn_oth[...].astype(F32)
    g = grad[...] + norm_back(dn, u, inverse, gr[later : later + 1, :])
    g_s[...] = g
    g_ref[...] = own_rows(g_s, t, half)
    dy = g.astype(BF16)
    dy_ref[...] = dy
    do = nn(dy, ws[0]()[...]).astype(BF16)
    if windowed:
        bias = window_bias(qkv.shape[0], scal, 0)
    else:
        bias = jnp.where(seg_c[...] == seg_r[...], 0.0, MASKED).astype(F32)
    attend_back(qkv, 0, qkv, HALF, 2 * HALF, bias, do, o_ref, lse_ref, dqkv, 0, dqkv, HALF, 2 * HALF)
    dn0 = nt(dqkv[...], ws[1]()[...])
    g_s[...] = dn0
    send[...] = own_rows(g_s, 1 - t, half).astype(BF16)
    keep[...] = own_rows(g_s, t, half)
    u, _ = unit_of(s0[...])
    dg_ref[...] = jnp.sum(dn0 * u, axis=0, keepdims=True)


def last_kernel(index, ws, scal, grad, keep, got, own, gr, out):
    u, inverse = unit_of(own[...].astype(F32))
    dn = keep[...] + got[...].astype(F32)
    out[...] = (grad[...] + norm_back(dn, u, inverse, gr[index : index + 1, :])).astype(BF16)


class Weight:
    def __init__(self, scal, pieces, rooms, sems, at, width, table):
        self.scal, self.pieces, self.rooms, self.sems = scal, pieces, rooms, sems
        self.at, self.width, self.table, self.waited = at, width, table, set()

    def start(self):
        for i, room in enumerate(self.rooms):
            if self.table is None:
                source = self.pieces[0].at[:, pl.ds(self.at + i * self.width, self.width)]
                pltpu.make_async_copy(source, room, self.sems[i]).start()
                continue
            for p in range(16):
                to = pl.multiple_of(self.scal[self.table + p] * 48, 16)
                pltpu.make_async_copy(
                    self.pieces[p // 8].at[pl.ds(p % 8 * 48, 48), pl.ds(self.at + i * self.width, self.width)],
                    room.at[pl.ds(to, 48), :],
                    self.sems[i],
                ).start()

    def __call__(self, i=0):
        if i not in self.waited:
            pltpu.make_async_copy(self.rooms[i], self.rooms[i], self.sems[i]).wait()
            self.waited.add(i)
        return self.rooms[i]


def deal(whole, outs, scal, table):
    for p in range(16):
        block = whole[pl.ds(pl.multiple_of(scal[table + p] * 48, 16), 48), :]
        outs[p // 8][p % 8 * 48 : p % 8 * 48 + 48, :] = block


TABLE = 4


def call(body, args, weights, outs, name, flops, scratch=(), grid=(1,), out_specs=None, into=None, gates=()):
    def whole(shape):
        return pl.BlockSpec(shape, lambda *_: (0,) * len(shape))

    in_specs = [pl.BlockSpec(memory_space=pltpu.SMEM)] + [whole(a.shape) for a in args[1:]]
    for i in into or {}:
        in_specs[i] = pl.BlockSpec(memory_space=pl.ANY)
    out_specs = out_specs or [whole(o.shape) for o in outs]
    pieces = [piece for unit, _, _, _ in weights for piece in unit[0]]
    moved = sum(a.size * a.dtype.itemsize for a in list(outs) + list(args)) + sum(1536 * w * n for _, _, w, n in weights)
    n_in, n_w, n_out = len(args), len(weights), len(outs)

    def run(*refs):
        ins, refs = refs[:n_in], refs[n_in:]
        held, refs = refs[: len(pieces)], refs[len(pieces) + len(gates) :]
        out, refs = refs[:n_out], refs[n_out:]
        own, refs = refs[: len(scratch)], refs[len(scratch) :]
        ws = []
        for i, (unit, at, width, n) in enumerate(weights):
            rooms, sems = refs[2 * i], refs[2 * i + 1]
            mine, held = held[: len(unit[0])], held[len(unit[0]) :]
            ws.append(Weight(ins[0], mine, [rooms.at[j] for j in range(n)],
                             [sems.at[j] for j in range(n)], at, width, unit[1]))
            ws[-1].stack = rooms
        if grid == (1,):
            for w in ws:
                w.start()
        body(ws, *ins, *out, *own)

    rooms = []
    for _, _, width, n in weights:
        rooms += [pltpu.VMEM((n, 768, width), BF16), pltpu.SemaphoreType.DMA((n,))]
    return pl.pallas_call(
        run,
        out_shape=outs,
        grid=grid,
        in_specs=in_specs + [pl.BlockSpec(memory_space=pl.ANY)] * (len(pieces) + len(gates)),
        out_specs=out_specs,
        scratch_shapes=list(scratch) + rooms,
        input_output_aliases=into or {},
        name=name,
        compiler_params=pltpu.CompilerParams(vmem_limit_bytes=56 * 2**20),
        cost_estimate=pl.CostEstimate(flops=int(10 * flops), bytes_accessed=int(10 * moved), transcendentals=0),
    )(*args, *pieces, *gates)


def part(body, *fixed):
    return lambda *refs: body(*fixed, *refs)


def sds(shape, dtype):
    return jax.ShapeDtypeStruct(shape, dtype)


def sds(shape, dtype):
    return jax.ShapeDtypeStruct(shape, dtype)


PLACES = [(p >> 3) | (p >> 2 & 1) << 1 | (p & 3) << 2 for p in range(16)]


def on_device(size, visual, query, seg_ids, shifts, valid_rows, attn_in, attn_out, mlp_in, mlp_out, gains, cot_visual, cot_query):
    by_steps = size == 16
    depth = gains.shape[1]
    rv, rq = 2 * visual.shape[0], 2 * query.shape[0]

    def swap(a):
        return lax.ppermute(a, "tensor", [(0, 1), (1, 0)])

    def across(a, bit):
        return lax.ppermute(a, "dp", [(i, i ^ bit) for i in range(size)])

    def gather(a):
        return [lax.all_gather(a, "dp", axis=0, tiled=True)], None

    def after(a, *others):
        return lax.optimization_barrier((a, *others))[0]

    def scatter(a):
        return lax.psum_scatter(a, "dp", scatter_dimension=0, tiled=True)

    table = TABLE if by_steps else None

    class Gather:
        def __init__(self, a, *others):
            self.cur = after(a, *others) if others else a
            if by_steps:
                self.cur = jnp.concatenate([self.cur] + [across(self.cur, 4 * k) for k in (1, 2, 3)], axis=0)

        def along_y(self, *others):
            if by_steps:
                cur = after(self.cur, *others) if others else self.cur
                self.cur = jnp.concatenate([cur, across(cur, 2)], axis=0)

        def finish(self, *others):
            if not by_steps:
                return gather(self.cur)
            cur = after(self.cur, *others) if others else self.cur
            return [cur, across(cur, 1)], table

    class Scatter:
        def __init__(self, dealt):
            self.kept, self.sent, self.step = dealt[0], [dealt[-1]], 0
            self.got = None
            if not by_steps:
                self.kept = self.total = scatter(dealt[0])

        @staticmethod
        def joined(a, b):
            both = Scatter.__new__(Scatter)
            both.kept, both.step = jnp.concatenate([a.kept, b.kept], axis=1), a.step
            if by_steps:
                both.sent = [jnp.concatenate(pair, axis=1) for pair in zip(a.sent, b.sent)]
            both.total = both.kept
            return both

        def send(self, *others):
            if not by_steps:
                return
            sent = [after(a, *others) if others else a for a in self.sent]
            bits = ((1,), (2,), (4, 8, 12))[self.step]
            self.got = [across(a, bit) for a, bit in zip(sent, bits)]
            self.step += 1

        def add(self):
            if not by_steps:
                return self.total
            total = sum([a.astype(F32) for a in self.got], self.kept.astype(F32))
            self.total, low = total, total.astype(BF16)
            if self.step == 1:
                self.kept, self.sent = low[:192], [low[192:]]
            else:
                self.kept, self.sent = low[:48], [low[48:96], low[96:144], low[144:]]
            return self.kept

    def dealt_shapes(width, table):
        return [sds((768, width), BF16)] if table is None else [sds((HALF, width), BF16)] * 2

    t = lax.axis_index("tensor").astype(jnp.int32)
    me = lax.axis_index("dp").astype(jnp.int32)
    scal = jnp.concatenate([t[None], shifts[0], valid_rows, jnp.array(PLACES, jnp.int32) ^ me])
    seg_r = seg_ids
    seg_c = seg_ids.reshape(-1, 1)

    a_in = attn_in.astype(BF16)
    gain_cols = jnp.pad(gains.T.astype(BF16), ((0, 0), (0, 122)))
    m_in = mlp_in.astype(BF16)
    m_out = mlp_out.astype(BF16).transpose(0, 2, 1)
    aot = attn_out.astype(BF16).transpose(0, 2, 1)
    g0 = Gather(jnp.concatenate([a_in[0].reshape(depth, WIDE), gain_cols, aot[0]], axis=1))
    g1 = Gather(jnp.concatenate([a_in[1].reshape(depth, WIDE), aot[1]], axis=1))
    bulk = [a_in[3][:, 0], a_in[2][:, 1], a_in[2][:, 2], a_in[2][:, 0], a_in[3][:, 1], a_in[3][:, 2], aot[2], aot[3]]
    bulk_own = jnp.concatenate(bulk, axis=1)
    bulk = gather(bulk_own)
    m0 = jnp.concatenate([m_in[0], m_out[0]], axis=1)
    m1 = gather(after(jnp.concatenate([m_in[1], m_out[1]], axis=1), m0))
    m0 = gather(after(m0, bulk_own))
    x_oth, q_oth = swap(visual), swap(query)
    cv_oth, cq_oth = swap(after(cot_visual, x_oth, q_oth)), swap(after(cot_query, x_oth, q_oth))
    g0.along_y()
    in0 = g0.finish()
    g1.along_y()
    in1 = g1.finish()

    def output(a):
        return ((in0, WIDE + 128), (in1, WIDE), (bulk, 2 * WIDE), (bulk, 2 * WIDE + HALF))[a] + (HALF, 1)

    def first(windowed, own, other, at, rows, unit, more, gates):
        outs = [sds((rows, 768), F32), sds((rows, 768), BF16), sds((rows, WIDE), BF16), sds((rows, HALF), BF16), sds((rows, 768), BF16), sds((8, rows), F32)]
        if windowed:
            outs.append(sds((8, 768), F32))
        width = WIDE + 128 if windowed else WIDE
        return call(part(first_kernel, windowed, at), [scal, own, other, *more], [(unit, 0, width, 1), output(at)], outs, "first_%d" % at, 4e9, gates=gates)

    sv0, nv0, qkv0, o0, p0, l0, gr = first(True, visual, x_oth, 0, rv, in0, [], [cv_oth])
    p0_oth = swap(p0)
    sq0, nq0, qkv1, o1, p1, l1 = first(False, query, q_oth, 1, rq, in1, [gr, seg_c, seg_r], [cq_oth])
    p1_oth = swap(p1)

    def middle(index, s, p, p_oth, at, rows):
        return call(
            part(middle_kernel, index), [scal, s, p, p_oth, gr], [(bulk, at, WIDE, 1)],
            [sds((rows, 768), F32), sds((rows, 768), BF16), sds((rows, WIDE), BF16)], "middle_%d" % index, 2e9)

    sv1, nv, pv = middle(2, sv0, p0, p0_oth, 0, rv)
    sq1, nq, pq = middle(3, sq0, p1, p1_oth, WIDE, rq)

    def cross(masked, q, kv, a, name, gates):
        outs = [sds((q.shape[0], HALF), BF16), sds((q.shape[0], 768), BF16), sds((8, q.shape[0]), F32)]
        return call(part(cross_kernel, masked), [scal, q, kv], [output(a)], outs, name, 2e9, gates=gates)

    o3, p3, l3 = cross(False, pv, pq, 3, "look", [])
    p3_oth = swap(p3)
    o2, p2, l2 = cross(True, pq, pv, 2, "read", [o3])
    p2_oth = swap(p2)

    fb = 512
    steps = 1536 // fb

    def mlp(index, s1, p, p_oth, cot, cot_oth, unit, rows, into, gates=()):
        half = rows // 2
        first = 0 if into is None else steps
        dealt = pl.BlockSpec((768, 2 * fb), lambda i: (0, first + i))
        args = [scal, s1, p, p_oth, gr, cot, cot_oth] + ([] if into is None else [into])
        outs = [sds((rows, 768), F32), sds((half, 768), BF16), sds((half, 768), F32), sds((rows, 768), BF16), sds((1, 768), F32)]
        return call(
            part(mlp_kernel, index, steps), args,
            [(unit, 0, fb, steps), (unit, 1536, fb, steps)], outs + [sds((768, 6144), BF16)],
            "mlp_%d" % index, 10 * rows * 768 * 1536,
            scratch=[pltpu.VMEM((rows, 768), BF16), pltpu.VMEM((rows, 768), BF16), pltpu.VMEM((768, rows), BF16),
                     pltpu.VMEM((768, rows), BF16), pltpu.VMEM((rows, 768), F32), pltpu.VMEM((rows, 768), F32),
                     pltpu.VMEM((rows, 768), F32)],
            grid=(steps,), out_specs=[pl.BlockSpec(o.shape, lambda i: (0, 0)) for o in outs] + [dealt], gates=gates, into={} if into is None else {7: 5})

    sv2, part_v, keep_v, dnv4, dg4, dm = mlp(4, sv1, p3, p3_oth, cot_visual, cv_oth, m0, rv, None, [o2])
    dnv4_oth = swap(dnv4)
    sq2, part_q, keep_q, dnq5, dg5, dm = mlp(5, sq1, p2, p2_oth, cot_query, cq_oth, m1, rq, dm, [dnv4])
    dnq5_oth = swap(dnq5)
    s3 = scatter(dm)

    def cross_back(masked, index, cot, cot_oth, dn, dn_oth, s2, a, q, kv, o, lse, name, gates=()):
        return call(
            part(cross_back_kernel, masked, index), [scal, cot, cot_oth, dn, dn_oth, s2, gr, q, kv, o, lse], [output(a)],
            [sds((q.shape[0], 768), F32), sds((q.shape[0], 768), BF16), sds((q.shape[0], HALF), BF16), sds((kv.shape[0], 768), BF16)],
            name, 6e9, gates=gates)

    gv2, dyv, dq3, dkv3 = cross_back(False, 4, cot_visual, cv_oth, dnv4, dnv4_oth, sv2, 3, pv, pq, o3, l3, "look_back", [sq2])
    def dn_of(dq, dkv, at, rows, name, gates):
        return call(dn_kernel, [scal, dq, dkv], [(bulk, at, WIDE, 1)], [sds((rows, 768), BF16)], name, 1e9, gates=gates)[0]

    def weights(grads, dy, o, name, gains=(), gates=(), at=0, blocks=1, into=()):
        width = WIDE + HALF + (128 if gains else 0)
        scratch = [] if table is None else [pltpu.VMEM((768, width), BF16)]
        if gains:
            scratch.append(pltpu.VMEM((128, 768), F32))
        args = [scal, dy, o, *grads, *gains, *into]
        shapes = dealt_shapes(width * blocks, table)
        return call(part(weights_kernel, table, len(gains), len(grads), len(into)), args, [], shapes, name, 1.5e9,
                    scratch=scratch, gates=gates, out_specs=[pl.BlockSpec((a.shape[0], width), lambda i: (0, at)) for a in shapes],
                    into={len(args) - len(into) + i: i for i in range(len(into))})

    hl = Scatter(weights([nv, dq3, nq, dkv3], dyv, o3, "weights_look"))
    gates = [hl.kept]
    hl.send()
    gq2, dyq, dq2, dkv2 = cross_back(True, 5, cot_query, cq_oth, dnq5, dnq5_oth, sq2, 2, pq, pv, o2, l2, "read_back", gates)

    dnv2 = dn_of(dq3, dkv2, 0, rv, "dn_2", [hl.add()])
    dnv2_oth = swap(dnv2)
    dnq3 = dn_of(dq2, dkv3, WIDE, rq, "dn_3", [dnv2])
    dnq3_oth = swap(dnq3)

    hl.send()
    hr = Scatter(weights([nq, dq2, nv, dkv2], dyq, o2, "weights_read", gates=[dnv2, dnq3]))
    hr.send()
    dg2, dg3 = call(gain_kernel, [scal, sv1, dnv2, sq1, dnq3], [], [sds((1, 768), F32)] * 2, "gain_sums", 1e7, gates=[hr.kept])
    gates = [dg2]

    def first_back(windowed, index, later, grad, dn, dn_oth, s1, s0, unit, qkv, o, lse, rows, more, gates):
        half = rows // 2
        outs = [sds((half, 768), F32), sds((rows, 768), BF16), sds((rows, WIDE), BF16), sds((half, 768), BF16),
                sds((half, 768), F32), sds((1, 768), F32)]
        return call(part(first_back_kernel, windowed, index, later), [scal, grad, dn, dn_oth, s1, s0, gr, qkv, o, lse, *more],
                    [output(index), (unit, 0, WIDE, 1)], outs, "first_back_%d" % index, 7e9,
                    scratch=[pltpu.VMEM((rows, 768), F32)], gates=gates)

    gv1, dy0, d0, send_v, hold_v, dg0 = first_back(True, 0, 2, gv2, dnv2, dnv2_oth, sv1, sv0, in0, qkv0, o0, l0, rv, [], gates)
    got_v = swap(send_v)
    h0 = Scatter(weights([nv0, d0], dy0, o0, "weights_0", gates=[hl.add(), hr.add()]))
    hl.send()
    hr.send()
    h0.send()
    gates = [h0.kept]
    gq1, dy1, d1, send_q, hold_q, dg1 = first_back(False, 1, 3, gq2, dnq3, dnq3_oth, sq1, sq0, in1, qkv1, o1, l1, rq, [seg_c, seg_r], gates)
    h1 = Scatter(weights([nq0, d1], dy1, o1, "weights_1", [dg0, dg1, dg2, dg3, dg4, dg5], [hl.add(), h0.add()]))
    h0.send()
    h1.send()
    hr.add()
    gates = [h1.add()]
    h1.send()
    hr.send(*gates)
    got_q = swap(send_q)
    h0.add()
    h1.add()
    hr.add()
    both = Scatter.joined(h0, h1)
    both.send()
    both.add()
    s0, s1 = both.total[:, : WIDE + HALF], both.total[:, WIDE + HALF :]
    m3 = s3.reshape(depth, 2, steps, 2, fb)
    grad_up = m3[:, :, :, 0].transpose(1, 0, 2, 3).reshape(2, depth, 1536).astype(F32)
    grad_down = m3[:, :, :, 1].reshape(depth, 2, 1536).transpose(1, 2, 0).astype(F32)
    look, read = hl.total, hr.total
    out_visual = (keep_v + swap(after(part_v, *gates)).astype(F32)).astype(BF16)
    out_query = (keep_q + swap(after(part_q, *gates)).astype(F32)).astype(BF16)

    def last(index, grad, keep, got, own, gates):
        return call(part(last_kernel, index), [scal, grad, keep, got, own, gr], [], [sds(own.shape, BF16)], "last_%d" % index, 1e7, gates=gates)[0]

    grad_visual = last(0, gv1, hold_v, got_v, visual, gates)
    grad_query = last(1, gq1, hold_q, got_q, query, gates)

    def slots(a):
        return a[:, 0:WIDE].reshape(depth, 3, HALF)

    grad_in = jnp.stack([slots(s0), slots(s1), slots(read), slots(look)]).astype(F32)
    grad_out = jnp.stack([a[:, WIDE : WIDE + HALF].T for a in (s0, s1, read, look)]).astype(F32)
    gsum = s1[:, WIDE + HALF :].astype(F32)
    gsum = gsum + swap(gsum)
    grad_gain = gsum[:, 0:6].T
    return out_visual, out_query, grad_visual, grad_query, grad_in, grad_out, grad_up, grad_down, grad_gain


def solution(mesh):
    rows = P(("dp", "tensor"), None)
    weights = (P(None, "dp", None, "tensor"), P(None, "tensor", "dp"), P(None, "dp", "tensor"), P(None, "tensor", "dp"), P(None, "dp"))
    in_specs = (rows, rows, P("dp", None), P("dp", None), P("dp")) + weights + (rows, rows)
    out_specs = (rows, rows, rows, rows) + weights
    body = part(on_device, mesh.shape["dp"])
    return jax.shard_map(body, mesh=mesh, in_specs=in_specs, out_specs=out_specs, check_vma=False)
```

```python
import jax
import jax.numpy as jnp
from jax import lax
from jax.experimental import pallas as pl
from jax.experimental.pallas import tpu as pltpu
from jax.sharding import PartitionSpec as P

PH = 36
PW = 12
SCALE = 0.125
EPSILON = 1e-05
MASKED = -1e30
ROOT_HALF = 0.7071067811865476
INV_ROOT_TAU = 0.3989422804014327
F32 = jnp.float32
BF16 = jnp.bfloat16
WIDE = 1152
HALF = 384


def nn(a, b):
    return lax.dot_general(a, b, (((1,), (0,)), ((), ())), preferred_element_type=F32)


def nt(a, b):
    return lax.dot_general(a, b, (((1,), (1,)), ((), ())), preferred_element_type=F32)


def tn(a, b):
    return lax.dot_general(a, b, (((0,), (0,)), ((), ())), preferred_element_type=F32)


def unit_of(s):
    centred = s - jnp.mean(s, axis=-1, keepdims=True)
    inverse = lax.rsqrt(jnp.mean(centred * centred, axis=-1, keepdims=True) + EPSILON)
    return centred * inverse, inverse


def norm_back(dn, u, inverse, gain):
    scaled = dn * gain
    centre = jnp.mean(scaled, axis=-1, keepdims=True)
    slope = jnp.mean(scaled * u, axis=-1, keepdims=True)
    return inverse * (scaled - centre - u * slope)


def assemble(dst, own, other, t):
    half = own.shape[0]
    dst[pl.ds(pl.multiple_of(t * half, 8), half), :] = own[...].astype(F32)
    dst[pl.ds(pl.multiple_of((1 - t) * half, 8), half), :] = other[...].astype(F32)


def own_rows(ref, which, half):
    return ref[pl.ds(pl.multiple_of(which * half, 8), half), :]


def head_mask(h, value):
    lane = lax.broadcasted_iota(jnp.int32, (1, 128), 1)
    return jnp.where((lane >= 64) == (h == 1), value, 0.0).astype(BF16)


def twelfth(v):
    return lax.shift_right_logical(v * 43691, 19)


def places(shape, axis, scal):
    a, b = scal[1], scal[2]
    i = lax.broadcasted_iota(jnp.int32, shape, axis)
    r = twelfth(i)
    c = i - 12 * r
    rolled = jnp.where(r < a, r - a + PH, r - a)
    region = jnp.where(r < a, 2, 0) + jnp.where(c < b, 1, 0)
    return i, r, twelfth(rolled) * 4 + region


def window_bias(n, scal, key_axis):
    shape_k = (1, n) if key_axis == 1 else (n, 1)
    shape_q = (n, 1) if key_axis == 1 else (1, n)
    ik, rk, pk = places(shape_k, key_axis, scal)
    iq, _, pq = places(shape_q, 1 - key_axis, scal)
    usable = jnp.where(rk < scal[3], pk, -1)
    allowed = (usable == pq) | (ik == iq)
    return jnp.where(allowed, 0.0, MASKED).astype(F32)


def read_bias(n, scal, key_axis):
    shape = (1, n) if key_axis == 1 else (n, 1)
    i = lax.broadcasted_iota(jnp.int32, shape, key_axis)
    return jnp.where(twelfth(i) < scal[3], 0.0, MASKED).astype(F32)


def attend(q_ref, q_at, kv_ref, k_at, v_at, bias, o_ref, lse_ref):
    lane = lax.broadcasted_iota(jnp.int32, (1, 128), 1)
    logs = jnp.zeros((q_ref.shape[0], 128), F32)
    for pair in range(3):
        at = pair * 128
        q = q_ref[:, q_at + at : q_at + at + 128]
        k = kv_ref[:, k_at + at : k_at + at + 128]
        v = kv_ref[:, v_at + at : v_at + at + 128]
        outs = []
        for h in range(2):
            s = nt(q * head_mask(h, SCALE), k)
            if bias is not None:
                s = s + bias
            top = jnp.max(s, axis=1, keepdims=True)
            e = jnp.exp(s - top)
            total = jnp.sum(e, axis=1, keepdims=True)
            outs.append(nn(e.astype(BF16), v) * (1.0 / total))
            logs = jnp.where(lane == 2 * pair + h, top + jnp.log(total), logs)
        o_ref[:, at : at + 128] = jnp.where(lane < 64, outs[0], outs[1]).astype(BF16)
    lse_ref[...] = logs.T[0:8, :]


def attend_back(q_ref, q_at, kv_ref, k_at, v_at, bias, do, o_ref, lse_ref, dq_ref, dq_at, dk_ref, dk_at, dv_at):
    product = do.astype(F32) * o_ref[...].astype(F32)
    high = product.astype(BF16)
    low = (product - high.astype(F32)).astype(BF16)
    head = lax.broadcasted_iota(jnp.int32, (8, HALF), 0)
    column = lax.broadcasted_iota(jnp.int32, (8, HALF), 1)
    pick = jnp.where((column >= 64 * head) & (column < 64 * head + 64), 1.0, 0.0).astype(BF16)
    deltas = nt(pick, high) + nt(pick, low)
    for pair in range(3):
        at = pair * 128
        q = q_ref[:, q_at + at : q_at + at + 128]
        k = kv_ref[:, k_at + at : k_at + at + 128]
        v = kv_ref[:, v_at + at : v_at + at + 128]
        dop = do[:, at : at + 128]
        dq, dk, dv = 0.0, 0.0, 0.0
        for h in range(2):
            row = 2 * pair + h
            keep = head_mask(h, 1.0)
            qm = q * head_mask(h, SCALE)
            dom = dop * keep
            s = nt(k, qm)
            if bias is not None:
                s = s + bias
            p = jnp.exp(s - lse_ref[row : row + 1, :])
            ds = (p * (nt(v, dom) - deltas[row : row + 1, :])).astype(BF16)
            dv = dv + nn(p.astype(BF16), dom)
            dk = dk + nn(ds, qm)
            dq = dq + tn(ds, k * keep)
        dq_ref[:, dq_at + at : dq_at + at + 128] = (dq * SCALE).astype(BF16)
        dk_ref[:, dk_at + at : dk_at + at + 128] = dk.astype(BF16)
        dk_ref[:, dv_at + at : dv_at + at + 128] = dv.astype(BF16)


def first_kernel(windowed, index, ws, *refs):
    if windowed:
        scal, own, other, s_ref, n_ref, qkv, o_ref, p_ref, lse_ref, gr_ref = refs
    else:
        scal, own, other, gr, seg_c, seg_r, s_ref, n_ref, qkv, o_ref, p_ref, lse_ref = refs
    assemble(s_ref, own, other, scal[0])
    u, _ = unit_of(s_ref[...])
    w = ws[0]()
    if windowed:
        gr = w[:, WIDE:].astype(F32).T[0:8, :]
        gr_ref[...] = gr
    n = (u * gr[index : index + 1, :]).astype(BF16)
    n_ref[...] = n
    qkv[...] = nn(n, w[:, 0:WIDE]).astype(BF16)
    if windowed:
        bias = window_bias(qkv.shape[0], scal, 1)
    else:
        bias = jnp.where(seg_c[...] == seg_r[...], 0.0, MASKED).astype(F32)
    attend(qkv, 0, qkv, HALF, 2 * HALF, bias, o_ref, lse_ref)
    p_ref[...] = nt(o_ref[...], ws[1]()[...]).astype(BF16)


def middle_kernel(index, ws, scal, s, p_own, p_oth, gr, s1, n_ref, proj):
    stream = s[...] + (p_own[...].astype(F32) + p_oth[...].astype(F32))
    s1[...] = stream
    u, _ = unit_of(stream)
    n = (u * gr[index : index + 1, :]).astype(BF16)
    n_ref[...] = n
    proj[...] = nn(n, ws[0]()[...]).astype(BF16)


def cross_kernel(masked, ws, scal, q_ref, kv_ref, o_ref, p_ref, lse_ref):
    bias = read_bias(kv_ref.shape[0], scal, 1) if masked else None
    attend(q_ref, 0, kv_ref, HALF, 2 * HALF, bias, o_ref, lse_ref)
    p_ref[...] = nt(o_ref[...], ws[0]()[...]).astype(BF16)


def mlp_kernel(index, steps, ws, scal, s1, p_own, p_oth, gr, cot_own, cot_oth,
               *refs):
    s2, send, keep, dn_ref, dg_ref, dm_ref, n_s, dy_s, nt_s, dyt_s, part_s, dn_s, cot_s = refs[-13:]
    step = pl.program_id(0)
    half = cot_own.shape[0]
    t = scal[0]

    @pl.when(step == 0)
    def _():
        for w in ws:
            w.start()
        stream = s1[...] + (p_own[...].astype(F32) + p_oth[...].astype(F32))
        s2[...] = stream
        u, _ = unit_of(stream)
        n = (u * gr[index : index + 1, :]).astype(BF16)
        n_s[...] = n
        nt_s[...] = n.T
        assemble(cot_s, cot_own, cot_oth, t)
        dy = cot_s[...].astype(BF16)
        dy_s[...] = dy
        dyt_s[...] = dy.T

    for i in range(steps):

        @pl.when(step == i)
        def _(i=i):
            ws[0](i)
            ws[1](i)

    fb = ws[0].width
    w_in = ws[0].stack[step]
    w_out = ws[1].stack[step]
    hidden = nn(n_s[...], w_in)
    phi = 0.5 * (1.0 + lax.erf(hidden * ROOT_HALF))
    act = (hidden * phi).astype(BF16)
    slope = phi + hidden * jnp.exp(-0.5 * hidden * hidden) * INV_ROOT_TAU
    dh = (nn(dy_s[...], w_out) * slope).astype(BF16)
    part = nt(act, w_out)
    dn = nt(dh, w_in)

    @pl.when(step == 0)
    def _():
        part_s[...] = part
        dn_s[...] = dn

    @pl.when(step > 0)
    def _():
        part_s[...] += part
        dn_s[...] += dn

    dm_ref[:, 0:fb] = nn(nt_s[...], dh).astype(BF16)
    dm_ref[:, fb : 2 * fb] = nn(dyt_s[...], act).astype(BF16)

    @pl.when(step == steps - 1)
    def _():
        send[...] = own_rows(part_s, 1 - t, half).astype(BF16)
        keep[...] = own_rows(part_s, t, half) + own_rows(s2, t, half)
        dn_all = dn_s[...]
        dn_ref[...] = dn_all.astype(BF16)
        u, _ = unit_of(s2[...])
        dg_ref[...] = jnp.sum(dn_all * u, axis=0, keepdims=True)


def cross_back_kernel(masked, index, ws, scal, cot_own, cot_oth, dn_own, dn_oth, s2, gr, q_ref, kv_ref, o_ref, lse_ref,
                      g_ref, dy_ref, dq_ref, dkv_ref):
    assemble(g_ref, cot_own, cot_oth, scal[0])
    u, inverse = unit_of(s2[...])
    dn = dn_own[...].astype(F32) + dn_oth[...].astype(F32)
    grad = g_ref[...] + norm_back(dn, u, inverse, gr[index : index + 1, :])
    g_ref[...] = grad
    dy = grad.astype(BF16)
    dy_ref[...] = dy
    do = nn(dy, ws[0]()[...]).astype(BF16)
    bias = read_bias(kv_ref.shape[0], scal, 0) if masked else None
    attend_back(q_ref, 0, kv_ref, HALF, 2 * HALF, bias, do, o_ref, lse_ref, dq_ref, 0, dkv_ref, 0, HALF)


def dn_kernel(ws, scal, dq, dkv, dn_ref):
    w = ws[0]()
    dn_ref[...] = (nt(dq[...], w[:, 0:HALF]) + nt(dkv[...], w[:, HALF:WIDE])).astype(BF16)


def fill_weights(out, grads, dy, o):
    at = 0
    for n, grad in zip(grads[0::2], grads[1::2]):
        width = grad.shape[1]
        out[:, at : at + width] = tn(n[...], grad[...]).astype(BF16)
        at += width
    out[:, at : at + HALF] = tn(dy[...], o[...]).astype(BF16)


def weights_kernel(table, gains, parts, held, ws, scal, dy, o, *refs):
    grads, rows = refs[:parts], refs[parts : parts + gains]
    refs = refs[parts + gains + held :]
    if table is None:
        out = refs[0]
    else:
        *dealt, out = refs[:3]
    fill_weights(out, grads, dy, o)
    if gains:
        stack = refs[-1]
        stack[...] = jnp.zeros_like(stack)
        for i, row in enumerate(rows):
            stack[i : i + 1, :] = row[...]
        out[:, WIDE + HALF :] = stack[...].T.astype(BF16)
    if table is not None:
        deal(out, dealt, scal, table)


def first_back_kernel(windowed, index, later, ws, scal, *refs):
    if windowed:
        grad, dn_own, dn_oth, s1, s0, gr, qkv, o_ref, lse_ref, g_ref, dy_ref, dqkv, send, keep, dg_ref, dg_later, g_s = refs
    else:
        (grad, dn_own, dn_oth, s1, s0, gr, qkv, o_ref, lse_ref, seg_c, seg_r,
         g_ref, dy_ref, dqkv, send, keep, dg_ref, dg_later, g_s) = refs
    t = scal[0]
    half = g_ref.shape[0]
    u, inverse = unit_of(s1[...])
    dn = dn_own[...].astype(F32) + dn_oth[...].astype(F32)
    dg_later[...] = jnp.sum(dn_own[...].astype(F32) * u, axis=0, keepdims=True)
    g = grad[...] + norm_back(dn, u, inverse, gr[later : later + 1, :])
    g_s[...] = g
    g_ref[...] = own_rows(g_s, t, half)
    dy = g.astype(BF16)
    dy_ref[...] = dy
    do = nn(dy, ws[0]()[...]).astype(BF16)
    if windowed:
        bias = window_bias(qkv.shape[0], scal, 0)
    else:
        bias = jnp.where(seg_c[...] == seg_r[...], 0.0, MASKED).astype(F32)
    attend_back(qkv, 0, qkv, HALF, 2 * HALF, bias, do, o_ref, lse_ref, dqkv, 0, dqkv, HALF, 2 * HALF)
    dn0 = nt(dqkv[...], ws[1]()[...])
    g_s[...] = dn0
    send[...] = own_rows(g_s, 1 - t, half).astype(BF16)
    keep[...] = own_rows(g_s, t, half)
    u, _ = unit_of(s0[...])
    dg_ref[...] = jnp.sum(dn0 * u, axis=0, keepdims=True)


def last_kernel(index, ws, scal, grad, keep, got, own, gr, out):
    u, inverse = unit_of(own[...].astype(F32))
    dn = keep[...] + got[...].astype(F32)
    out[...] = (grad[...] + norm_back(dn, u, inverse, gr[index : index + 1, :])).astype(BF16)


class Weight:
    def __init__(self, scal, pieces, rooms, sems, at, width, table):
        self.scal, self.pieces, self.rooms, self.sems = scal, pieces, rooms, sems
        self.at, self.width, self.table, self.waited = at, width, table, set()

    def start(self):
        for i, room in enumerate(self.rooms):
            if self.table is None:
                source = self.pieces[0].at[:, pl.ds(self.at + i * self.width, self.width)]
                pltpu.make_async_copy(source, room, self.sems[i]).start()
                continue
            for p in range(16):
                to = pl.multiple_of(self.scal[self.table + p] * 48, 16)
                pltpu.make_async_copy(
                    self.pieces[p // 8].at[pl.ds(p % 8 * 48, 48), pl.ds(self.at + i * self.width, self.width)],
                    room.at[pl.ds(to, 48), :],
                    self.sems[i],
                ).start()

    def __call__(self, i=0):
        if i not in self.waited:
            pltpu.make_async_copy(self.rooms[i], self.rooms[i], self.sems[i]).wait()
            self.waited.add(i)
        return self.rooms[i]


def deal(whole, outs, scal, table):
    for p in range(16):
        block = whole[pl.ds(pl.multiple_of(scal[table + p] * 48, 16), 48), :]
        outs[p // 8][p % 8 * 48 : p % 8 * 48 + 48, :] = block


TABLE = 4


def call(body, args, weights, outs, name, flops, scratch=(), grid=(1,), out_specs=None, into=None, gates=()):
    def whole(shape):
        return pl.BlockSpec(shape, lambda *_: (0,) * len(shape))

    in_specs = [pl.BlockSpec(memory_space=pltpu.SMEM)] + [whole(a.shape) for a in args[1:]]
    for i in into or {}:
        in_specs[i] = pl.BlockSpec(memory_space=pl.ANY)
    out_specs = out_specs or [whole(o.shape) for o in outs]
    pieces = [piece for unit, _, _, _ in weights for piece in unit[0]]
    moved = sum(a.size * a.dtype.itemsize for a in list(outs) + list(args)) + sum(1536 * w * n for _, _, w, n in weights)
    n_in, n_w, n_out = len(args), len(weights), len(outs)

    def run(*refs):
        ins, refs = refs[:n_in], refs[n_in:]
        held, refs = refs[: len(pieces)], refs[len(pieces) + len(gates) :]
        out, refs = refs[:n_out], refs[n_out:]
        own, refs = refs[: len(scratch)], refs[len(scratch) :]
        ws = []
        for i, (unit, at, width, n) in enumerate(weights):
            rooms, sems = refs[2 * i], refs[2 * i + 1]
            mine, held = held[: len(unit[0])], held[len(unit[0]) :]
            ws.append(Weight(ins[0], mine, [rooms.at[j] for j in range(n)],
                             [sems.at[j] for j in range(n)], at, width, unit[1]))
            ws[-1].stack = rooms
        if grid == (1,):
            for w in ws:
                w.start()
        body(ws, *ins, *out, *own)

    rooms = []
    for _, _, width, n in weights:
        rooms += [pltpu.VMEM((n, 768, width), BF16), pltpu.SemaphoreType.DMA((n,))]
    return pl.pallas_call(
        run,
        out_shape=outs,
        grid=grid,
        in_specs=in_specs + [pl.BlockSpec(memory_space=pl.ANY)] * (len(pieces) + len(gates)),
        out_specs=out_specs,
        scratch_shapes=list(scratch) + rooms,
        input_output_aliases=into or {},
        name=name,
        compiler_params=pltpu.CompilerParams(vmem_limit_bytes=56 * 2**20),
        cost_estimate=pl.CostEstimate(flops=int(10 * flops), bytes_accessed=int(10 * moved), transcendentals=0),
    )(*args, *pieces, *gates)


def part(body, *fixed):
    return lambda *refs: body(*fixed, *refs)


def sds(shape, dtype):
    return jax.ShapeDtypeStruct(shape, dtype)


def sds(shape, dtype):
    return jax.ShapeDtypeStruct(shape, dtype)


PLACES = [(p >> 3) | (p >> 2 & 1) << 1 | (p & 3) << 2 for p in range(16)]


def on_device(size, visual, query, seg_ids, shifts, valid_rows, attn_in, attn_out, mlp_in, mlp_out, gains, cot_visual, cot_query):
    by_steps = size == 16
    depth = gains.shape[1]
    rv, rq = 2 * visual.shape[0], 2 * query.shape[0]

    def swap(a):
        return lax.ppermute(a, "tensor", [(0, 1), (1, 0)])

    def across(a, bit):
        return lax.ppermute(a, "dp", [(i, i ^ bit) for i in range(size)])

    def gather(a):
        return [lax.all_gather(a, "dp", axis=0, tiled=True)], None

    def after(a, *others):
        return lax.optimization_barrier((a, *others))[0]

    def scatter(a):
        return lax.psum_scatter(a, "dp", scatter_dimension=0, tiled=True)

    table = TABLE if by_steps else None

    class Gather:
        def __init__(self, a, *others):
            self.cur = after(a, *others) if others else a
            if by_steps:
                self.cur = jnp.concatenate([self.cur] + [across(self.cur, 4 * k) for k in (1, 2, 3)], axis=0)

        def along_y(self, *others):
            if by_steps:
                cur = after(self.cur, *others) if others else self.cur
                self.cur = jnp.concatenate([cur, across(cur, 2)], axis=0)

        def finish(self, *others):
            if not by_steps:
                return gather(self.cur)
            cur = after(self.cur, *others) if others else self.cur
            return [cur, across(cur, 1)], table

    class Scatter:
        def __init__(self, dealt):
            self.kept, self.sent, self.step = dealt[0], [dealt[-1]], 0
            self.got = None
            if not by_steps:
                self.kept = self.total = scatter(dealt[0])

        @staticmethod
        def joined(a, b):
            both = Scatter.__new__(Scatter)
            both.kept, both.step = jnp.concatenate([a.kept, b.kept], axis=1), a.step
            if by_steps:
                both.sent = [jnp.concatenate(pair, axis=1) for pair in zip(a.sent, b.sent)]
            both.total = both.kept
            return both

        def send(self, *others):
            if not by_steps:
                return
            sent = [after(a, *others) if others else a for a in self.sent]
            bits = ((1,), (2,), (4, 8, 12))[self.step]
            self.got = [across(a, bit) for a, bit in zip(sent, bits)]
            self.step += 1

        def add(self, *others):
            if not by_steps:
                return self.total
            got = [after(a, *others) if others else a for a in self.got]
            total = sum([a.astype(F32) for a in got], self.kept.astype(F32))
            self.total, low = total, total.astype(BF16)
            if self.step == 1:
                self.kept, self.sent = low[:192], [low[192:]]
            else:
                self.kept, self.sent = low[:48], [low[48:96], low[96:144], low[144:]]
            return self.kept

    def dealt_shapes(width, table):
        return [sds((768, width), BF16)] if table is None else [sds((HALF, width), BF16)] * 2

    t = lax.axis_index("tensor").astype(jnp.int32)
    me = lax.axis_index("dp").astype(jnp.int32)
    scal = jnp.concatenate([t[None], shifts[0], valid_rows, jnp.array(PLACES, jnp.int32) ^ me])
    seg_r = seg_ids
    seg_c = seg_ids.reshape(-1, 1)

    a_in = attn_in.astype(BF16)
    gain_cols = jnp.pad(gains.T.astype(BF16), ((0, 0), (0, 122)))
    m_in = mlp_in.astype(BF16)
    m_out = mlp_out.astype(BF16).transpose(0, 2, 1)
    aot = attn_out.astype(BF16).transpose(0, 2, 1)
    g0 = Gather(jnp.concatenate([a_in[0].reshape(depth, WIDE), gain_cols, aot[0]], axis=1))
    g1 = Gather(jnp.concatenate([a_in[1].reshape(depth, WIDE), aot[1]], axis=1))
    bulk = [a_in[3][:, 0], a_in[2][:, 1], a_in[2][:, 2], a_in[2][:, 0], a_in[3][:, 1], a_in[3][:, 2], aot[2], aot[3]]
    bulk_own = jnp.concatenate(bulk, axis=1)
    bulk = gather(bulk_own)
    m0 = jnp.concatenate([m_in[0], m_out[0]], axis=1)
    m1 = gather(after(jnp.concatenate([m_in[1], m_out[1]], axis=1), m0))
    m0 = gather(after(m0, bulk_own))
    x_oth, q_oth = swap(visual), swap(query)
    cv_oth, cq_oth = swap(after(cot_visual, x_oth, q_oth)), swap(after(cot_query, x_oth, q_oth))
    g0.along_y()
    in0 = g0.finish()
    g1.along_y()
    in1 = g1.finish()

    def output(a):
        return ((in0, WIDE + 128), (in1, WIDE), (bulk, 2 * WIDE), (bulk, 2 * WIDE + HALF))[a] + (HALF, 1)

    def first(windowed, own, other, at, rows, unit, more, gates):
        outs = [sds((rows, 768), F32), sds((rows, 768), BF16), sds((rows, WIDE), BF16), sds((rows, HALF), BF16), sds((rows, 768), BF16), sds((8, rows), F32)]
        if windowed:
            outs.append(sds((8, 768), F32))
        width = WIDE + 128 if windowed else WIDE
        return call(part(first_kernel, windowed, at), [scal, own, other, *more], [(unit, 0, width, 1), output(at)], outs, "first_%d" % at, 4e9, gates=gates)

    sv0, nv0, qkv0, o0, p0, l0, gr = first(True, visual, x_oth, 0, rv, in0, [], [cv_oth])
    p0_oth = swap(p0)
    sq0, nq0, qkv1, o1, p1, l1 = first(False, query, q_oth, 1, rq, in1, [gr, seg_c, seg_r], [cq_oth])
    p1_oth = swap(p1)

    def middle(index, s, p, p_oth, at, rows):
        return call(
            part(middle_kernel, index), [scal, s, p, p_oth, gr], [(bulk, at, WIDE, 1)],
            [sds((rows, 768), F32), sds((rows, 768), BF16), sds((rows, WIDE), BF16)], "middle_%d" % index, 2e9)

    sv1, nv, pv = middle(2, sv0, p0, p0_oth, 0, rv)
    sq1, nq, pq = middle(3, sq0, p1, p1_oth, WIDE, rq)

    def cross(masked, q, kv, a, name, gates):
        outs = [sds((q.shape[0], HALF), BF16), sds((q.shape[0], 768), BF16), sds((8, q.shape[0]), F32)]
        return call(part(cross_kernel, masked), [scal, q, kv], [output(a)], outs, name, 2e9, gates=gates)

    o3, p3, l3 = cross(False, pv, pq, 3, "look", [])
    p3_oth = swap(p3)
    o2, p2, l2 = cross(True, pq, pv, 2, "read", [o3])
    p2_oth = swap(p2)

    fb = 768
    steps = 1536 // fb

    def mlp(index, s1, p, p_oth, cot, cot_oth, unit, rows, into, gates=()):
        half = rows // 2
        first = 0 if into is None else steps
        dealt = pl.BlockSpec((768, 2 * fb), lambda i: (0, first + i))
        args = [scal, s1, p, p_oth, gr, cot, cot_oth] + ([] if into is None else [into])
        outs = [sds((rows, 768), F32), sds((half, 768), BF16), sds((half, 768), F32), sds((rows, 768), BF16), sds((1, 768), F32)]
        return call(
            part(mlp_kernel, index, steps), args,
            [(unit, 0, fb, steps), (unit, 1536, fb, steps)], outs + [sds((768, 6144), BF16)],
            "mlp_%d" % index, 10 * rows * 768 * 1536,
            scratch=[pltpu.VMEM((rows, 768), BF16), pltpu.VMEM((rows, 768), BF16), pltpu.VMEM((768, rows), BF16),
                     pltpu.VMEM((768, rows), BF16), pltpu.VMEM((rows, 768), F32), pltpu.VMEM((rows, 768), F32),
                     pltpu.VMEM((rows, 768), F32)],
            grid=(steps,), out_specs=[pl.BlockSpec(o.shape, lambda i: (0, 0)) for o in outs] + [dealt], gates=gates, into={} if into is None else {7: 5})

    sv2, part_v, keep_v, dnv4, dg4, dm = mlp(4, sv1, p3, p3_oth, cot_visual, cv_oth, m0, rv, None, [o2])
    dnv4_oth = swap(dnv4)
    sq2, part_q, keep_q, dnq5, dg5, dm = mlp(5, sq1, p2, p2_oth, cot_query, cq_oth, m1, rq, dm, [dnv4])
    dnq5_oth = swap(dnq5)
    s3 = scatter(dm)

    def cross_back(masked, index, cot, cot_oth, dn, dn_oth, s2, a, q, kv, o, lse, name, gates=()):
        return call(
            part(cross_back_kernel, masked, index), [scal, cot, cot_oth, dn, dn_oth, s2, gr, q, kv, o, lse], [output(a)],
            [sds((q.shape[0], 768), F32), sds((q.shape[0], 768), BF16), sds((q.shape[0], HALF), BF16), sds((kv.shape[0], 768), BF16)],
            name, 6e9, gates=gates)

    gv2, dyv, dq3, dkv3 = cross_back(False, 4, cot_visual, cv_oth, dnv4, dnv4_oth, sv2, 3, pv, pq, o3, l3, "look_back", [sq2])
    def dn_of(dq, dkv, at, rows, name, gates):
        return call(dn_kernel, [scal, dq, dkv], [(bulk, at, WIDE, 1)], [sds((rows, 768), BF16)], name, 1e9, gates=gates)[0]

    def weights(grads, dy, o, name, gains=(), gates=(), at=0, blocks=1, into=()):
        width = WIDE + HALF + (128 if gains else 0)
        scratch = [] if table is None else [pltpu.VMEM((768, width), BF16)]
        if gains:
            scratch.append(pltpu.VMEM((128, 768), F32))
        args = [scal, dy, o, *grads, *gains, *into]
        shapes = dealt_shapes(width * blocks, table)
        return call(part(weights_kernel, table, len(gains), len(grads), len(into)), args, [], shapes, name, 1.5e9,
                    scratch=scratch, gates=gates, out_specs=[pl.BlockSpec((a.shape[0], width), lambda i: (0, at)) for a in shapes],
                    into={len(args) - len(into) + i: i for i in range(len(into))})

    hl = Scatter(weights([nv, dq3, nq, dkv3], dyv, o3, "weights_look"))
    gates = [hl.kept]
    hl.send()
    gq2, dyq, dq2, dkv2 = cross_back(True, 5, cot_query, cq_oth, dnq5, dnq5_oth, sq2, 2, pq, pv, o2, l2, "read_back", gates)

    dnv2 = dn_of(dq3, dkv2, 0, rv, "dn_2", [hl.add()])
    dnv2_oth = swap(dnv2)
    dnq3 = dn_of(dq2, dkv3, WIDE, rq, "dn_3", [dnv2])
    dnq3_oth = swap(dnq3)

    hl.send()
    hr = Scatter(weights([nq, dq2, nv, dkv2], dyq, o2, "weights_read", gates=[dnv2, dnq3]))
    hr.send()
    gates = [hr.kept]

    def first_back(windowed, index, later, grad, dn, dn_oth, s1, s0, unit, qkv, o, lse, rows, more, gates):
        half = rows // 2
        outs = [sds((half, 768), F32), sds((rows, 768), BF16), sds((rows, WIDE), BF16), sds((half, 768), BF16),
                sds((half, 768), F32), sds((1, 768), F32), sds((1, 768), F32)]
        return call(part(first_back_kernel, windowed, index, later), [scal, grad, dn, dn_oth, s1, s0, gr, qkv, o, lse, *more],
                    [output(index), (unit, 0, WIDE, 1)], outs, "first_back_%d" % index, 7e9,
                    scratch=[pltpu.VMEM((rows, 768), F32)], gates=gates)

    gv1, dy0, d0, send_v, hold_v, dg0, dg2 = first_back(True, 0, 2, gv2, dnv2, dnv2_oth, sv1, sv0, in0, qkv0, o0, l0, rv, [], gates)
    got_v = swap(send_v)
    h0 = Scatter(weights([nv0, d0], dy0, o0, "weights_0", gates=[hr.add()]))
    hr.send()
    h0.send()
    gates = [h0.kept]
    gq1, dy1, d1, send_q, hold_q, dg1, dg3 = first_back(False, 1, 3, gq2, dnq3, dnq3_oth, sq1, sq0, in1, qkv1, o1, l1, rq, [seg_c, seg_r], gates)
    h1 = Scatter(weights([nq0, d1], dy1, o1, "weights_1", [dg0, dg1, dg2, dg3, dg4, dg5], [hl.add(), h0.add(), hr.add()]))
    h1.send()
    gates = [h1.add()]
    both = Scatter.joined(h0, h1)
    both.send()
    hl.send(*gates)
    hr.send(*gates)
    got_q = swap(send_q)
    late = both.add()
    hl.add()
    hr.add()
    both.send()
    m3 = s3.reshape(depth, 2, steps, 2, fb)
    grad_up = m3[:, :, :, 0].transpose(1, 0, 2, 3).reshape(2, depth, 1536).astype(F32)
    grad_down = m3[:, :, :, 1].reshape(depth, 2, 1536).transpose(1, 2, 0).astype(F32)
    both.add(grad_up, grad_down)
    s0, s1 = both.total[:, : WIDE + HALF], both.total[:, WIDE + HALF :]
    look, read = hl.total, hr.total
    out_visual = (keep_v + after(swap(after(part_v, *gates)), late).astype(F32)).astype(BF16)
    out_query = (keep_q + after(swap(after(part_q, *gates)), late).astype(F32)).astype(BF16)

    def last(index, grad, keep, got, own, gates):
        return call(part(last_kernel, index), [scal, grad, keep, got, own, gr], [], [sds(own.shape, BF16)], "last_%d" % index, 1e7, gates=gates)[0]

    grad_visual = last(0, gv1, hold_v, got_v, visual, [late])
    grad_query = last(1, gq1, hold_q, got_q, query, [late])

    def slots(a):
        return a[:, 0:WIDE].reshape(depth, 3, HALF)

    grad_in = jnp.stack([slots(s0), slots(s1), slots(read), slots(look)]).astype(F32)
    grad_out = jnp.stack([a[:, WIDE : WIDE + HALF].T for a in (s0, s1, read, look)]).astype(F32)
    gsum = s1[:, WIDE + HALF :].astype(F32)
    gsum = gsum + swap(gsum)
    grad_gain = gsum[:, 0:6].T
    return out_visual, out_query, grad_visual, grad_query, grad_in, grad_out, grad_up, grad_down, grad_gain


def solution(mesh):
    rows = P(("dp", "tensor"), None)
    weights = (P(None, "dp", None, "tensor"), P(None, "tensor", "dp"), P(None, "dp", "tensor"), P(None, "tensor", "dp"), P(None, "dp"))
    in_specs = (rows, rows, P("dp", None), P("dp", None), P("dp")) + weights + (rows, rows)
    out_specs = (rows, rows, rows, rows) + weights
    body = part(on_device, mesh.shape["dp"])
    return jax.shard_map(body, mesh=mesh, in_specs=in_specs, out_specs=out_specs, check_vma=False)
```

```python
import jax
import jax.numpy as jnp
from jax import lax
from jax.experimental import pallas as pl
from jax.experimental.pallas import tpu as pltpu
from jax.sharding import PartitionSpec as P

PH = 36
PW = 12
SCALE = 0.125
EPSILON = 1e-05
MASKED = -1e30
ROOT_HALF = 0.7071067811865476
INV_ROOT_TAU = 0.3989422804014327
F32 = jnp.float32
BF16 = jnp.bfloat16
WIDE = 1152
HALF = 384


def nn(a, b):
    return lax.dot_general(a, b, (((1,), (0,)), ((), ())), preferred_element_type=F32)


def nt(a, b):
    return lax.dot_general(a, b, (((1,), (1,)), ((), ())), preferred_element_type=F32)


def tn(a, b):
    return lax.dot_general(a, b, (((0,), (0,)), ((), ())), preferred_element_type=F32)


def unit_of(s):
    centred = s - jnp.mean(s, axis=-1, keepdims=True)
    inverse = lax.rsqrt(jnp.mean(centred * centred, axis=-1, keepdims=True) + EPSILON)
    return centred * inverse, inverse


def norm_back(dn, u, inverse, gain):
    scaled = dn * gain
    centre = jnp.mean(scaled, axis=-1, keepdims=True)
    slope = jnp.mean(scaled * u, axis=-1, keepdims=True)
    return inverse * (scaled - centre - u * slope)


def assemble(dst, own, other, t):
    half = own.shape[0]
    dst[pl.ds(pl.multiple_of(t * half, 8), half), :] = own[...].astype(F32)
    dst[pl.ds(pl.multiple_of((1 - t) * half, 8), half), :] = other[...].astype(F32)


def own_rows(ref, which, half):
    return ref[pl.ds(pl.multiple_of(which * half, 8), half), :]


def head_mask(h, value):
    lane = lax.broadcasted_iota(jnp.int32, (1, 128), 1)
    return jnp.where((lane >= 64) == (h == 1), value, 0.0).astype(BF16)


def twelfth(v):
    return lax.shift_right_logical(v * 43691, 19)


def places(shape, axis, scal):
    a, b = scal[1], scal[2]
    i = lax.broadcasted_iota(jnp.int32, shape, axis)
    r = twelfth(i)
    c = i - 12 * r
    rolled = jnp.where(r < a, r - a + PH, r - a)
    region = jnp.where(r < a, 2, 0) + jnp.where(c < b, 1, 0)
    return i, r, twelfth(rolled) * 4 + region


def window_bias(n, scal, key_axis):
    shape_k = (1, n) if key_axis == 1 else (n, 1)
    shape_q = (n, 1) if key_axis == 1 else (1, n)
    ik, rk, pk = places(shape_k, key_axis, scal)
    iq, _, pq = places(shape_q, 1 - key_axis, scal)
    usable = jnp.where(rk < scal[3], pk, -1)
    allowed = (usable == pq) | (ik == iq)
    return jnp.where(allowed, 0.0, MASKED).astype(F32)


def read_bias(n, scal, key_axis):
    shape = (1, n) if key_axis == 1 else (n, 1)
    i = lax.broadcasted_iota(jnp.int32, shape, key_axis)
    return jnp.where(twelfth(i) < scal[3], 0.0, MASKED).astype(F32)


def attend(q_ref, q_at, kv_ref, k_at, v_at, bias, o_ref, lse_ref):
    lane = lax.broadcasted_iota(jnp.int32, (1, 128), 1)
    logs = jnp.zeros((q_ref.shape[0], 128), F32)
    for pair in range(3):
        at = pair * 128
        q = q_ref[:, q_at + at : q_at + at + 128]
        k = kv_ref[:, k_at + at : k_at + at + 128]
        v = kv_ref[:, v_at + at : v_at + at + 128]
        outs = []
        for h in range(2):
            s = nt(q * head_mask(h, SCALE), k)
            if bias is not None:
                s = s + bias
            top = jnp.max(s, axis=1, keepdims=True)
            e = jnp.exp(s - top)
            total = jnp.sum(e, axis=1, keepdims=True)
            outs.append(nn(e.astype(BF16), v) * (1.0 / total))
            logs = jnp.where(lane == 2 * pair + h, top + jnp.log(total), logs)
        o_ref[:, at : at + 128] = jnp.where(lane < 64, outs[0], outs[1]).astype(BF16)
    lse_ref[...] = logs.T[0:8, :]


def attend_back(q_ref, q_at, kv_ref, k_at, v_at, bias, do, o_ref, lse_ref, dq_ref, dq_at, dk_ref, dk_at, dv_at):
    product = do.astype(F32) * o_ref[...].astype(F32)
    high = product.astype(BF16)
    low = (product - high.astype(F32)).astype(BF16)
    head = lax.broadcasted_iota(jnp.int32, (8, HALF), 0)
    column = lax.broadcasted_iota(jnp.int32, (8, HALF), 1)
    pick = jnp.where((column >= 64 * head) & (column < 64 * head + 64), 1.0, 0.0).astype(BF16)
    deltas = nt(pick, high) + nt(pick, low)
    for pair in range(3):
        at = pair * 128
        q = q_ref[:, q_at + at : q_at + at + 128]
        k = kv_ref[:, k_at + at : k_at + at + 128]
        v = kv_ref[:, v_at + at : v_at + at + 128]
        dop = do[:, at : at + 128]
        dq, dk, dv = 0.0, 0.0, 0.0
        for h in range(2):
            row = 2 * pair + h
            keep = head_mask(h, 1.0)
            qm = q * head_mask(h, SCALE)
            dom = dop * keep
            s = nt(k, qm)
            if bias is not None:
                s = s + bias
            p = jnp.exp(s - lse_ref[row : row + 1, :])
            ds = (p * (nt(v, dom) - deltas[row : row + 1, :])).astype(BF16)
            dv = dv + nn(p.astype(BF16), dom)
            dk = dk + nn(ds, qm)
            dq = dq + tn(ds, k * keep)
        dq_ref[:, dq_at + at : dq_at + at + 128] = (dq * SCALE).astype(BF16)
        dk_ref[:, dk_at + at : dk_at + at + 128] = dk.astype(BF16)
        dk_ref[:, dv_at + at : dv_at + at + 128] = dv.astype(BF16)


def first_kernel(windowed, index, ws, *refs):
    if windowed:
        scal, own, other, s_ref, n_ref, qkv, o_ref, p_ref, lse_ref, gr_ref = refs
    else:
        scal, own, other, gr, seg_c, seg_r, s_ref, n_ref, qkv, o_ref, p_ref, lse_ref = refs
    assemble(s_ref, own, other, scal[0])
    u, _ = unit_of(s_ref[...])
    w = ws[0]()
    if windowed:
        gr = w[:, WIDE:].astype(F32).T[0:8, :]
        gr_ref[...] = gr
    n = (u * gr[index : index + 1, :]).astype(BF16)
    n_ref[...] = n
    qkv[...] = nn(n, w[:, 0:WIDE]).astype(BF16)
    if windowed:
        bias = window_bias(qkv.shape[0], scal, 1)
    else:
        bias = jnp.where(seg_c[...] == seg_r[...], 0.0, MASKED).astype(F32)
    attend(qkv, 0, qkv, HALF, 2 * HALF, bias, o_ref, lse_ref)
    p_ref[...] = nt(o_ref[...], ws[1]()[...]).astype(BF16)


def middle_kernel(index, ws, scal, s, p_own, p_oth, gr, s1, n_ref, proj):
    stream = s[...] + (p_own[...].astype(F32) + p_oth[...].astype(F32))
    s1[...] = stream
    u, _ = unit_of(stream)
    n = (u * gr[index : index + 1, :]).astype(BF16)
    n_ref[...] = n
    proj[...] = nn(n, ws[0]()[...]).astype(BF16)


def cross_kernel(masked, ws, scal, q_ref, kv_ref, o_ref, p_ref, lse_ref):
    bias = read_bias(kv_ref.shape[0], scal, 1) if masked else None
    attend(q_ref, 0, kv_ref, HALF, 2 * HALF, bias, o_ref, lse_ref)
    p_ref[...] = nt(o_ref[...], ws[0]()[...]).astype(BF16)


def mlp_kernel(index, steps, ws, scal, s1, p_own, p_oth, gr, cot_own, cot_oth,
               *refs):
    s2, send, keep, dn_ref, dg_ref, dm_ref, n_s, dy_s, nt_s, dyt_s, part_s, dn_s, cot_s = refs[-13:]
    step = pl.program_id(0)
    half = cot_own.shape[0]
    t = scal[0]

    @pl.when(step == 0)
    def _():
        for w in ws:
            w.start()
        stream = s1[...] + (p_own[...].astype(F32) + p_oth[...].astype(F32))
        s2[...] = stream
        u, _ = unit_of(stream)
        n = (u * gr[index : index + 1, :]).astype(BF16)
        n_s[...] = n
        nt_s[...] = n.T
        assemble(cot_s, cot_own, cot_oth, t)
        dy = cot_s[...].astype(BF16)
        dy_s[...] = dy
        dyt_s[...] = dy.T

    for i in range(steps):

        @pl.when(step == i)
        def _(i=i):
            ws[0](i)
            ws[1](i)

    fb = ws[0].width
    w_in = ws[0].stack[step]
    w_out = ws[1].stack[step]
    hidden = nn(n_s[...], w_in)
    phi = 0.5 * (1.0 + lax.erf(hidden * ROOT_HALF))
    act = (hidden * phi).astype(BF16)
    slope = phi + hidden * jnp.exp(-0.5 * hidden * hidden) * INV_ROOT_TAU
    dh = (nn(dy_s[...], w_out) * slope).astype(BF16)
    part = nt(act, w_out)
    dn = nt(dh, w_in)

    @pl.when(step == 0)
    def _():
        part_s[...] = part
        dn_s[...] = dn

    @pl.when(step > 0)
    def _():
        part_s[...] += part
        dn_s[...] += dn

    dm_ref[:, 0:fb] = nn(nt_s[...], dh).astype(BF16)
    dm_ref[:, fb : 2 * fb] = nn(dyt_s[...], act).astype(BF16)

    @pl.when(step == steps - 1)
    def _():
        send[...] = own_rows(part_s, 1 - t, half).astype(BF16)
        keep[...] = own_rows(part_s, t, half) + own_rows(s2, t, half)
        dn_all = dn_s[...]
        dn_ref[...] = dn_all.astype(BF16)
        u, _ = unit_of(s2[...])
        dg_ref[...] = jnp.sum(dn_all * u, axis=0, keepdims=True)


def cross_back_kernel(masked, index, ws, scal, cot_own, cot_oth, dn_own, dn_oth, s2, gr, q_ref, kv_ref, o_ref, lse_ref,
                      g_ref, dy_ref, dq_ref, dkv_ref):
    assemble(g_ref, cot_own, cot_oth, scal[0])
    u, inverse = unit_of(s2[...])
    dn = dn_own[...].astype(F32) + dn_oth[...].astype(F32)
    grad = g_ref[...] + norm_back(dn, u, inverse, gr[index : index + 1, :])
    g_ref[...] = grad
    dy = grad.astype(BF16)
    dy_ref[...] = dy
    do = nn(dy, ws[0]()[...]).astype(BF16)
    bias = read_bias(kv_ref.shape[0], scal, 0) if masked else None
    attend_back(q_ref, 0, kv_ref, HALF, 2 * HALF, bias, do, o_ref, lse_ref, dq_ref, 0, dkv_ref, 0, HALF)


def dn_kernel(ws, scal, dq, dkv, dn_ref):
    w = ws[0]()
    dn_ref[...] = (nt(dq[...], w[:, 0:HALF]) + nt(dkv[...], w[:, HALF:WIDE])).astype(BF16)


def fill_weights(out, grads, dy, o):
    at = 0
    for n, grad in zip(grads[0::2], grads[1::2]):
        width = grad.shape[1]
        out[:, at : at + width] = tn(n[...], grad[...]).astype(BF16)
        at += width
    out[:, at : at + HALF] = tn(dy[...], o[...]).astype(BF16)


def weights_kernel(table, gains, parts, held, ws, scal, dy, o, *refs):
    grads, rows = refs[:parts], refs[parts : parts + gains]
    refs = refs[parts + gains + held :]
    if table is None:
        out = refs[0]
    else:
        *dealt, out = refs[:3]
    fill_weights(out, grads, dy, o)
    if gains:
        stack = refs[-1]
        stack[...] = jnp.zeros_like(stack)
        for i, row in enumerate(rows):
            stack[i : i + 1, :] = row[...]
        out[:, WIDE + HALF :] = stack[...].T.astype(BF16)
    if table is not None:
        deal(out, dealt, scal, table)


def first_back_kernel(windowed, index, later, ws, scal, *refs):
    if windowed:
        grad, dn_own, dn_oth, s1, s0, gr, qkv, o_ref, lse_ref, g_ref, dy_ref, dqkv, send, keep, dg_ref, dg_later, g_s = refs
    else:
        (grad, dn_own, dn_oth, s1, s0, gr, qkv, o_ref, lse_ref, seg_c, seg_r,
         g_ref, dy_ref, dqkv, send, keep, dg_ref, dg_later, g_s) = refs
    t = scal[0]
    half = g_ref.shape[0]
    u, inverse = unit_of(s1[...])
    dn = dn_own[...].astype(F32) + dn_oth[...].astype(F32)
    dg_later[...] = jnp.sum(dn_own[...].astype(F32) * u, axis=0, keepdims=True)
    g = grad[...] + norm_back(dn, u, inverse, gr[later : later + 1, :])
    g_s[...] = g
    g_ref[...] = own_rows(g_s, t, half)
    dy = g.astype(BF16)
    dy_ref[...] = dy
    do = nn(dy, ws[0]()[...]).astype(BF16)
    if windowed:
        bias = window_bias(qkv.shape[0], scal, 0)
    else:
        bias = jnp.where(seg_c[...] == seg_r[...], 0.0, MASKED).astype(F32)
    attend_back(qkv, 0, qkv, HALF, 2 * HALF, bias, do, o_ref, lse_ref, dqkv, 0, dqkv, HALF, 2 * HALF)
    dn0 = nt(dqkv[...], ws[1]()[...])
    g_s[...] = dn0
    send[...] = own_rows(g_s, 1 - t, half).astype(BF16)
    keep[...] = own_rows(g_s, t, half)
    u, _ = unit_of(s0[...])
    dg_ref[...] = jnp.sum(dn0 * u, axis=0, keepdims=True)


def last_kernel(index, ws, scal, grad, keep, got, own, gr, out):
    u, inverse = unit_of(own[...].astype(F32))
    dn = keep[...] + got[...].astype(F32)
    out[...] = (grad[...] + norm_back(dn, u, inverse, gr[index : index + 1, :])).astype(BF16)


class Weight:
    def __init__(self, scal, pieces, rooms, sems, at, width, table):
        self.scal, self.pieces, self.rooms, self.sems = scal, pieces, rooms, sems
        self.at, self.width, self.table, self.waited = at, width, table, set()

    def start(self):
        for i, room in enumerate(self.rooms):
            if self.table is None:
                source = self.pieces[0].at[:, pl.ds(self.at + i * self.width, self.width)]
                pltpu.make_async_copy(source, room, self.sems[i]).start()
                continue
            for p in range(16):
                to = pl.multiple_of(self.scal[self.table + p] * 48, 16)
                pltpu.make_async_copy(
                    self.pieces[p // 8].at[pl.ds(p % 8 * 48, 48), pl.ds(self.at + i * self.width, self.width)],
                    room.at[pl.ds(to, 48), :],
                    self.sems[i],
                ).start()

    def __call__(self, i=0):
        if i not in self.waited:
            pltpu.make_async_copy(self.rooms[i], self.rooms[i], self.sems[i]).wait()
            self.waited.add(i)
        return self.rooms[i]


def deal(whole, outs, scal, table):
    for p in range(16):
        block = whole[pl.ds(pl.multiple_of(scal[table + p] * 48, 16), 48), :]
        outs[p // 8][p % 8 * 48 : p % 8 * 48 + 48, :] = block


TABLE = 4


def call(body, args, weights, outs, name, flops, scratch=(), grid=(1,), out_specs=None, into=None, gates=()):
    def whole(shape):
        return pl.BlockSpec(shape, lambda *_: (0,) * len(shape))

    in_specs = [pl.BlockSpec(memory_space=pltpu.SMEM)] + [whole(a.shape) for a in args[1:]]
    for i in into or {}:
        in_specs[i] = pl.BlockSpec(memory_space=pl.ANY)
    out_specs = out_specs or [whole(o.shape) for o in outs]
    pieces = [piece for unit, _, _, _ in weights for piece in unit[0]]
    moved = sum(a.size * a.dtype.itemsize for a in list(outs) + list(args)) + sum(1536 * w * n for _, _, w, n in weights)
    n_in, n_w, n_out = len(args), len(weights), len(outs)

    def run(*refs):
        ins, refs = refs[:n_in], refs[n_in:]
        held, refs = refs[: len(pieces)], refs[len(pieces) + len(gates) :]
        out, refs = refs[:n_out], refs[n_out:]
        own, refs = refs[: len(scratch)], refs[len(scratch) :]
        ws = []
        for i, (unit, at, width, n) in enumerate(weights):
            rooms, sems = refs[2 * i], refs[2 * i + 1]
            mine, held = held[: len(unit[0])], held[len(unit[0]) :]
            ws.append(Weight(ins[0], mine, [rooms.at[j] for j in range(n)],
                             [sems.at[j] for j in range(n)], at, width, unit[1]))
            ws[-1].stack = rooms
        if grid == (1,):
            for w in ws:
                w.start()
        body(ws, *ins, *out, *own)

    rooms = []
    for _, _, width, n in weights:
        rooms += [pltpu.VMEM((n, 768, width), BF16), pltpu.SemaphoreType.DMA((n,))]
    return pl.pallas_call(
        run,
        out_shape=outs,
        grid=grid,
        in_specs=in_specs + [pl.BlockSpec(memory_space=pl.ANY)] * (len(pieces) + len(gates)),
        out_specs=out_specs,
        scratch_shapes=list(scratch) + rooms,
        input_output_aliases=into or {},
        name=name,
        compiler_params=pltpu.CompilerParams(vmem_limit_bytes=56 * 2**20),
        cost_estimate=pl.CostEstimate(flops=int(10 * flops), bytes_accessed=int(10 * moved), transcendentals=0),
    )(*args, *pieces, *gates)


def part(body, *fixed):
    return lambda *refs: body(*fixed, *refs)


def sds(shape, dtype):
    return jax.ShapeDtypeStruct(shape, dtype)


def sds(shape, dtype):
    return jax.ShapeDtypeStruct(shape, dtype)


PLACES = [(p >> 3) | (p >> 2 & 1) << 1 | (p & 3) << 2 for p in range(16)]


def on_device(size, visual, query, seg_ids, shifts, valid_rows, attn_in, attn_out, mlp_in, mlp_out, gains, cot_visual, cot_query):
    by_steps = size == 16
    depth = gains.shape[1]
    rv, rq = 2 * visual.shape[0], 2 * query.shape[0]

    def swap(a):
        return lax.ppermute(a, "tensor", [(0, 1), (1, 0)])

    def across(a, bit):
        return lax.ppermute(a, "dp", [(i, i ^ bit) for i in range(size)])

    def gather(a):
        return [lax.all_gather(a, "dp", axis=0, tiled=True)], None

    def after(a, *others):
        return lax.optimization_barrier((a, *others))[0]

    def scatter(a):
        return lax.psum_scatter(a, "dp", scatter_dimension=0, tiled=True)

    table = TABLE if by_steps else None

    class Gather:
        def __init__(self, a, *others):
            self.cur = after(a, *others) if others else a
            if by_steps:
                self.cur = jnp.concatenate([self.cur] + [across(self.cur, 4 * k) for k in (1, 2, 3)], axis=0)

        def along_y(self, *others):
            if by_steps:
                cur = after(self.cur, *others) if others else self.cur
                self.cur = jnp.concatenate([cur, across(cur, 2)], axis=0)

        def finish(self, *others):
            if not by_steps:
                return gather(self.cur)
            cur = after(self.cur, *others) if others else self.cur
            return [cur, across(cur, 1)], table

    class Scatter:
        def __init__(self, dealt):
            self.kept, self.sent, self.step = dealt[0], [dealt[-1]], 0
            self.got = None
            if not by_steps:
                self.kept = self.total = scatter(dealt[0])

        @staticmethod
        def joined(a, b):
            both = Scatter.__new__(Scatter)
            both.kept, both.step = jnp.concatenate([a.kept, b.kept], axis=1), a.step
            if by_steps:
                both.sent = [jnp.concatenate(pair, axis=1) for pair in zip(a.sent, b.sent)]
            both.total = both.kept
            return both

        def send(self, *others):
            if not by_steps:
                return
            sent = [after(a, *others) if others else a for a in self.sent]
            bits = ((1,), (2,), (4, 8, 12))[self.step]
            self.got = [across(a, bit) for a, bit in zip(sent, bits)]
            self.step += 1

        def add(self, *others):
            if not by_steps:
                return self.total
            got = [after(a, *others) if others else a for a in self.got]
            total = sum([a.astype(F32) for a in got], self.kept.astype(F32))
            self.total, low = total, total.astype(BF16)
            if self.step == 1:
                self.kept, self.sent = low[:192], [low[192:]]
            else:
                self.kept, self.sent = low[:48], [low[48:96], low[96:144], low[144:]]
            return self.kept

    def dealt_shapes(width, table):
        return [sds((768, width), BF16)] if table is None else [sds((HALF, width), BF16)] * 2

    t = lax.axis_index("tensor").astype(jnp.int32)
    me = lax.axis_index("dp").astype(jnp.int32)
    scal = jnp.concatenate([t[None], shifts[0], valid_rows, jnp.array(PLACES, jnp.int32) ^ me])
    seg_r = seg_ids
    seg_c = seg_ids.reshape(-1, 1)

    a_in = attn_in.astype(BF16)
    gain_cols = jnp.pad(gains.T.astype(BF16), ((0, 0), (0, 122)))
    m_in = mlp_in.astype(BF16)
    m_out = mlp_out.astype(BF16).transpose(0, 2, 1)
    aot = attn_out.astype(BF16).transpose(0, 2, 1)
    g0 = Gather(jnp.concatenate([a_in[0].reshape(depth, WIDE), gain_cols, aot[0]], axis=1))
    g1 = Gather(jnp.concatenate([a_in[1].reshape(depth, WIDE), aot[1]], axis=1))
    bulk = [a_in[3][:, 0], a_in[2][:, 1], a_in[2][:, 2], a_in[2][:, 0], a_in[3][:, 1], a_in[3][:, 2], aot[2], aot[3]]
    bulk_own = jnp.concatenate(bulk, axis=1)
    bulk = gather(bulk_own)
    mlps = gather(after(jnp.concatenate([m_in[0], m_out[0], m_in[1], m_out[1]], axis=1), bulk_own))
    x_oth, q_oth = swap(visual), swap(query)
    cv_oth, cq_oth = swap(after(cot_visual, x_oth, q_oth)), swap(after(cot_query, x_oth, q_oth))
    g0.along_y()
    in0 = g0.finish()
    g1.along_y()
    in1 = g1.finish()

    def output(a):
        return ((in0, WIDE + 128), (in1, WIDE), (bulk, 2 * WIDE), (bulk, 2 * WIDE + HALF))[a] + (HALF, 1)

    def first(windowed, own, other, at, rows, unit, more, gates):
        outs = [sds((rows, 768), F32), sds((rows, 768), BF16), sds((rows, WIDE), BF16), sds((rows, HALF), BF16), sds((rows, 768), BF16), sds((8, rows), F32)]
        if windowed:
            outs.append(sds((8, 768), F32))
        width = WIDE + 128 if windowed else WIDE
        return call(part(first_kernel, windowed, at), [scal, own, other, *more], [(unit, 0, width, 1), output(at)], outs, "first_%d" % at, 4e9, gates=gates)

    sv0, nv0, qkv0, o0, p0, l0, gr = first(True, visual, x_oth, 0, rv, in0, [], [cv_oth])
    p0_oth = swap(p0)
    sq0, nq0, qkv1, o1, p1, l1 = first(False, query, q_oth, 1, rq, in1, [gr, seg_c, seg_r], [cq_oth])
    p1_oth = swap(p1)

    def middle(index, s, p, p_oth, at, rows):
        return call(
            part(middle_kernel, index), [scal, s, p, p_oth, gr], [(bulk, at, WIDE, 1)],
            [sds((rows, 768), F32), sds((rows, 768), BF16), sds((rows, WIDE), BF16)], "middle_%d" % index, 2e9)

    sv1, nv, pv = middle(2, sv0, p0, p0_oth, 0, rv)
    sq1, nq, pq = middle(3, sq0, p1, p1_oth, WIDE, rq)

    def cross(masked, q, kv, a, name, gates):
        outs = [sds((q.shape[0], HALF), BF16), sds((q.shape[0], 768), BF16), sds((8, q.shape[0]), F32)]
        return call(part(cross_kernel, masked), [scal, q, kv], [output(a)], outs, name, 2e9, gates=gates)

    o3, p3, l3 = cross(False, pv, pq, 3, "look", [])
    p3_oth = swap(p3)
    o2, p2, l2 = cross(True, pq, pv, 2, "read", [o3])
    p2_oth = swap(p2)

    fb = 768
    steps = 1536 // fb

    def mlp(index, s1, p, p_oth, cot, cot_oth, at, rows, into, gates=()):
        half = rows // 2
        first = 0 if into is None else steps
        dealt = pl.BlockSpec((768, 2 * fb), lambda i: (0, first + i))
        args = [scal, s1, p, p_oth, gr, cot, cot_oth] + ([] if into is None else [into])
        outs = [sds((rows, 768), F32), sds((half, 768), BF16), sds((half, 768), F32), sds((rows, 768), BF16), sds((1, 768), F32)]
        return call(
            part(mlp_kernel, index, steps), args,
            [(mlps, at, fb, steps), (mlps, at + 1536, fb, steps)], outs + [sds((768, 6144), BF16)],
            "mlp_%d" % index, 10 * rows * 768 * 1536,
            scratch=[pltpu.VMEM((rows, 768), BF16), pltpu.VMEM((rows, 768), BF16), pltpu.VMEM((768, rows), BF16),
                     pltpu.VMEM((768, rows), BF16), pltpu.VMEM((rows, 768), F32), pltpu.VMEM((rows, 768), F32),
                     pltpu.VMEM((rows, 768), F32)],
            grid=(steps,), out_specs=[pl.BlockSpec(o.shape, lambda i: (0, 0)) for o in outs] + [dealt], gates=gates, into={} if into is None else {7: 5})

    sv2, part_v, keep_v, dnv4, dg4, dm = mlp(4, sv1, p3, p3_oth, cot_visual, cv_oth, 0, rv, None, [o2])
    dnv4_oth = swap(dnv4)
    sq2, part_q, keep_q, dnq5, dg5, dm = mlp(5, sq1, p2, p2_oth, cot_query, cq_oth, 3072, rq, dm, [dnv4])
    dnq5_oth = swap(dnq5)
    s3 = scatter(dm)

    def cross_back(masked, index, cot, cot_oth, dn, dn_oth, s2, a, q, kv, o, lse, name, gates=()):
        return call(
            part(cross_back_kernel, masked, index), [scal, cot, cot_oth, dn, dn_oth, s2, gr, q, kv, o, lse], [output(a)],
            [sds((q.shape[0], 768), F32), sds((q.shape[0], 768), BF16), sds((q.shape[0], HALF), BF16), sds((kv.shape[0], 768), BF16)],
            name, 6e9, gates=gates)

    gv2, dyv, dq3, dkv3 = cross_back(False, 4, cot_visual, cv_oth, dnv4, dnv4_oth, sv2, 3, pv, pq, o3, l3, "look_back", [sq2])
    def dn_of(dq, dkv, at, rows, name, gates):
        return call(dn_kernel, [scal, dq, dkv], [(bulk, at, WIDE, 1)], [sds((rows, 768), BF16)], name, 1e9, gates=gates)[0]

    def weights(grads, dy, o, name, gains=(), gates=(), at=0, blocks=1, into=()):
        width = WIDE + HALF + (128 if gains else 0)
        scratch = [] if table is None else [pltpu.VMEM((768, width), BF16)]
        if gains:
            scratch.append(pltpu.VMEM((128, 768), F32))
        args = [scal, dy, o, *grads, *gains, *into]
        shapes = dealt_shapes(width * blocks, table)
        return call(part(weights_kernel, table, len(gains), len(grads), len(into)), args, [], shapes, name, 1.5e9,
                    scratch=scratch, gates=gates, out_specs=[pl.BlockSpec((a.shape[0], width), lambda i: (0, at)) for a in shapes],
                    into={len(args) - len(into) + i: i for i in range(len(into))})

    hl = Scatter(weights([nv, dq3, nq, dkv3], dyv, o3, "weights_look"))
    gates = [hl.kept]
    hl.send()
    gq2, dyq, dq2, dkv2 = cross_back(True, 5, cot_query, cq_oth, dnq5, dnq5_oth, sq2, 2, pq, pv, o2, l2, "read_back", gates)

    dnv2 = dn_of(dq3, dkv2, 0, rv, "dn_2", [hl.add()])
    dnv2_oth = swap(dnv2)
    dnq3 = dn_of(dq2, dkv3, WIDE, rq, "dn_3", [dnv2])
    dnq3_oth = swap(dnq3)

    hl.send()
    hr = Scatter(weights([nq, dq2, nv, dkv2], dyq, o2, "weights_read", gates=[dnv2, dnq3]))
    hr.send()
    gates = [hr.kept]

    def first_back(windowed, index, later, grad, dn, dn_oth, s1, s0, unit, qkv, o, lse, rows, more, gates):
        half = rows // 2
        outs = [sds((half, 768), F32), sds((rows, 768), BF16), sds((rows, WIDE), BF16), sds((half, 768), BF16),
                sds((half, 768), F32), sds((1, 768), F32), sds((1, 768), F32)]
        return call(part(first_back_kernel, windowed, index, later), [scal, grad, dn, dn_oth, s1, s0, gr, qkv, o, lse, *more],
                    [output(index), (unit, 0, WIDE, 1)], outs, "first_back_%d" % index, 7e9,
                    scratch=[pltpu.VMEM((rows, 768), F32)], gates=gates)

    gv1, dy0, d0, send_v, hold_v, dg0, dg2 = first_back(True, 0, 2, gv2, dnv2, dnv2_oth, sv1, sv0, in0, qkv0, o0, l0, rv, [], gates)
    got_v = swap(send_v)
    h0 = Scatter(weights([nv0, d0], dy0, o0, "weights_0", gates=[hr.add()]))
    hr.send()
    h0.send()
    gates = [h0.kept]
    gq1, dy1, d1, send_q, hold_q, dg1, dg3 = first_back(False, 1, 3, gq2, dnq3, dnq3_oth, sq1, sq0, in1, qkv1, o1, l1, rq, [seg_c, seg_r], gates)
    h1 = Scatter(weights([nq0, d1], dy1, o1, "weights_1", [dg0, dg1, dg2, dg3, dg4, dg5], [hl.add(), h0.add(), hr.add()]))
    h1.send()
    gates = [h1.add()]
    both = Scatter.joined(h0, h1)
    both.send()
    hl.send(*gates)
    hr.send(*gates)
    got_q = swap(send_q)
    late = both.add()
    hl.add()
    hr.add()
    both.send()
    m3 = s3.reshape(depth, 2, steps, 2, fb)
    grad_up = m3[:, :, :, 0].transpose(1, 0, 2, 3).reshape(2, depth, 1536).astype(F32)
    grad_down = m3[:, :, :, 1].reshape(depth, 2, 1536).transpose(1, 2, 0).astype(F32)
    both.add(grad_up, grad_down)
    s0, s1 = both.total[:, : WIDE + HALF], both.total[:, WIDE + HALF :]
    look, read = hl.total, hr.total
    out_visual = (keep_v + after(swap(after(part_v, *gates)), late).astype(F32)).astype(BF16)
    out_query = (keep_q + after(swap(after(part_q, *gates)), late).astype(F32)).astype(BF16)

    def last(index, grad, keep, got, own, gates):
        return call(part(last_kernel, index), [scal, grad, keep, got, own, gr], [], [sds(own.shape, BF16)], "last_%d" % index, 1e7, gates=gates)[0]

    grad_visual = last(0, gv1, hold_v, got_v, visual, [late])
    grad_query = last(1, gq1, hold_q, got_q, query, [late])

    def slots(a):
        return a[:, 0:WIDE].reshape(depth, 3, HALF)

    grad_in = jnp.stack([slots(s0), slots(s1), slots(read), slots(look)]).astype(F32)
    grad_out = jnp.stack([a[:, WIDE : WIDE + HALF].T for a in (s0, s1, read, look)]).astype(F32)
    gsum = s1[:, WIDE + HALF :].astype(F32)
    gsum = gsum + swap(gsum)
    grad_gain = gsum[:, 0:6].T
    return out_visual, out_query, grad_visual, grad_query, grad_in, grad_out, grad_up, grad_down, grad_gain


def solution(mesh):
    rows = P(("dp", "tensor"), None)
    weights = (P(None, "dp", None, "tensor"), P(None, "tensor", "dp"), P(None, "dp", "tensor"), P(None, "tensor", "dp"), P(None, "dp"))
    in_specs = (rows, rows, P("dp", None), P("dp", None), P("dp")) + weights + (rows, rows)
    out_specs = (rows, rows, rows, rows) + weights
    body = part(on_device, mesh.shape["dp"])
    return jax.shard_map(body, mesh=mesh, in_specs=in_specs, out_specs=out_specs, check_vma=False)
```

```python
import jax
import jax.numpy as jnp
from jax import lax
from jax.experimental import pallas as pl
from jax.experimental.pallas import tpu as pltpu
from jax.sharding import PartitionSpec as P

PH = 36
PW = 12
SCALE = 0.125
EPSILON = 1e-05
MASKED = -1e30
ROOT_HALF = 0.7071067811865476
INV_ROOT_TAU = 0.3989422804014327
F32 = jnp.float32
BF16 = jnp.bfloat16
WIDE = 1152
HALF = 384


def nn(a, b):
    return lax.dot_general(a, b, (((1,), (0,)), ((), ())), preferred_element_type=F32)


def nt(a, b):
    return lax.dot_general(a, b, (((1,), (1,)), ((), ())), preferred_element_type=F32)


def tn(a, b):
    return lax.dot_general(a, b, (((0,), (0,)), ((), ())), preferred_element_type=F32)


def unit_of(s):
    centred = s - jnp.mean(s, axis=-1, keepdims=True)
    inverse = lax.rsqrt(jnp.mean(centred * centred, axis=-1, keepdims=True) + EPSILON)
    return centred * inverse, inverse


def norm_back(dn, u, inverse, gain):
    scaled = dn * gain
    centre = jnp.mean(scaled, axis=-1, keepdims=True)
    slope = jnp.mean(scaled * u, axis=-1, keepdims=True)
    return inverse * (scaled - centre - u * slope)


def assemble(dst, own, other, t):
    half = own.shape[0]
    dst[pl.ds(pl.multiple_of(t * half, 8), half), :] = own[...].astype(F32)
    dst[pl.ds(pl.multiple_of((1 - t) * half, 8), half), :] = other[...].astype(F32)


def own_rows(ref, which, half):
    return ref[pl.ds(pl.multiple_of(which * half, 8), half), :]


def head_mask(h, value):
    lane = lax.broadcasted_iota(jnp.int32, (1, 128), 1)
    return jnp.where((lane >= 64) == (h == 1), value, 0.0).astype(BF16)


def twelfth(v):
    return lax.shift_right_logical(v * 43691, 19)


def places(shape, axis, scal):
    a, b = scal[1], scal[2]
    i = lax.broadcasted_iota(jnp.int32, shape, axis)
    r = twelfth(i)
    c = i - 12 * r
    rolled = jnp.where(r < a, r - a + PH, r - a)
    region = jnp.where(r < a, 2, 0) + jnp.where(c < b, 1, 0)
    return i, r, twelfth(rolled) * 4 + region


def window_bias(n, scal, key_axis):
    shape_k = (1, n) if key_axis == 1 else (n, 1)
    shape_q = (n, 1) if key_axis == 1 else (1, n)
    ik, rk, pk = places(shape_k, key_axis, scal)
    iq, _, pq = places(shape_q, 1 - key_axis, scal)
    usable = jnp.where(rk < scal[3], pk, -1)
    allowed = (usable == pq) | (ik == iq)
    return jnp.where(allowed, 0.0, MASKED).astype(F32)


def read_bias(n, scal, key_axis):
    shape = (1, n) if key_axis == 1 else (n, 1)
    i = lax.broadcasted_iota(jnp.int32, shape, key_axis)
    return jnp.where(twelfth(i) < scal[3], 0.0, MASKED).astype(F32)


def attend(q_ref, q_at, kv_ref, k_at, v_at, bias, o_ref, lse_ref):
    lane = lax.broadcasted_iota(jnp.int32, (1, 128), 1)
    logs = jnp.zeros((q_ref.shape[0], 128), F32)
    for pair in range(3):
        at = pair * 128
        q = q_ref[:, q_at + at : q_at + at + 128]
        k = kv_ref[:, k_at + at : k_at + at + 128]
        v = kv_ref[:, v_at + at : v_at + at + 128]
        outs = []
        for h in range(2):
            s = nt(q * head_mask(h, SCALE), k)
            if bias is not None:
                s = s + bias
            top = jnp.max(s, axis=1, keepdims=True)
            e = jnp.exp(s - top)
            total = jnp.sum(e, axis=1, keepdims=True)
            outs.append(nn(e.astype(BF16), v) * (1.0 / total))
            logs = jnp.where(lane == 2 * pair + h, top + jnp.log(total), logs)
        o_ref[:, at : at + 128] = jnp.where(lane < 64, outs[0], outs[1]).astype(BF16)
    lse_ref[...] = logs.T[0:8, :]


def attend_back(q_ref, q_at, kv_ref, k_at, v_at, bias, do, o_ref, lse_ref, dq_ref, dq_at, dk_ref, dk_at, dv_at):
    product = do.astype(F32) * o_ref[...].astype(F32)
    high = product.astype(BF16)
    low = (product - high.astype(F32)).astype(BF16)
    head = lax.broadcasted_iota(jnp.int32, (8, HALF), 0)
    column = lax.broadcasted_iota(jnp.int32, (8, HALF), 1)
    pick = jnp.where((column >= 64 * head) & (column < 64 * head + 64), 1.0, 0.0).astype(BF16)
    deltas = nt(pick, high) + nt(pick, low)
    for pair in range(3):
        at = pair * 128
        q = q_ref[:, q_at + at : q_at + at + 128]
        k = kv_ref[:, k_at + at : k_at + at + 128]
        v = kv_ref[:, v_at + at : v_at + at + 128]
        dop = do[:, at : at + 128]
        dq, dk, dv = 0.0, 0.0, 0.0
        for h in range(2):
            row = 2 * pair + h
            keep = head_mask(h, 1.0)
            qm = q * head_mask(h, SCALE)
            dom = dop * keep
            s = nt(k, qm)
            if bias is not None:
                s = s + bias
            p = jnp.exp(s - lse_ref[row : row + 1, :])
            ds = (p * (nt(v, dom) - deltas[row : row + 1, :])).astype(BF16)
            dv = dv + nn(p.astype(BF16), dom)
            dk = dk + nn(ds, qm)
            dq = dq + tn(ds, k * keep)
        dq_ref[:, dq_at + at : dq_at + at + 128] = (dq * SCALE).astype(BF16)
        dk_ref[:, dk_at + at : dk_at + at + 128] = dk.astype(BF16)
        dk_ref[:, dv_at + at : dv_at + at + 128] = dv.astype(BF16)


def first_kernel(windowed, index, ws, *refs):
    if windowed:
        scal, own, other, s_ref, n_ref, qkv, o_ref, p_ref, lse_ref, gr_ref = refs
    else:
        scal, own, other, gr, seg_c, seg_r, s_ref, n_ref, qkv, o_ref, p_ref, lse_ref = refs
    assemble(s_ref, own, other, scal[0])
    u, _ = unit_of(s_ref[...])
    w = ws[0]()
    if windowed:
        gr = w[:, WIDE:].astype(F32).T[0:8, :]
        gr_ref[...] = gr
    n = (u * gr[index : index + 1, :]).astype(BF16)
    n_ref[...] = n.T
    qkv[...] = nn(n, w[:, 0:WIDE]).astype(BF16)
    if windowed:
        bias = window_bias(qkv.shape[0], scal, 1)
    else:
        bias = jnp.where(seg_c[...] == seg_r[...], 0.0, MASKED).astype(F32)
    attend(qkv, 0, qkv, HALF, 2 * HALF, bias, o_ref, lse_ref)
    p_ref[...] = nt(o_ref[...], ws[1]()[...]).astype(BF16)


def middle_kernel(index, ws, scal, s, p_own, p_oth, gr, s1, n_ref, proj):
    stream = s[...] + (p_own[...].astype(F32) + p_oth[...].astype(F32))
    s1[...] = stream
    u, _ = unit_of(stream)
    n = (u * gr[index : index + 1, :]).astype(BF16)
    n_ref[...] = n.T
    proj[...] = nn(n, ws[0]()[...]).astype(BF16)


def cross_kernel(masked, ws, scal, q_ref, kv_ref, o_ref, p_ref, lse_ref):
    bias = read_bias(kv_ref.shape[0], scal, 1) if masked else None
    attend(q_ref, 0, kv_ref, HALF, 2 * HALF, bias, o_ref, lse_ref)
    p_ref[...] = nt(o_ref[...], ws[0]()[...]).astype(BF16)


def mlp_kernel(index, steps, ws, scal, s1, p_own, p_oth, gr, cot_own, cot_oth,
               *refs):
    s2, send, keep, dn_ref, dg_ref, dm_ref, n_s, dy_s, nt_s, dyt_s, part_s, dn_s, cot_s = refs[-13:]
    step = pl.program_id(0)
    half = cot_own.shape[0]
    t = scal[0]

    @pl.when(step == 0)
    def _():
        for w in ws:
            w.start()
        stream = s1[...] + (p_own[...].astype(F32) + p_oth[...].astype(F32))
        s2[...] = stream
        u, _ = unit_of(stream)
        n = (u * gr[index : index + 1, :]).astype(BF16)
        n_s[...] = n
        nt_s[...] = n.T
        assemble(cot_s, cot_own, cot_oth, t)
        dy = cot_s[...].astype(BF16)
        dy_s[...] = dy
        dyt_s[...] = dy.T

    for i in range(steps):

        @pl.when(step == i)
        def _(i=i):
            ws[0](i)
            ws[1](i)

    fb = ws[0].width
    w_in = ws[0].stack[step]
    w_out = ws[1].stack[step]
    hidden = nn(n_s[...], w_in)
    phi = 0.5 * (1.0 + lax.erf(hidden * ROOT_HALF))
    act = (hidden * phi).astype(BF16)
    slope = phi + hidden * jnp.exp(-0.5 * hidden * hidden) * INV_ROOT_TAU
    dh = (nn(dy_s[...], w_out) * slope).astype(BF16)
    part = nt(act, w_out)
    dn = nt(dh, w_in)

    @pl.when(step == 0)
    def _():
        part_s[...] = part
        dn_s[...] = dn

    @pl.when(step > 0)
    def _():
        part_s[...] += part
        dn_s[...] += dn

    dm_ref[:, 0:fb] = nn(nt_s[...], dh).astype(BF16)
    dm_ref[:, fb : 2 * fb] = nn(dyt_s[...], act).astype(BF16)

    @pl.when(step == steps - 1)
    def _():
        send[...] = own_rows(part_s, 1 - t, half).astype(BF16)
        keep[...] = own_rows(part_s, t, half) + own_rows(s2, t, half)
        dn_all = dn_s[...]
        dn_ref[...] = dn_all.astype(BF16)
        u, _ = unit_of(s2[...])
        dg_ref[...] = jnp.sum(dn_all * u, axis=0, keepdims=True)


def cross_back_kernel(masked, index, ws, scal, cot_own, cot_oth, dn_own, dn_oth, s2, gr, q_ref, kv_ref, o_ref, lse_ref,
                      g_ref, dy_ref, dq_ref, dkv_ref):
    assemble(g_ref, cot_own, cot_oth, scal[0])
    u, inverse = unit_of(s2[...])
    dn = dn_own[...].astype(F32) + dn_oth[...].astype(F32)
    grad = g_ref[...] + norm_back(dn, u, inverse, gr[index : index + 1, :])
    g_ref[...] = grad
    dy = grad.astype(BF16)
    dy_ref[...] = dy
    do = nn(dy, ws[0]()[...]).astype(BF16)
    bias = read_bias(kv_ref.shape[0], scal, 0) if masked else None
    attend_back(q_ref, 0, kv_ref, HALF, 2 * HALF, bias, do, o_ref, lse_ref, dq_ref, 0, dkv_ref, 0, HALF)


def dn_kernel(ws, scal, dq, dkv, dn_ref):
    w = ws[0]()
    dn_ref[...] = (nt(dq[...], w[:, 0:HALF]) + nt(dkv[...], w[:, HALF:WIDE])).astype(BF16)


def fill_weights(out, grads, dy, o):
    at = 0
    for n, grad in zip(grads[0::2], grads[1::2]):
        width = grad.shape[1]
        out[:, at : at + width] = nn(n[...], grad[...]).astype(BF16)
        at += width
    out[:, at : at + HALF] = tn(dy[...], o[...]).astype(BF16)


def weights_kernel(table, gains, parts, held, ws, scal, dy, o, *refs):
    grads, rows = refs[:parts], refs[parts : parts + gains]
    refs = refs[parts + gains + held :]
    if table is None:
        out = refs[0]
    else:
        *dealt, out = refs[:3]
    fill_weights(out, grads, dy, o)
    if gains:
        stack = refs[-1]
        stack[...] = jnp.zeros_like(stack)
        for i, row in enumerate(rows):
            stack[i : i + 1, :] = row[...]
        out[:, WIDE + HALF :] = stack[...].T.astype(BF16)
    if table is not None:
        deal(out, dealt, scal, table)


def first_back_kernel(windowed, index, later, ws, scal, *refs):
    if windowed:
        grad, dn_own, dn_oth, s1, s0, gr, qkv, o_ref, lse_ref, g_ref, dy_ref, dqkv, send, keep, dg_ref, dg_later, g_s = refs
    else:
        (grad, dn_own, dn_oth, s1, s0, gr, qkv, o_ref, lse_ref, seg_c, seg_r,
         g_ref, dy_ref, dqkv, send, keep, dg_ref, dg_later, g_s) = refs
    t = scal[0]
    half = g_ref.shape[0]
    u, inverse = unit_of(s1[...])
    dn = dn_own[...].astype(F32) + dn_oth[...].astype(F32)
    dg_later[...] = jnp.sum(dn_own[...].astype(F32) * u, axis=0, keepdims=True)
    g = grad[...] + norm_back(dn, u, inverse, gr[later : later + 1, :])
    g_s[...] = g
    g_ref[...] = own_rows(g_s, t, half)
    dy = g.astype(BF16)
    dy_ref[...] = dy
    do = nn(dy, ws[0]()[...]).astype(BF16)
    if windowed:
        bias = window_bias(qkv.shape[0], scal, 0)
    else:
        bias = jnp.where(seg_c[...] == seg_r[...], 0.0, MASKED).astype(F32)
    attend_back(qkv, 0, qkv, HALF, 2 * HALF, bias, do, o_ref, lse_ref, dqkv, 0, dqkv, HALF, 2 * HALF)
    dn0 = nt(dqkv[...], ws[1]()[...])
    g_s[...] = dn0
    send[...] = own_rows(g_s, 1 - t, half).astype(BF16)
    keep[...] = own_rows(g_s, t, half)
    u, _ = unit_of(s0[...])
    dg_ref[...] = jnp.sum(dn0 * u, axis=0, keepdims=True)


def last_kernel(index, ws, scal, grad, keep, got, own, gr, out):
    u, inverse = unit_of(own[...].astype(F32))
    dn = keep[...] + got[...].astype(F32)
    out[...] = (grad[...] + norm_back(dn, u, inverse, gr[index : index + 1, :])).astype(BF16)


class Weight:
    def __init__(self, scal, pieces, rooms, sems, at, width, table):
        self.scal, self.pieces, self.rooms, self.sems = scal, pieces, rooms, sems
        self.at, self.width, self.table, self.waited = at, width, table, set()

    def start(self):
        for i, room in enumerate(self.rooms):
            if self.table is None:
                source = self.pieces[0].at[:, pl.ds(self.at + i * self.width, self.width)]
                pltpu.make_async_copy(source, room, self.sems[i]).start()
                continue
            for p in range(16):
                to = pl.multiple_of(self.scal[self.table + p] * 48, 16)
                pltpu.make_async_copy(
                    self.pieces[p // 8].at[pl.ds(p % 8 * 48, 48), pl.ds(self.at + i * self.width, self.width)],
                    room.at[pl.ds(to, 48), :],
                    self.sems[i],
                ).start()

    def __call__(self, i=0):
        if i not in self.waited:
            pltpu.make_async_copy(self.rooms[i], self.rooms[i], self.sems[i]).wait()
            self.waited.add(i)
        return self.rooms[i]


def deal(whole, outs, scal, table):
    for p in range(16):
        block = whole[pl.ds(pl.multiple_of(scal[table + p] * 48, 16), 48), :]
        outs[p // 8][p % 8 * 48 : p % 8 * 48 + 48, :] = block


TABLE = 4


def call(body, args, weights, outs, name, flops, scratch=(), grid=(1,), out_specs=None, into=None, gates=()):
    def whole(shape):
        return pl.BlockSpec(shape, lambda *_: (0,) * len(shape))

    in_specs = [pl.BlockSpec(memory_space=pltpu.SMEM)] + [whole(a.shape) for a in args[1:]]
    for i in into or {}:
        in_specs[i] = pl.BlockSpec(memory_space=pl.ANY)
    out_specs = out_specs or [whole(o.shape) for o in outs]
    pieces = [piece for unit, _, _, _ in weights for piece in unit[0]]
    moved = sum(a.size * a.dtype.itemsize for a in list(outs) + list(args)) + sum(1536 * w * n for _, _, w, n in weights)
    n_in, n_w, n_out = len(args), len(weights), len(outs)

    def run(*refs):
        ins, refs = refs[:n_in], refs[n_in:]
        held, refs = refs[: len(pieces)], refs[len(pieces) + len(gates) :]
        out, refs = refs[:n_out], refs[n_out:]
        own, refs = refs[: len(scratch)], refs[len(scratch) :]
        ws = []
        for i, (unit, at, width, n) in enumerate(weights):
            rooms, sems = refs[2 * i], refs[2 * i + 1]
            mine, held = held[: len(unit[0])], held[len(unit[0]) :]
            ws.append(Weight(ins[0], mine, [rooms.at[j] for j in range(n)],
                             [sems.at[j] for j in range(n)], at, width, unit[1]))
            ws[-1].stack = rooms
        if grid == (1,):
            for w in ws:
                w.start()
        body(ws, *ins, *out, *own)

    rooms = []
    for _, _, width, n in weights:
        rooms += [pltpu.VMEM((n, 768, width), BF16), pltpu.SemaphoreType.DMA((n,))]
    return pl.pallas_call(
        run,
        out_shape=outs,
        grid=grid,
        in_specs=in_specs + [pl.BlockSpec(memory_space=pl.ANY)] * (len(pieces) + len(gates)),
        out_specs=out_specs,
        scratch_shapes=list(scratch) + rooms,
        input_output_aliases=into or {},
        name=name,
        compiler_params=pltpu.CompilerParams(vmem_limit_bytes=56 * 2**20),
        cost_estimate=pl.CostEstimate(flops=int(10 * flops), bytes_accessed=int(10 * moved), transcendentals=0),
    )(*args, *pieces, *gates)


def part(body, *fixed):
    return lambda *refs: body(*fixed, *refs)


def sds(shape, dtype):
    return jax.ShapeDtypeStruct(shape, dtype)


def sds(shape, dtype):
    return jax.ShapeDtypeStruct(shape, dtype)


PLACES = [(p >> 3) | (p >> 2 & 1) << 1 | (p & 3) << 2 for p in range(16)]


def on_device(size, visual, query, seg_ids, shifts, valid_rows, attn_in, attn_out, mlp_in, mlp_out, gains, cot_visual, cot_query):
    by_steps = size == 16
    depth = gains.shape[1]
    rv, rq = 2 * visual.shape[0], 2 * query.shape[0]

    def swap(a):
        return lax.ppermute(a, "tensor", [(0, 1), (1, 0)])

    def across(a, bit):
        return lax.ppermute(a, "dp", [(i, i ^ bit) for i in range(size)])

    def gather(a):
        return [lax.all_gather(a, "dp", axis=0, tiled=True)], None

    def after(a, *others):
        return lax.optimization_barrier((a, *others))[0]

    def scatter(a):
        return lax.psum_scatter(a, "dp", scatter_dimension=0, tiled=True)

    table = TABLE if by_steps else None

    class Gather:
        def __init__(self, a, *others):
            self.cur = after(a, *others) if others else a
            if by_steps:
                self.cur = jnp.concatenate([self.cur] + [across(self.cur, 4 * k) for k in (1, 2, 3)], axis=0)

        def along_y(self, *others):
            if by_steps:
                cur = after(self.cur, *others) if others else self.cur
                self.cur = jnp.concatenate([cur, across(cur, 2)], axis=0)

        def finish(self, *others):
            if not by_steps:
                return gather(self.cur)
            cur = after(self.cur, *others) if others else self.cur
            return [cur, across(cur, 1)], table

    class Scatter:
        def __init__(self, dealt):
            self.kept, self.sent, self.step = dealt[0], [dealt[-1]], 0
            self.got = None
            if not by_steps:
                self.kept = self.total = scatter(dealt[0])

        @staticmethod
        def joined(a, b):
            both = Scatter.__new__(Scatter)
            both.kept, both.step = jnp.concatenate([a.kept, b.kept], axis=1), a.step
            if by_steps:
                both.sent = [jnp.concatenate(pair, axis=1) for pair in zip(a.sent, b.sent)]
            both.total = both.kept
            return both

        def send(self, *others):
            if not by_steps:
                return
            sent = [after(a, *others) if others else a for a in self.sent]
            bits = ((1,), (2,), (4, 8, 12))[self.step]
            self.got = [across(a, bit) for a, bit in zip(sent, bits)]
            self.step += 1

        def add(self, *others):
            if not by_steps:
                return self.total
            got = [after(a, *others) if others else a for a in self.got]
            total = sum([a.astype(F32) for a in got], self.kept.astype(F32))
            self.total, low = total, total.astype(BF16)
            if self.step == 1:
                self.kept, self.sent = low[:192], [low[192:]]
            else:
                self.kept, self.sent = low[:48], [low[48:96], low[96:144], low[144:]]
            return self.kept

    def dealt_shapes(width, table):
        return [sds((768, width), BF16)] if table is None else [sds((HALF, width), BF16)] * 2

    t = lax.axis_index("tensor").astype(jnp.int32)
    me = lax.axis_index("dp").astype(jnp.int32)
    scal = jnp.concatenate([t[None], shifts[0], valid_rows, jnp.array(PLACES, jnp.int32) ^ me])
    seg_r = seg_ids
    seg_c = seg_ids.reshape(-1, 1)

    a_in = attn_in.astype(BF16)
    gain_cols = jnp.pad(gains.T.astype(BF16), ((0, 0), (0, 122)))
    m_in = mlp_in.astype(BF16)
    m_out = mlp_out.astype(BF16).transpose(0, 2, 1)
    aot = attn_out.astype(BF16).transpose(0, 2, 1)
    g0 = Gather(jnp.concatenate([a_in[0].reshape(depth, WIDE), gain_cols, aot[0]], axis=1))
    g1 = Gather(jnp.concatenate([a_in[1].reshape(depth, WIDE), aot[1]], axis=1))
    bulk = [a_in[3][:, 0], a_in[2][:, 1], a_in[2][:, 2], a_in[2][:, 0], a_in[3][:, 1], a_in[3][:, 2], aot[2], aot[3]]
    bulk_own = jnp.concatenate(bulk, axis=1)
    bulk = gather(bulk_own)
    mlps = gather(after(jnp.concatenate([m_in[0], m_out[0], m_in[1], m_out[1]], axis=1), bulk_own))
    x_oth, q_oth = swap(visual), swap(query)
    cv_oth, cq_oth = swap(after(cot_visual, x_oth, q_oth)), swap(after(cot_query, x_oth, q_oth))
    g0.along_y()
    in0 = g0.finish()
    g1.along_y()
    in1 = g1.finish()

    def output(a):
        return ((in0, WIDE + 128), (in1, WIDE), (bulk, 2 * WIDE), (bulk, 2 * WIDE + HALF))[a] + (HALF, 1)

    def first(windowed, own, other, at, rows, unit, more, gates):
        outs = [sds((rows, 768), F32), sds((768, rows), BF16), sds((rows, WIDE), BF16), sds((rows, HALF), BF16), sds((rows, 768), BF16), sds((8, rows), F32)]
        if windowed:
            outs.append(sds((8, 768), F32))
        width = WIDE + 128 if windowed else WIDE
        return call(part(first_kernel, windowed, at), [scal, own, other, *more], [(unit, 0, width, 1), output(at)], outs, "first_%d" % at, 4e9, gates=gates)

    sv0, nv0, qkv0, o0, p0, l0, gr = first(True, visual, x_oth, 0, rv, in0, [], [cv_oth])
    p0_oth = swap(p0)
    sq0, nq0, qkv1, o1, p1, l1 = first(False, query, q_oth, 1, rq, in1, [gr, seg_c, seg_r], [cq_oth])
    p1_oth = swap(p1)

    def middle(index, s, p, p_oth, at, rows):
        return call(
            part(middle_kernel, index), [scal, s, p, p_oth, gr], [(bulk, at, WIDE, 1)],
            [sds((rows, 768), F32), sds((768, rows), BF16), sds((rows, WIDE), BF16)], "middle_%d" % index, 2e9)

    sv1, nv, pv = middle(2, sv0, p0, p0_oth, 0, rv)
    sq1, nq, pq = middle(3, sq0, p1, p1_oth, WIDE, rq)

    def cross(masked, q, kv, a, name, gates):
        outs = [sds((q.shape[0], HALF), BF16), sds((q.shape[0], 768), BF16), sds((8, q.shape[0]), F32)]
        return call(part(cross_kernel, masked), [scal, q, kv], [output(a)], outs, name, 2e9, gates=gates)

    o3, p3, l3 = cross(False, pv, pq, 3, "look", [])
    p3_oth = swap(p3)
    o2, p2, l2 = cross(True, pq, pv, 2, "read", [o3])
    p2_oth = swap(p2)

    fb = 768
    steps = 1536 // fb

    def mlp(index, s1, p, p_oth, cot, cot_oth, at, rows, into, gates=()):
        half = rows // 2
        first = 0 if into is None else steps
        dealt = pl.BlockSpec((768, 2 * fb), lambda i: (0, first + i))
        args = [scal, s1, p, p_oth, gr, cot, cot_oth] + ([] if into is None else [into])
        outs = [sds((rows, 768), F32), sds((half, 768), BF16), sds((half, 768), F32), sds((rows, 768), BF16), sds((1, 768), F32)]
        return call(
            part(mlp_kernel, index, steps), args,
            [(mlps, at, fb, steps), (mlps, at + 1536, fb, steps)], outs + [sds((768, 6144), BF16)],
            "mlp_%d" % index, 10 * rows * 768 * 1536,
            scratch=[pltpu.VMEM((rows, 768), BF16), pltpu.VMEM((rows, 768), BF16), pltpu.VMEM((768, rows), BF16),
                     pltpu.VMEM((768, rows), BF16), pltpu.VMEM((rows, 768), F32), pltpu.VMEM((rows, 768), F32),
                     pltpu.VMEM((rows, 768), F32)],
            grid=(steps,), out_specs=[pl.BlockSpec(o.shape, lambda i: (0, 0)) for o in outs] + [dealt], gates=gates, into={} if into is None else {7: 5})

    sv2, part_v, keep_v, dnv4, dg4, dm = mlp(4, sv1, p3, p3_oth, cot_visual, cv_oth, 0, rv, None, [o2])
    dnv4_oth = swap(dnv4)
    sq2, part_q, keep_q, dnq5, dg5, dm = mlp(5, sq1, p2, p2_oth, cot_query, cq_oth, 3072, rq, dm, [dnv4])
    dnq5_oth = swap(dnq5)
    s3 = scatter(dm)

    def cross_back(masked, index, cot, cot_oth, dn, dn_oth, s2, a, q, kv, o, lse, name, gates=()):
        return call(
            part(cross_back_kernel, masked, index), [scal, cot, cot_oth, dn, dn_oth, s2, gr, q, kv, o, lse], [output(a)],
            [sds((q.shape[0], 768), F32), sds((q.shape[0], 768), BF16), sds((q.shape[0], HALF), BF16), sds((kv.shape[0], 768), BF16)],
            name, 6e9, gates=gates)

    gv2, dyv, dq3, dkv3 = cross_back(False, 4, cot_visual, cv_oth, dnv4, dnv4_oth, sv2, 3, pv, pq, o3, l3, "look_back", [sq2])
    def dn_of(dq, dkv, at, rows, name, gates):
        return call(dn_kernel, [scal, dq, dkv], [(bulk, at, WIDE, 1)], [sds((rows, 768), BF16)], name, 1e9, gates=gates)[0]

    def weights(grads, dy, o, name, gains=(), gates=(), at=0, blocks=1, into=()):
        width = WIDE + HALF + (128 if gains else 0)
        scratch = [] if table is None else [pltpu.VMEM((768, width), BF16)]
        if gains:
            scratch.append(pltpu.VMEM((128, 768), F32))
        args = [scal, dy, o, *grads, *gains, *into]
        shapes = dealt_shapes(width * blocks, table)
        return call(part(weights_kernel, table, len(gains), len(grads), len(into)), args, [], shapes, name, 1.5e9,
                    scratch=scratch, gates=gates, out_specs=[pl.BlockSpec((a.shape[0], width), lambda i: (0, at)) for a in shapes],
                    into={len(args) - len(into) + i: i for i in range(len(into))})

    hl = Scatter(weights([nv, dq3, nq, dkv3], dyv, o3, "weights_look"))
    gates = [hl.kept]
    hl.send()
    gq2, dyq, dq2, dkv2 = cross_back(True, 5, cot_query, cq_oth, dnq5, dnq5_oth, sq2, 2, pq, pv, o2, l2, "read_back", gates)

    dnv2 = dn_of(dq3, dkv2, 0, rv, "dn_2", [hl.add()])
    dnv2_oth = swap(dnv2)
    dnq3 = dn_of(dq2, dkv3, WIDE, rq, "dn_3", [dnv2])
    dnq3_oth = swap(dnq3)

    hl.send()
    hr = Scatter(weights([nq, dq2, nv, dkv2], dyq, o2, "weights_read", gates=[dnv2, dnq3]))
    hr.send()
    gates = [hr.kept]

    def first_back(windowed, index, later, grad, dn, dn_oth, s1, s0, unit, qkv, o, lse, rows, more, gates):
        half = rows // 2
        outs = [sds((half, 768), F32), sds((rows, 768), BF16), sds((rows, WIDE), BF16), sds((half, 768), BF16),
                sds((half, 768), F32), sds((1, 768), F32), sds((1, 768), F32)]
        return call(part(first_back_kernel, windowed, index, later), [scal, grad, dn, dn_oth, s1, s0, gr, qkv, o, lse, *more],
                    [output(index), (unit, 0, WIDE, 1)], outs, "first_back_%d" % index, 7e9,
                    scratch=[pltpu.VMEM((rows, 768), F32)], gates=gates)

    gv1, dy0, d0, send_v, hold_v, dg0, dg2 = first_back(True, 0, 2, gv2, dnv2, dnv2_oth, sv1, sv0, in0, qkv0, o0, l0, rv, [], gates)
    got_v = swap(send_v)
    h0 = Scatter(weights([nv0, d0], dy0, o0, "weights_0", gates=[hr.add()]))
    hr.send()
    h0.send()
    gates = [h0.kept]
    gq1, dy1, d1, send_q, hold_q, dg1, dg3 = first_back(False, 1, 3, gq2, dnq3, dnq3_oth, sq1, sq0, in1, qkv1, o1, l1, rq, [seg_c, seg_r], gates)
    h1 = Scatter(weights([nq0, d1], dy1, o1, "weights_1", [dg0, dg1, dg2, dg3, dg4, dg5], [hl.add(), h0.add(), hr.add()]))
    h1.send()
    gates = [h1.add()]
    both = Scatter.joined(h0, h1)
    both.send()
    hl.send(*gates)
    hr.send(*gates)
    got_q = swap(send_q)
    late = both.add()
    hl.add()
    hr.add()
    both.send()
    m3 = s3.reshape(depth, 2, steps, 2, fb)
    grad_up = m3[:, :, :, 0].transpose(1, 0, 2, 3).reshape(2, depth, 1536).astype(F32)
    grad_down = m3[:, :, :, 1].reshape(depth, 2, 1536).transpose(1, 2, 0).astype(F32)
    both.add(grad_up, grad_down)
    s0, s1 = both.total[:, : WIDE + HALF], both.total[:, WIDE + HALF :]
    look, read = hl.total, hr.total
    out_visual = (keep_v + after(swap(after(part_v, *gates)), late).astype(F32)).astype(BF16)
    out_query = (keep_q + after(swap(after(part_q, *gates)), late).astype(F32)).astype(BF16)

    def last(index, grad, keep, got, own, gates):
        return call(part(last_kernel, index), [scal, grad, keep, got, own, gr], [], [sds(own.shape, BF16)], "last_%d" % index, 1e7, gates=gates)[0]

    grad_visual = last(0, gv1, hold_v, got_v, visual, [late])
    grad_query = last(1, gq1, hold_q, got_q, query, [late])

    def slots(a):
        return a[:, 0:WIDE].reshape(depth, 3, HALF)

    grad_in = jnp.stack([slots(s0), slots(s1), slots(read), slots(look)]).astype(F32)
    grad_out = jnp.stack([a[:, WIDE : WIDE + HALF].T for a in (s0, s1, read, look)]).astype(F32)
    gsum = s1[:, WIDE + HALF :].astype(F32)
    gsum = gsum + swap(gsum)
    grad_gain = gsum[:, 0:6].T
    return out_visual, out_query, grad_visual, grad_query, grad_in, grad_out, grad_up, grad_down, grad_gain


def solution(mesh):
    rows = P(("dp", "tensor"), None)
    weights = (P(None, "dp", None, "tensor"), P(None, "tensor", "dp"), P(None, "dp", "tensor"), P(None, "tensor", "dp"), P(None, "dp"))
    in_specs = (rows, rows, P("dp", None), P("dp", None), P("dp")) + weights + (rows, rows)
    out_specs = (rows, rows, rows, rows) + weights
    body = part(on_device, mesh.shape["dp"])
    return jax.shard_map(body, mesh=mesh, in_specs=in_specs, out_specs=out_specs, check_vma=False)
```

```python
import jax
import jax.numpy as jnp
from jax import lax
from jax.experimental import pallas as pl
from jax.experimental.pallas import tpu as pltpu
from jax.sharding import PartitionSpec as P

PH = 36
PW = 12
SCALE = 0.125
EPSILON = 1e-05
MASKED = -1e30
ROOT_HALF = 0.7071067811865476
INV_ROOT_TAU = 0.3989422804014327
F32 = jnp.float32
BF16 = jnp.bfloat16
WIDE = 1152
HALF = 384


def nn(a, b):
    return lax.dot_general(a, b, (((1,), (0,)), ((), ())), preferred_element_type=F32)


def nt(a, b):
    return lax.dot_general(a, b, (((1,), (1,)), ((), ())), preferred_element_type=F32)


def tn(a, b):
    return lax.dot_general(a, b, (((0,), (0,)), ((), ())), preferred_element_type=F32)


def unit_of(s):
    centred = s - jnp.mean(s, axis=-1, keepdims=True)
    inverse = lax.rsqrt(jnp.mean(centred * centred, axis=-1, keepdims=True) + EPSILON)
    return centred * inverse, inverse


def norm_back(dn, u, inverse, gain):
    scaled = dn * gain
    centre = jnp.mean(scaled, axis=-1, keepdims=True)
    slope = jnp.mean(scaled * u, axis=-1, keepdims=True)
    return inverse * (scaled - centre - u * slope)


def assemble(dst, own, other, t):
    half = own.shape[0]
    dst[pl.ds(pl.multiple_of(t * half, 8), half), :] = own[...].astype(F32)
    dst[pl.ds(pl.multiple_of((1 - t) * half, 8), half), :] = other[...].astype(F32)


def own_rows(ref, which, half):
    return ref[pl.ds(pl.multiple_of(which * half, 8), half), :]


def head_mask(h, value):
    lane = lax.broadcasted_iota(jnp.int32, (1, 128), 1)
    return jnp.where((lane >= 64) == (h == 1), value, 0.0).astype(BF16)


def twelfth(v):
    return lax.shift_right_logical(v * 43691, 19)


def places(shape, axis, scal):
    a, b = scal[1], scal[2]
    i = lax.broadcasted_iota(jnp.int32, shape, axis)
    r = twelfth(i)
    c = i - 12 * r
    rolled = jnp.where(r < a, r - a + PH, r - a)
    region = jnp.where(r < a, 2, 0) + jnp.where(c < b, 1, 0)
    return i, r, twelfth(rolled) * 4 + region


def window_bias(n, scal, key_axis):
    shape_k = (1, n) if key_axis == 1 else (n, 1)
    shape_q = (n, 1) if key_axis == 1 else (1, n)
    ik, rk, pk = places(shape_k, key_axis, scal)
    iq, _, pq = places(shape_q, 1 - key_axis, scal)
    usable = jnp.where(rk < scal[3], pk, -1)
    allowed = (usable == pq) | (ik == iq)
    return jnp.where(allowed, 0.0, MASKED).astype(F32)


def read_bias(n, scal, key_axis):
    shape = (1, n) if key_axis == 1 else (n, 1)
    i = lax.broadcasted_iota(jnp.int32, shape, key_axis)
    return jnp.where(twelfth(i) < scal[3], 0.0, MASKED).astype(F32)


def attend(q_ref, q_at, kv_ref, k_at, v_at, bias, o_ref, lse_ref):
    lane = lax.broadcasted_iota(jnp.int32, (1, 128), 1)
    logs = jnp.zeros((q_ref.shape[0], 128), F32)
    for pair in range(3):
        at = pair * 128
        q = q_ref[:, q_at + at : q_at + at + 128]
        k = kv_ref[:, k_at + at : k_at + at + 128]
        v = kv_ref[:, v_at + at : v_at + at + 128]
        outs = []
        for h in range(2):
            s = nt(q * head_mask(h, SCALE), k)
            if bias is not None:
                s = s + bias
            top = jnp.max(s, axis=1, keepdims=True)
            e = jnp.exp(s - top)
            total = jnp.sum(e, axis=1, keepdims=True)
            outs.append(nn(e.astype(BF16), v) * (1.0 / total))
            logs = jnp.where(lane == 2 * pair + h, top + jnp.log(total), logs)
        o_ref[:, at : at + 128] = jnp.where(lane < 64, outs[0], outs[1]).astype(BF16)
    lse_ref[...] = logs.T[0:8, :]


def attend_back(q_ref, q_at, kv_ref, k_at, v_at, bias, do, o_ref, lse_ref, dq_ref, dq_at, dk_ref, dk_at, dv_at):
    product = do.astype(F32) * o_ref[...].astype(F32)
    high = product.astype(BF16)
    low = (product - high.astype(F32)).astype(BF16)
    head = lax.broadcasted_iota(jnp.int32, (8, HALF), 0)
    column = lax.broadcasted_iota(jnp.int32, (8, HALF), 1)
    pick = jnp.where((column >= 64 * head) & (column < 64 * head + 64), 1.0, 0.0).astype(BF16)
    deltas = nt(pick, high) + nt(pick, low)
    for pair in range(3):
        at = pair * 128
        q = q_ref[:, q_at + at : q_at + at + 128]
        k = kv_ref[:, k_at + at : k_at + at + 128]
        v = kv_ref[:, v_at + at : v_at + at + 128]
        dop = do[:, at : at + 128]
        dq, dk, dv = 0.0, 0.0, 0.0
        for h in range(2):
            row = 2 * pair + h
            keep = head_mask(h, 1.0)
            qm = q * head_mask(h, SCALE)
            dom = dop * keep
            s = nt(k, qm)
            if bias is not None:
                s = s + bias
            p = jnp.exp(s - lse_ref[row : row + 1, :])
            ds = (p * (nt(v, dom) - deltas[row : row + 1, :])).astype(BF16)
            dv = dv + nn(p.astype(BF16), dom)
            dk = dk + nn(ds, qm)
            dq = dq + tn(ds, k * keep)
        dq_ref[:, dq_at + at : dq_at + at + 128] = (dq * SCALE).astype(BF16)
        dk_ref[:, dk_at + at : dk_at + at + 128] = dk.astype(BF16)
        dk_ref[:, dv_at + at : dv_at + at + 128] = dv.astype(BF16)


def first_kernel(windowed, index, ws, *refs):
    if windowed:
        scal, own, other, s_ref, n_ref, qkv, o_ref, p_ref, lse_ref, gr_ref = refs
    else:
        scal, own, other, gr, seg_c, seg_r, s_ref, n_ref, qkv, o_ref, p_ref, lse_ref = refs
    assemble(s_ref, own, other, scal[0])
    u, _ = unit_of(s_ref[...])
    w = ws[0]()
    if windowed:
        gr = w[:, WIDE:].astype(F32).T[0:8, :]
        gr_ref[...] = gr
    n = (u * gr[index : index + 1, :]).astype(BF16)
    n_ref[...] = n
    qkv[...] = nn(n, w[:, 0:WIDE]).astype(BF16)
    if windowed:
        bias = window_bias(qkv.shape[0], scal, 1)
    else:
        bias = jnp.where(seg_c[...] == seg_r[...], 0.0, MASKED).astype(F32)
    attend(qkv, 0, qkv, HALF, 2 * HALF, bias, o_ref, lse_ref)
    p_ref[...] = nt(o_ref[...], ws[1]()[...]).astype(BF16)


def middle_kernel(index, ws, scal, s, p_own, p_oth, gr, s1, n_ref, proj):
    stream = s[...] + (p_own[...].astype(F32) + p_oth[...].astype(F32))
    s1[...] = stream
    u, _ = unit_of(stream)
    n = (u * gr[index : index + 1, :]).astype(BF16)
    n_ref[...] = n
    proj[...] = nn(n, ws[0]()[...]).astype(BF16)


def cross_kernel(masked, ws, scal, q_ref, kv_ref, o_ref, p_ref, lse_ref):
    bias = read_bias(kv_ref.shape[0], scal, 1) if masked else None
    attend(q_ref, 0, kv_ref, HALF, 2 * HALF, bias, o_ref, lse_ref)
    p_ref[...] = nt(o_ref[...], ws[0]()[...]).astype(BF16)


def mlp_kernel(index, steps, ws, scal, s1, p_own, p_oth, gr, cot_own, cot_oth,
               *refs):
    s2, send, keep, dn_ref, dg_ref, dm_ref, n_s, dy_s, nt_s, dyt_s, part_s, dn_s, cot_s = refs[-13:]
    step = pl.program_id(0)
    half = cot_own.shape[0]
    t = scal[0]

    @pl.when(step == 0)
    def _():
        stream = s1[...] + (p_own[...].astype(F32) + p_oth[...].astype(F32))
        s2[...] = stream
        u, _ = unit_of(stream)
        n = (u * gr[index : index + 1, :]).astype(BF16)
        n_s[...] = n
        nt_s[...] = n.T
        assemble(cot_s, cot_own, cot_oth, t)
        dy = cot_s[...].astype(BF16)
        dy_s[...] = dy
        dyt_s[...] = dy.T

    for i in range(steps):

        @pl.when(step == i)
        def _(i=i):
            ws[0](i)
            ws[1](i)

    fb = ws[0].width
    w_in = ws[0].stack[step]
    w_out = ws[1].stack[step]
    hidden = nn(n_s[...], w_in)
    phi = 0.5 * (1.0 + lax.erf(hidden * ROOT_HALF))
    act = (hidden * phi).astype(BF16)
    slope = phi + hidden * jnp.exp(-0.5 * hidden * hidden) * INV_ROOT_TAU
    dh = (nn(dy_s[...], w_out) * slope).astype(BF16)
    part = nt(act, w_out)
    dn = nt(dh, w_in)

    @pl.when(step == 0)
    def _():
        part_s[...] = part
        dn_s[...] = dn

    @pl.when(step > 0)
    def _():
        part_s[...] += part
        dn_s[...] += dn

    dm_ref[:, 0:fb] = nn(nt_s[...], dh).astype(BF16)
    dm_ref[:, fb : 2 * fb] = nn(dyt_s[...], act).astype(BF16)

    @pl.when(step == steps - 1)
    def _():
        send[...] = own_rows(part_s, 1 - t, half).astype(BF16)
        keep[...] = own_rows(part_s, t, half) + own_rows(s2, t, half)
        dn_all = dn_s[...]
        dn_ref[...] = dn_all.astype(BF16)
        u, _ = unit_of(s2[...])
        dg_ref[...] = jnp.sum(dn_all * u, axis=0, keepdims=True)


def cross_back_kernel(masked, index, ws, scal, cot_own, cot_oth, dn_own, dn_oth, s2, gr, q_ref, kv_ref, o_ref, lse_ref,
                      g_ref, dy_ref, dq_ref, dkv_ref):
    assemble(g_ref, cot_own, cot_oth, scal[0])
    u, inverse = unit_of(s2[...])
    dn = dn_own[...].astype(F32) + dn_oth[...].astype(F32)
    grad = g_ref[...] + norm_back(dn, u, inverse, gr[index : index + 1, :])
    g_ref[...] = grad
    dy = grad.astype(BF16)
    dy_ref[...] = dy
    do = nn(dy, ws[0]()[...]).astype(BF16)
    bias = read_bias(kv_ref.shape[0], scal, 0) if masked else None
    attend_back(q_ref, 0, kv_ref, HALF, 2 * HALF, bias, do, o_ref, lse_ref, dq_ref, 0, dkv_ref, 0, HALF)


def dn_kernel(ws, scal, dq, dkv, dn_ref):
    w = ws[0]()
    dn_ref[...] = (nt(dq[...], w[:, 0:HALF]) + nt(dkv[...], w[:, HALF:WIDE])).astype(BF16)


def fill_weights(out, grads, dy, o):
    at = 0
    for n, grad in zip(grads[0::2], grads[1::2]):
        width = grad.shape[1]
        out[:, at : at + width] = tn(n[...], grad[...]).astype(BF16)
        at += width
    out[:, at : at + HALF] = tn(dy[...], o[...]).astype(BF16)


def weights_kernel(table, gains, parts, held, ws, scal, dy, o, *refs):
    grads, rows = refs[:parts], refs[parts : parts + gains]
    refs = refs[parts + gains + held :]
    if table is None:
        out = refs[0]
    else:
        *dealt, out = refs[:3]
    fill_weights(out, grads, dy, o)
    if gains:
        stack = refs[-1]
        stack[...] = jnp.zeros_like(stack)
        for i, row in enumerate(rows):
            stack[i : i + 1, :] = row[...]
        out[:, WIDE + HALF :] = stack[...].T.astype(BF16)
    if table is not None:
        deal(out, dealt, scal, table)


def first_back_kernel(windowed, index, later, ws, scal, *refs):
    if windowed:
        grad, dn_own, dn_oth, s1, s0, gr, qkv, o_ref, lse_ref, g_ref, dy_ref, dqkv, send, keep, dg_ref, dg_later, g_s = refs
    else:
        (grad, dn_own, dn_oth, s1, s0, gr, qkv, o_ref, lse_ref, seg_c, seg_r,
         g_ref, dy_ref, dqkv, send, keep, dg_ref, dg_later, g_s) = refs
    t = scal[0]
    half = g_ref.shape[0]
    u, inverse = unit_of(s1[...])
    dn = dn_own[...].astype(F32) + dn_oth[...].astype(F32)
    dg_later[...] = jnp.sum(dn_own[...].astype(F32) * u, axis=0, keepdims=True)
    g = grad[...] + norm_back(dn, u, inverse, gr[later : later + 1, :])
    g_s[...] = g
    g_ref[...] = own_rows(g_s, t, half)
    dy = g.astype(BF16)
    dy_ref[...] = dy
    do = nn(dy, ws[0]()[...]).astype(BF16)
    if windowed:
        bias = window_bias(qkv.shape[0], scal, 0)
    else:
        bias = jnp.where(seg_c[...] == seg_r[...], 0.0, MASKED).astype(F32)
    attend_back(qkv, 0, qkv, HALF, 2 * HALF, bias, do, o_ref, lse_ref, dqkv, 0, dqkv, HALF, 2 * HALF)
    dn0 = nt(dqkv[...], ws[1]()[...])
    g_s[...] = dn0
    send[...] = own_rows(g_s, 1 - t, half).astype(BF16)
    keep[...] = own_rows(g_s, t, half)
    u, _ = unit_of(s0[...])
    dg_ref[...] = jnp.sum(dn0 * u, axis=0, keepdims=True)


def last_kernel(index, ws, scal, grad, keep, got, own, gr, out):
    u, inverse = unit_of(own[...].astype(F32))
    dn = keep[...] + got[...].astype(F32)
    out[...] = (grad[...] + norm_back(dn, u, inverse, gr[index : index + 1, :])).astype(BF16)


class Weight:
    def __init__(self, scal, pieces, rooms, sems, at, width, table):
        self.scal, self.pieces, self.rooms, self.sems = scal, pieces, rooms, sems
        self.at, self.width, self.table, self.waited = at, width, table, set()

    def start(self):
        for i, room in enumerate(self.rooms):
            if self.table is None:
                source = self.pieces[0].at[:, pl.ds(self.at + i * self.width, self.width)]
                pltpu.make_async_copy(source, room, self.sems[i]).start()
                continue
            for p in range(16):
                to = pl.multiple_of(self.scal[self.table + p] * 48, 16)
                pltpu.make_async_copy(
                    self.pieces[p // 8].at[pl.ds(p % 8 * 48, 48), pl.ds(self.at + i * self.width, self.width)],
                    room.at[pl.ds(to, 48), :],
                    self.sems[i],
                ).start()

    def __call__(self, i=0):
        if i not in self.waited:
            pltpu.make_async_copy(self.rooms[i], self.rooms[i], self.sems[i]).wait()
            self.waited.add(i)
        return self.rooms[i]


def deal(whole, outs, scal, table):
    for p in range(16):
        block = whole[pl.ds(pl.multiple_of(scal[table + p] * 48, 16), 48), :]
        outs[p // 8][p % 8 * 48 : p % 8 * 48 + 48, :] = block


TABLE = 4


def call(body, args, weights, outs, name, flops, scratch=(), grid=(1,), out_specs=None, into=None, gates=()):
    def whole(shape):
        return pl.BlockSpec(shape, lambda *_: (0,) * len(shape))

    in_specs = [pl.BlockSpec(memory_space=pltpu.SMEM)] + [whole(a.shape) for a in args[1:]]
    for i in into or {}:
        in_specs[i] = pl.BlockSpec(memory_space=pl.ANY)
    out_specs = out_specs or [whole(o.shape) for o in outs]
    pieces = [piece for unit, _, _, _ in weights for piece in unit[0]]
    moved = sum(a.size * a.dtype.itemsize for a in list(outs) + list(args)) + sum(1536 * w * n for _, _, w, n in weights)
    n_in, n_w, n_out = len(args), len(weights), len(outs)

    def run(*refs):
        ins, refs = refs[:n_in], refs[n_in:]
        held, refs = refs[: len(pieces)], refs[len(pieces) + len(gates) :]
        out, refs = refs[:n_out], refs[n_out:]
        own, refs = refs[: len(scratch)], refs[len(scratch) :]
        ws = []
        for i, (unit, at, width, n) in enumerate(weights):
            rooms, sems = refs[2 * i], refs[2 * i + 1]
            mine, held = held[: len(unit[0])], held[len(unit[0]) :]
            ws.append(Weight(ins[0], mine, [rooms.at[j] for j in range(n)],
                             [sems.at[j] for j in range(n)], at, width, unit[1]))
            ws[-1].stack = rooms
        if grid == (1,):
            for w in ws:
                w.start()
        body(ws, *ins, *out, *own)

    rooms = []
    for _, _, width, n in weights:
        rooms += [pltpu.VMEM((n, 768, width), BF16), pltpu.SemaphoreType.DMA((n,))]
    return pl.pallas_call(
        run,
        out_shape=outs,
        grid=grid,
        in_specs=in_specs + [pl.BlockSpec(memory_space=pl.ANY)] * (len(pieces) + len(gates)),
        out_specs=out_specs,
        scratch_shapes=list(scratch) + rooms,
        input_output_aliases=into or {},
        name=name,
        compiler_params=pltpu.CompilerParams(vmem_limit_bytes=56 * 2**20),
        cost_estimate=pl.CostEstimate(flops=int(10 * flops), bytes_accessed=int(10 * moved), transcendentals=0),
    )(*args, *pieces, *gates)


def part(body, *fixed):
    return lambda *refs: body(*fixed, *refs)


def sds(shape, dtype):
    return jax.ShapeDtypeStruct(shape, dtype)


def sds(shape, dtype):
    return jax.ShapeDtypeStruct(shape, dtype)


PLACES = [(p >> 3) | (p >> 2 & 1) << 1 | (p & 3) << 2 for p in range(16)]


def on_device(size, visual, query, seg_ids, shifts, valid_rows, attn_in, attn_out, mlp_in, mlp_out, gains, cot_visual, cot_query):
    by_steps = size == 16
    depth = gains.shape[1]
    rv, rq = 2 * visual.shape[0], 2 * query.shape[0]

    def swap(a):
        return lax.ppermute(a, "tensor", [(0, 1), (1, 0)])

    def across(a, bit):
        return lax.ppermute(a, "dp", [(i, i ^ bit) for i in range(size)])

    def gather(a):
        return [lax.all_gather(a, "dp", axis=0, tiled=True)], None

    def after(a, *others):
        return lax.optimization_barrier((a, *others))[0]

    def scatter(a):
        return lax.psum_scatter(a, "dp", scatter_dimension=0, tiled=True)

    table = TABLE if by_steps else None

    class Gather:
        def __init__(self, a, *others):
            self.cur = after(a, *others) if others else a
            if by_steps:
                self.cur = jnp.concatenate([self.cur] + [across(self.cur, 4 * k) for k in (1, 2, 3)], axis=0)

        def along_y(self, *others):
            if by_steps:
                cur = after(self.cur, *others) if others else self.cur
                self.cur = jnp.concatenate([cur, across(cur, 2)], axis=0)

        def finish(self, *others):
            if not by_steps:
                return gather(self.cur)
            cur = after(self.cur, *others) if others else self.cur
            return [cur, across(cur, 1)], table

    class Scatter:
        def __init__(self, dealt):
            self.kept, self.sent, self.step = dealt[0], [dealt[-1]], 0
            self.got = None
            if not by_steps:
                self.kept = self.total = scatter(dealt[0])

        @staticmethod
        def joined(a, b):
            both = Scatter.__new__(Scatter)
            both.kept, both.step = jnp.concatenate([a.kept, b.kept], axis=1), a.step
            if by_steps:
                both.sent = [jnp.concatenate(pair, axis=1) for pair in zip(a.sent, b.sent)]
            both.total = both.kept
            return both

        def send(self, *others):
            if not by_steps:
                return
            sent = [after(a, *others) if others else a for a in self.sent]
            bits = ((1,), (2,), (4, 8, 12))[self.step]
            self.got = [across(a, bit) for a, bit in zip(sent, bits)]
            self.step += 1

        def add(self, *others):
            if not by_steps:
                return self.total
            got = [after(a, *others) if others else a for a in self.got]
            total = sum([a.astype(F32) for a in got], self.kept.astype(F32))
            self.total, low = total, total.astype(BF16)
            if self.step == 1:
                self.kept, self.sent = low[:192], [low[192:]]
            else:
                self.kept, self.sent = low[:48], [low[48:96], low[96:144], low[144:]]
            return self.kept

    def dealt_shapes(width, table):
        return [sds((768, width), BF16)] if table is None else [sds((HALF, width), BF16)] * 2

    t = lax.axis_index("tensor").astype(jnp.int32)
    me = lax.axis_index("dp").astype(jnp.int32)
    scal = jnp.concatenate([t[None], shifts[0], valid_rows, jnp.array(PLACES, jnp.int32) ^ me])
    seg_r = seg_ids
    seg_c = seg_ids.reshape(-1, 1)

    a_in = attn_in.astype(BF16)
    gain_cols = jnp.pad(gains.T.astype(BF16), ((0, 0), (0, 122)))
    m_in = mlp_in.astype(BF16)
    m_out = mlp_out.astype(BF16).transpose(0, 2, 1)
    aot = attn_out.astype(BF16).transpose(0, 2, 1)
    g0 = Gather(jnp.concatenate([a_in[0].reshape(depth, WIDE), gain_cols, aot[0]], axis=1))
    g1 = Gather(jnp.concatenate([a_in[1].reshape(depth, WIDE), aot[1]], axis=1))
    bulk = [a_in[3][:, 0], a_in[2][:, 1], a_in[2][:, 2], a_in[2][:, 0], a_in[3][:, 1], a_in[3][:, 2], aot[2], aot[3]]
    bulk_own = jnp.concatenate(bulk, axis=1)
    bulk = gather(bulk_own)
    mlps = gather(after(jnp.concatenate([m_in[0], m_out[0], m_in[1], m_out[1]], axis=1), bulk_own))
    x_oth, q_oth = swap(visual), swap(query)
    cv_oth, cq_oth = swap(after(cot_visual, x_oth, q_oth)), swap(after(cot_query, x_oth, q_oth))
    g0.along_y()
    in0 = g0.finish()
    g1.along_y()
    in1 = g1.finish()

    def output(a):
        return ((in0, WIDE + 128), (in1, WIDE), (bulk, 2 * WIDE), (bulk, 2 * WIDE + HALF))[a] + (HALF, 1)

    def first(windowed, own, other, at, rows, unit, more, gates):
        outs = [sds((rows, 768), F32), sds((rows, 768), BF16), sds((rows, WIDE), BF16), sds((rows, HALF), BF16), sds((rows, 768), BF16), sds((8, rows), F32)]
        if windowed:
            outs.append(sds((8, 768), F32))
        width = WIDE + 128 if windowed else WIDE
        return call(part(first_kernel, windowed, at), [scal, own, other, *more], [(unit, 0, width, 1), output(at)], outs, "first_%d" % at, 4e9, gates=gates)

    sv0, nv0, qkv0, o0, p0, l0, gr = first(True, visual, x_oth, 0, rv, in0, [], [cv_oth])
    p0_oth = swap(p0)
    sq0, nq0, qkv1, o1, p1, l1 = first(False, query, q_oth, 1, rq, in1, [gr, seg_c, seg_r], [cq_oth])
    p1_oth = swap(p1)

    def middle(index, s, p, p_oth, at, rows):
        return call(
            part(middle_kernel, index), [scal, s, p, p_oth, gr], [(bulk, at, WIDE, 1)],
            [sds((rows, 768), F32), sds((rows, 768), BF16), sds((rows, WIDE), BF16)], "middle_%d" % index, 2e9)

    sv1, nv, pv = middle(2, sv0, p0, p0_oth, 0, rv)
    sq1, nq, pq = middle(3, sq0, p1, p1_oth, WIDE, rq)

    def cross(masked, q, kv, a, name, gates):
        outs = [sds((q.shape[0], HALF), BF16), sds((q.shape[0], 768), BF16), sds((8, q.shape[0]), F32)]
        return call(part(cross_kernel, masked), [scal, q, kv], [output(a)], outs, name, 2e9, gates=gates)

    o3, p3, l3 = cross(False, pv, pq, 3, "look", [])
    p3_oth = swap(p3)
    o2, p2, l2 = cross(True, pq, pv, 2, "read", [o3])
    p2_oth = swap(p2)

    fb = 1536
    steps = 1536 // fb

    def mlp(index, s1, p, p_oth, cot, cot_oth, at, rows, into, gates=()):
        half = rows // 2
        first = 0 if into is None else steps
        dealt = pl.BlockSpec((768, 2 * fb), lambda i: (0, first + i))
        args = [scal, s1, p, p_oth, gr, cot, cot_oth] + ([] if into is None else [into])
        outs = [sds((rows, 768), F32), sds((half, 768), BF16), sds((half, 768), F32), sds((rows, 768), BF16), sds((1, 768), F32)]
        return call(
            part(mlp_kernel, index, steps), args,
            [(mlps, at, fb, steps), (mlps, at + 1536, fb, steps)], outs + [sds((768, 6144), BF16)],
            "mlp_%d" % index, 10 * rows * 768 * 1536,
            scratch=[pltpu.VMEM((rows, 768), BF16), pltpu.VMEM((rows, 768), BF16), pltpu.VMEM((768, rows), BF16),
                     pltpu.VMEM((768, rows), BF16), pltpu.VMEM((rows, 768), F32), pltpu.VMEM((rows, 768), F32),
                     pltpu.VMEM((rows, 768), F32)],
            grid=(steps,), out_specs=[pl.BlockSpec(o.shape, lambda i: (0, 0)) for o in outs] + [dealt], gates=gates, into={} if into is None else {7: 5})

    sv2, part_v, keep_v, dnv4, dg4, dm = mlp(4, sv1, p3, p3_oth, cot_visual, cv_oth, 0, rv, None, [o2])
    dnv4_oth = swap(dnv4)
    sq2, part_q, keep_q, dnq5, dg5, dm = mlp(5, sq1, p2, p2_oth, cot_query, cq_oth, 3072, rq, dm, [dnv4])
    dnq5_oth = swap(dnq5)
    s3 = scatter(dm)

    def cross_back(masked, index, cot, cot_oth, dn, dn_oth, s2, a, q, kv, o, lse, name, gates=()):
        return call(
            part(cross_back_kernel, masked, index), [scal, cot, cot_oth, dn, dn_oth, s2, gr, q, kv, o, lse], [output(a)],
            [sds((q.shape[0], 768), F32), sds((q.shape[0], 768), BF16), sds((q.shape[0], HALF), BF16), sds((kv.shape[0], 768), BF16)],
            name, 6e9, gates=gates)

    gv2, dyv, dq3, dkv3 = cross_back(False, 4, cot_visual, cv_oth, dnv4, dnv4_oth, sv2, 3, pv, pq, o3, l3, "look_back", [sq2])
    def dn_of(dq, dkv, at, rows, name, gates):
        return call(dn_kernel, [scal, dq, dkv], [(bulk, at, WIDE, 1)], [sds((rows, 768), BF16)], name, 1e9, gates=gates)[0]

    def weights(grads, dy, o, name, gains=(), gates=(), at=0, blocks=1, into=()):
        width = WIDE + HALF + (128 if gains else 0)
        scratch = [] if table is None else [pltpu.VMEM((768, width), BF16)]
        if gains:
            scratch.append(pltpu.VMEM((128, 768), F32))
        args = [scal, dy, o, *grads, *gains, *into]
        shapes = dealt_shapes(width * blocks, table)
        return call(part(weights_kernel, table, len(gains), len(grads), len(into)), args, [], shapes, name, 1.5e9,
                    scratch=scratch, gates=gates, out_specs=[pl.BlockSpec((a.shape[0], width), lambda i: (0, at)) for a in shapes],
                    into={len(args) - len(into) + i: i for i in range(len(into))})

    hl = Scatter(weights([nv, dq3, nq, dkv3], dyv, o3, "weights_look"))
    gates = [hl.kept]
    hl.send()
    gq2, dyq, dq2, dkv2 = cross_back(True, 5, cot_query, cq_oth, dnq5, dnq5_oth, sq2, 2, pq, pv, o2, l2, "read_back", gates)

    dnv2 = dn_of(dq3, dkv2, 0, rv, "dn_2", [hl.add()])
    dnv2_oth = swap(dnv2)
    dnq3 = dn_of(dq2, dkv3, WIDE, rq, "dn_3", [dnv2])
    dnq3_oth = swap(dnq3)

    hl.send()
    hr = Scatter(weights([nq, dq2, nv, dkv2], dyq, o2, "weights_read", gates=[dnv2, dnq3]))
    hr.send()
    gates = [hr.kept]

    def first_back(windowed, index, later, grad, dn, dn_oth, s1, s0, unit, qkv, o, lse, rows, more, gates):
        half = rows // 2
        outs = [sds((half, 768), F32), sds((rows, 768), BF16), sds((rows, WIDE), BF16), sds((half, 768), BF16),
                sds((half, 768), F32), sds((1, 768), F32), sds((1, 768), F32)]
        return call(part(first_back_kernel, windowed, index, later), [scal, grad, dn, dn_oth, s1, s0, gr, qkv, o, lse, *more],
                    [output(index), (unit, 0, WIDE, 1)], outs, "first_back_%d" % index, 7e9,
                    scratch=[pltpu.VMEM((rows, 768), F32)], gates=gates)

    gv1, dy0, d0, send_v, hold_v, dg0, dg2 = first_back(True, 0, 2, gv2, dnv2, dnv2_oth, sv1, sv0, in0, qkv0, o0, l0, rv, [], gates)
    got_v = swap(send_v)
    h0 = Scatter(weights([nv0, d0], dy0, o0, "weights_0", gates=[hr.add()]))
    hr.send()
    h0.send()
    gates = [h0.kept]
    gq1, dy1, d1, send_q, hold_q, dg1, dg3 = first_back(False, 1, 3, gq2, dnq3, dnq3_oth, sq1, sq0, in1, qkv1, o1, l1, rq, [seg_c, seg_r], gates)
    h1 = Scatter(weights([nq0, d1], dy1, o1, "weights_1", [dg0, dg1, dg2, dg3, dg4, dg5], [hl.add(), h0.add(), hr.add()]))
    h1.send()
    gates = [h1.add()]
    both = Scatter.joined(h0, h1)
    both.send()
    hl.send(*gates)
    hr.send(*gates)
    got_q = swap(send_q)
    late = both.add()
    hl.add()
    hr.add()
    both.send()
    m3 = s3.reshape(depth, 2, steps, 2, fb)
    grad_up = m3[:, :, :, 0].transpose(1, 0, 2, 3).reshape(2, depth, 1536).astype(F32)
    grad_down = m3[:, :, :, 1].reshape(depth, 2, 1536).transpose(1, 2, 0).astype(F32)
    both.add(grad_up, grad_down)
    s0, s1 = both.total[:, : WIDE + HALF], both.total[:, WIDE + HALF :]
    look, read = hl.total, hr.total
    out_visual = (keep_v + after(swap(after(part_v, *gates)), late).astype(F32)).astype(BF16)
    out_query = (keep_q + after(swap(after(part_q, *gates)), late).astype(F32)).astype(BF16)

    def last(index, grad, keep, got, own, gates):
        return call(part(last_kernel, index), [scal, grad, keep, got, own, gr], [], [sds(own.shape, BF16)], "last_%d" % index, 1e7, gates=gates)[0]

    grad_visual = last(0, gv1, hold_v, got_v, visual, [late])
    grad_query = last(1, gq1, hold_q, got_q, query, [late])

    def slots(a):
        return a[:, 0:WIDE].reshape(depth, 3, HALF)

    grad_in = jnp.stack([slots(s0), slots(s1), slots(read), slots(look)]).astype(F32)
    grad_out = jnp.stack([a[:, WIDE : WIDE + HALF].T for a in (s0, s1, read, look)]).astype(F32)
    gsum = s1[:, WIDE + HALF :].astype(F32)
    gsum = gsum + swap(gsum)
    grad_gain = gsum[:, 0:6].T
    return out_visual, out_query, grad_visual, grad_query, grad_in, grad_out, grad_up, grad_down, grad_gain


def solution(mesh):
    rows = P(("dp", "tensor"), None)
    weights = (P(None, "dp", None, "tensor"), P(None, "tensor", "dp"), P(None, "dp", "tensor"), P(None, "tensor", "dp"), P(None, "dp"))
    in_specs = (rows, rows, P("dp", None), P("dp", None), P("dp")) + weights + (rows, rows)
    out_specs = (rows, rows, rows, rows) + weights
    body = part(on_device, mesh.shape["dp"])
    return jax.shard_map(body, mesh=mesh, in_specs=in_specs, out_specs=out_specs, check_vma=False)
```
